128 devices in a mesh: row: 4 (over y), col: 32 (over z, x, core).
Axes of the slice: x: 4, y: 4, z: 4, core: 2. Of those that a mesh axis runs over, the one named last changes fastest.
Arguments:
- tokens_in: bfloat16 [32768, 1024], P(('row', 'col')), may hold values from -6 to 6
- out_cot: bfloat16 [32768, 1024], P(('row', 'col')), may hold values from -6 to 6
- long_lengths: int32 [32], P('col'), may hold values from 385 to 512, as said below
- short_lengths: int32 [128], P(('row', 'col')), may hold values from 32 to 128, as said below
- routes: int32 [32768, 2], P(('row', 'col')), may hold values from 0 to 31, all different within a row; in each aligned block of 256 rows (0 to 255, 256 to 511, ...) at most 20 rows name the same one
- gain_attn: float32 [1024], replicated, may hold values from 0.5 to 1.5
- w_query: bfloat16 [1024, 1024], replicated, may hold values from -0.1875 to 0.1875
- w_key: bfloat16 [1024, 1024], replicated, may hold values from -0.1875 to 0.1875
- w_value: bfloat16 [1024, 1024], replicated, may hold values from -0.1875 to 0.1875
- w_out: bfloat16 [1024, 1024], replicated, may hold values from -1 to 1
- rel_bias: float32 [32, 16], replicated, may hold values from -4 to 4
- gain_moe: float32 [1024], replicated, may hold values from 0.5 to 1.5
- router: float32 [1024, 32], replicated, may hold values from -0.125 to 0.125
- w_gate: bfloat16 [32, 1024, 2816], P('col', None, 'row'), may hold values from -0.1875 to 0.1875
- w_up: bfloat16 [32, 1024, 2816], P('col', None, 'row'), may hold values from -0.1875 to 0.1875
- w_down: bfloat16 [32, 2816, 1024], P('col', 'row'), may hold values from -0.15625 to 0.15625
Outputs:
- block_out: float32 [32768, 1024], P(('row', 'col'))
- tokens_grad: float32 [32768, 1024], P(('row', 'col'))
- gain_attn_grad: float32 [1024], replicated
- query_grad: float32 [1024, 1024], replicated
- key_grad: float32 [1024, 1024], replicated
- value_grad: float32 [1024, 1024], replicated
- out_proj_grad: float32 [1024, 1024], replicated
- bias_grad: float32 [32, 16], replicated
- gain_moe_grad: float32 [1024], replicated
- router_grad: float32 [1024, 32], replicated
- gate_grad: float32 [32, 1024, 2816], P('col', None, 'row')
- up_grad: float32 [32, 1024, 2816], P('col', None, 'row')
- down_grad: float32 [32, 2816, 1024], P('col', 'row')
- statistics: float32 [3], replicated
The draws below stay inside these ranges and needn't reach their ends.
Inputs may be any that keep to these rules, and one draw needn't show every extreme that they name: `routes`: each row names two different experts. Within the rows of one device no expert is named by more than 20 rows, and in some device one expert is named by exactly 20. `long_lengths`: one long sequence has all 512 positions live. `short_lengths`: one short sequence has all 128 positions live.
All inputs are finite; a program needn't handle non-finite values.
Results may differ from the reference program's by a relative error of at most 0.017.
Values may be sent and summed in bfloat16 or wider, within the bound.
A program may use at most 192 MiB of HBM per device.

```python
import math
import jax
import jax.numpy as jnp
import numpy as np
from jax import lax

D = 1024
HEADS = 16
HEAD_DIM = 64
FF = 2816
TOPK = 2
NBUCKETS = 32
LONG_DEV = 128
SHORT_LEN = 128
UNITS = 1
EXPERTS = 32
TOK_DEV = 256
LONG_LEN = 512
LONG_SEQS = 32
SHORT_SEQS = 128
TOKENS = 32768
CAP = 20
N_ROW = 4
N_COL = 32


def draw_long_lengths(key, part):
    key = jax.random.fold_in(key, 11)
    length_key, pick_key = jax.random.split(key)
    lengths = jax.random.randint(length_key, (LONG_SEQS,), LONG_LEN - LONG_DEV + 1, LONG_LEN + 1, dtype=jnp.int32)
    picked = jax.random.randint(pick_key, (), 0, LONG_SEQS, dtype=jnp.int32)
    return jnp.where(jnp.arange(LONG_SEQS, dtype=jnp.int32) == picked, LONG_LEN, lengths).astype(jnp.int32)


def draw_short_lengths(key, part):
    key = jax.random.fold_in(key, 23)
    length_key, pick_key = jax.random.split(key)
    lengths = jax.random.randint(length_key, (SHORT_SEQS,), SHORT_LEN // 4, SHORT_LEN + 1, dtype=jnp.int32)
    picked = jax.random.randint(pick_key, (), 0, SHORT_SEQS, dtype=jnp.int32)
    return jnp.where(jnp.arange(SHORT_SEQS, dtype=jnp.int32) == picked, SHORT_LEN, lengths).astype(jnp.int32)


def levels(stream_key, shape, cuts, least, high):
    level, own = 1.0, jax.random.fold_in(stream_key, 6)
    for dim, shards_of in cuts:
        heights = jnp.exp(jax.random.uniform(jax.random.fold_in(own, dim), (shards_of,), jnp.float32, least / len(cuts), high / len(cuts)))
        level = level * jnp.repeat(heights, shape[dim] // shards_of).reshape([-1 if axis == dim else 1 for axis in range(len(shape))])
    return level


def routed_block(rng, own, number, rows, amount, top, most, slope):
    ranking = jax.random.permutation(rng, amount)
    crowded, ordinary = portions_of(amount, rows * top, most, slope, True), portions_of(amount, rows * top, most, slope, False)
    places = jnp.arange(amount)

    def named(sizes, turn):
        used = int((sizes > 0).sum())
        fixed = max(1, used // 4)
        moved = fixed + (places - fixed + turn * (used - fixed)) % max(1, amount - fixed)
        return jnp.zeros((amount,), jnp.int32).at[ranking[jnp.where(places < fixed, places, moved)]].set(jnp.asarray(sizes, jnp.int32))

    sizes = jnp.where(number % 4 == 0, named(crowded, number // 4), named(ordinary, number - number // 4 - 1))
    mixed = jax.random.permutation(jax.random.fold_in(own, 3), amount)
    giver, taker = mixed[0:amount // 2 * 2:2], mixed[1:amount // 2 * 2:2]
    margin = jnp.minimum(sizes[giver] - 1, most - sizes[taker]) // 2
    margin = jnp.where((giver == ranking[0]) | (taker == ranking[0]) | (sizes[taker] == 0), 0, jnp.maximum(margin, 0))
    moved = jax.random.randint(jax.random.fold_in(own, 4), (amount // 2,), 0, 1 << 20) % (margin + 1)
    sizes = sizes.at[giver].add(-moved).at[taker].add(moved)
    items = jnp.searchsorted(jnp.cumsum(sizes), jnp.arange(rows * top), side="right").astype(jnp.int32)
    table = items.reshape(top, rows).T
    table = table[jax.random.permutation(jax.random.fold_in(own, 1), rows)]
    turn = jax.random.randint(jax.random.fold_in(own, 2), (rows, 1), 0, top)
    return jnp.take_along_axis(table, (jnp.arange(top)[None, :] + turn) % top, axis=1)


def portions_of(count, total, limit, slope, full):
    portions = [(1 << 20) // math.isqrt(standing ** slope) + 1 for standing in range(1, count + 1)]
    largest = limit if full else min(limit, max(-(-total // count), total * portions[0] // sum(portions)))
    least = 1 if total - largest >= count - 1 else 0
    given, spare = [largest] + [least] * (count - 1), total - largest - least * (count - 1)
    while spare > 0:
        movable = [i for i in range(1, count) if given[i] < largest] or [i for i in range(1, count) if given[i] < limit]
        mass, left = sum([portions[i] for i in movable]), spare
        for i in movable:
            more = min(limit - given[i], max(1, left * portions[i] // mass), spare)
            given[i] = given[i] + more
            spare = spare - more
    return np.array(given)


def gaussian(own_key, dims, scale, reach, cuts=(), held_as=jnp.bfloat16):
    drawn = jax.random.normal(own_key, dims, jnp.float32) * scale
    if len(cuts) > 0:
        drawn = levels(own_key, dims, cuts, -0.22, 0.18) * drawn
    return jnp.clip(drawn, min=-reach, max=reach).astype(held_as)


def setup_inputs(seed: int = 0) -> dict:
    arg_keys = jax.random.split(jax.random.key(seed), 17)
    tokens_in = gaussian(arg_keys[0], (TOKENS, D), 1.0, 6.0, ((0, 128),))
    out_cot = gaussian(arg_keys[1], (TOKENS, D), 1.0, 6.0, ((0, 128),))
    long_lengths = draw_long_lengths(jax.random.fold_in(arg_keys[16], 71), 0)
    short_lengths = draw_short_lengths(jax.random.fold_in(arg_keys[16], 71), 0)
    routes_keys = jax.random.split(jax.random.fold_in(arg_keys[4], 1), TOKENS // TOK_DEV)
    routes_turns = jax.random.permutation(jax.random.fold_in(arg_keys[4], 3), TOKENS // TOK_DEV)
    routes = jax.vmap(lambda own, number: routed_block(jax.random.fold_in(arg_keys[4], 2), own, number, TOK_DEV, EXPERTS, 2, CAP, 1))(routes_keys, routes_turns).reshape((TOKENS, TOPK))
    gain_attn = jnp.clip(1.0 + 0.1 * jax.random.normal(arg_keys[5], (D,), jnp.float32), 0.5, 1.5)
    w_query = gaussian(arg_keys[6], (D, D), D ** -0.5, 0.1875)
    w_key = gaussian(arg_keys[7], (D, D), D ** -0.5, 0.1875)
    w_value = gaussian(arg_keys[8], (D, D), D ** -0.5, 0.1875)
    w_out = gaussian(arg_keys[9], (D, D), (D // 32) ** -0.5, 1.0)
    rel_bias = gaussian(arg_keys[10], (NBUCKETS, HEADS), 1.0, 4.0, (), jnp.float32)
    gain_moe = jnp.clip(1.0 + 0.1 * jax.random.normal(arg_keys[11], (D,), jnp.float32), 0.5, 1.5)
    router = gaussian(arg_keys[12], (D, EXPERTS), (2 * D) ** -0.5, 0.125, (), jnp.float32)
    w_gate = gaussian(arg_keys[13], (EXPERTS, D, FF), D ** -0.5, 0.1875, ((0, 32), (2, 4)))
    w_up = gaussian(arg_keys[14], (EXPERTS, D, FF), D ** -0.5, 0.1875, ((0, 32), (2, 4)))
    w_down = gaussian(arg_keys[15], (EXPERTS, FF, D), (FF // 2) ** -0.5, 0.15625, ((0, 32), (1, 4)))
    return dict(tokens_in=tokens_in, out_cot=out_cot, long_lengths=long_lengths, short_lengths=short_lengths, routes=routes, gain_attn=gain_attn, w_query=w_query, w_key=w_key, w_value=w_value, w_out=w_out, rel_bias=rel_bias, gain_moe=gain_moe, router=router, w_gate=w_gate, w_up=w_up, w_down=w_down)


@jax.custom_vjp
def low(v):
    return lax.optimization_barrier(v.astype(jnp.bfloat16)).astype(jnp.float32)

@jax.custom_vjp
def low_back(v):
    return v

def low_keep(v):
    return (low(v), None)

def low_pass(kept, grad):
    return (grad,)

def back_keep(v):
    return (v, None)

def back_low(kept, grad):
    return (low(grad),)
low.defvjp(low_keep, low_pass)
low_back.defvjp(back_keep, back_low)
bucket_edges = (1, 2, 3, 4, 5, 6, 7, 8, 12, 16, 23, 32, 46, 64, 91)
norm_eps = 1e-06
balance_coef = 0.01
zloss_coef = 0.001
masked_score = -1e+30
highest = lax.Precision.HIGHEST

def matmul(left, right):
    return jnp.dot(left, right, precision=highest, preferred_element_type=jnp.float32)

def rms_norm(values, gain):
    return values * lax.rsqrt(lax.optimization_barrier(jnp.mean(values * values, axis=-1, keepdims=True)) + norm_eps) * gain

def geglu(gate_pre, up_pre):
    return jax.nn.gelu(gate_pre, approximate=True) * up_pre

def rel_buckets(query_pos, key_pos):
    relative = key_pos[None, :] - query_pos[:, None]
    magnitude = jnp.abs(relative)
    edges = jnp.array(bucket_edges, jnp.int32)
    level = lax.optimization_barrier(jnp.sum((magnitude[:, :, None] >= edges[None, None, :]).astype(jnp.int32), axis=2))
    shifted = level + jnp.where(relative > 0, len(bucket_edges) + 1, 0)
    return shifted.astype(jnp.int32)

def attend(query, keys, values, valid, bias):
    raw = jnp.einsum('bqhe,bkhe->bhqk', query, keys, precision=highest) * HEAD_DIM ** (-0.5) + bias[None]
    scores = low_back(jnp.where(valid[:, None, None, :], raw, masked_score))
    row_max = lax.optimization_barrier(jnp.max(scores, axis=-1, keepdims=True))
    exp_terms = jnp.exp(scores - row_max)
    probs = low(exp_terms / lax.optimization_barrier(jnp.sum(exp_terms, axis=-1, keepdims=True)))
    mixed = jnp.einsum('bhqk,bkhe->bqhe', probs, values, precision=highest)
    return low_back(low(mixed))

def run_attention(query, keys, values, valid, bias, per):
    count = query.shape[0]

    def one_block(operands):
        block_q, block_k, block_v, block_valid = operands
        return attend(block_q, block_k, block_v, block_valid, bias)
    stacked = tuple((member.reshape((count // per, per) + member.shape[1:]) for member in (query, keys, values, valid)))
    return lax.map(jax.checkpoint(one_block), stacked).reshape(query.shape)

def to_long(source_rows):
    width = source_rows.shape[-1]
    grid = source_rows.reshape(N_ROW, N_COL, TOK_DEV, width)[:, :, :UNITS * LONG_DEV]
    grid = grid.reshape(N_ROW, N_COL, UNITS, LONG_DEV, width).transpose(1, 2, 0, 3, 4)
    return grid.reshape(LONG_SEQS, LONG_LEN, width)

def to_short(source_rows):
    width = source_rows.shape[-1]
    grid = source_rows.reshape(N_ROW, N_COL, TOK_DEV, width)[:, :, UNITS * LONG_DEV:]
    return grid.reshape(SHORT_SEQS, SHORT_LEN, width)

def from_parts(long_part, short_part):
    width = long_part.shape[-1]
    long_grid = long_part.reshape(N_COL, UNITS, N_ROW, LONG_DEV, width).transpose(2, 0, 1, 3, 4)
    long_grid = long_grid.reshape(N_ROW, N_COL, UNITS * LONG_DEV, width)
    short_grid = short_part.reshape(N_ROW, N_COL, UNITS * SHORT_LEN, width)
    return jnp.concatenate([long_grid, short_grid], axis=2).reshape(TOKENS, width)

def reference(tokens_in, out_cot, long_lengths, short_lengths, routes, gain_attn, w_query, w_key, w_value, w_out, rel_bias, gain_moe, router, w_gate, w_up, w_down):
    devices = N_ROW * N_COL
    expert_ids = jnp.arange(EXPERTS, dtype=jnp.int32)
    flat_routes = routes.reshape(devices, TOK_DEV * TOPK).astype(jnp.int32)
    flat_hot = (flat_routes[:, :, None] == expert_ids[None, None, :]).astype(jnp.int32)
    earlier = jnp.cumsum(flat_hot, axis=1) - flat_hot
    slots = lax.optimization_barrier(jnp.sum(earlier * flat_hot, axis=2)).astype(jnp.int32)
    group_ids = jnp.arange(devices, dtype=jnp.int32)[:, None]
    position = ((flat_routes * devices + group_ids) * CAP + slots).reshape(TOKENS, TOPK).astype(jnp.int32)
    owners = (jnp.arange(TOKENS * TOPK, dtype=jnp.int32) // TOPK).astype(jnp.int32)
    source = jnp.full((EXPERTS * devices * CAP,), TOKENS, jnp.int32).at[position.reshape(-1)].set(owners)
    source = source.reshape(EXPERTS, devices * CAP)
    fraction = lax.optimization_barrier(jnp.sum(flat_hot, axis=1)).astype(jnp.float32) / (TOPK * TOK_DEV)
    route_hot = (routes[:, :, None] == expert_ids[None, None, :]).astype(jnp.float32)
    long_pos = jnp.arange(LONG_LEN, dtype=jnp.int32)
    short_pos = jnp.arange(SHORT_LEN, dtype=jnp.int32)
    long_valid = long_pos[None, :] < long_lengths[:, None]
    short_valid = short_pos[None, :] < short_lengths[:, None]
    long_buckets = rel_buckets(long_pos, long_pos)
    short_buckets = rel_buckets(short_pos, short_pos)
    long_per = math.gcd(LONG_SEQS, max(1, 4096 // LONG_LEN))
    short_per = math.gcd(SHORT_SEQS, max(1, 4096 // SHORT_LEN))

    def forward(inputs, gain_a, query_w, key_w, value_w, out_w, table, gain_m, router_w, gate_w, up_w, down_w):
        normed_a = low(rms_norm(inputs, gain_a))
        query = low_back(low(matmul(normed_a, query_w)))
        keys = low_back(low(matmul(normed_a, key_w)))
        values = low_back(low(matmul(normed_a, value_w)))
        long_bias = jnp.take(table, long_buckets, axis=0).transpose(2, 0, 1)
        short_bias = jnp.take(table, short_buckets, axis=0).transpose(2, 0, 1)

        def long_heads(rows):
            return to_long(rows).reshape(LONG_SEQS, LONG_LEN, HEADS, HEAD_DIM)

        def short_heads(rows):
            return to_short(rows).reshape(SHORT_SEQS, SHORT_LEN, HEADS, HEAD_DIM)
        long_mixed = run_attention(long_heads(query), long_heads(keys), long_heads(values), long_valid, long_bias, long_per)
        short_mixed = run_attention(short_heads(query), short_heads(keys), short_heads(values), short_valid, short_bias, short_per)
        mixed = from_parts(long_mixed.reshape(LONG_SEQS, LONG_LEN, D), short_mixed.reshape(SHORT_SEQS, SHORT_LEN, D))
        branch_a = low_back(matmul(mixed, out_w))
        resid = inputs + branch_a
        normed_m = rms_norm(resid, gain_m)
        logits = matmul(normed_m, router_w)
        row_max = lax.optimization_barrier(jnp.max(logits, axis=1, keepdims=True))
        exp_terms = jnp.exp(logits - row_max)
        row_total = lax.optimization_barrier(jnp.sum(exp_terms, axis=1, keepdims=True))
        probs = exp_terms / row_total
        router_norm = row_max[:, 0] + jnp.log(row_total[:, 0])
        picked = lax.optimization_barrier(jnp.sum(probs[:, None, :] * route_hot, axis=2))
        gates = picked / lax.optimization_barrier(jnp.sum(picked, axis=1, keepdims=True))
        aux_total = balance_coef * EXPERTS * jnp.sum(probs.reshape(devices, TOK_DEV, EXPERTS) * fraction[:, None, :]) + zloss_coef * jnp.sum(router_norm * router_norm)
        padded = jnp.concatenate([low(normed_m), jnp.zeros((1, D), normed_m.dtype)], axis=0)

        def expert(operands):
            rows, gate_e, up_e, down_e = operands
            buffer = low_back(jnp.take(padded, rows, axis=0))
            gate_pre = low_back(matmul(buffer, gate_e))
            up_pre = low_back(matmul(buffer, up_e))
            act = low(geglu(gate_pre, up_pre))
            return low_back(low(matmul(act, down_e)))
        expert_out = lax.map(jax.checkpoint(expert), (source, gate_w, up_w, down_w)).reshape(-1, D)
        chosen = jnp.take(expert_out, position, axis=0)
        branch_m = lax.optimization_barrier(jnp.sum(gates[:, :, None] * chosen, axis=1))
        return ((resid + branch_m, aux_total), (branch_a, branch_m))
    primals = (tokens_in.astype(jnp.float32), gain_attn, w_query.astype(jnp.float32), w_key.astype(jnp.float32), w_value.astype(jnp.float32), w_out.astype(jnp.float32), rel_bias, gain_moe, router, w_gate.astype(jnp.float32), w_up.astype(jnp.float32), w_down.astype(jnp.float32))
    (outputs, aux_total), back, (branch_a, branch_m) = jax.vjp(forward, *primals, has_aux=True)
    grads = back((out_cot.astype(jnp.float32), jnp.ones_like(aux_total)))
    live = from_parts(long_valid.astype(jnp.float32)[:, :, None], short_valid.astype(jnp.float32)[:, :, None])[:, 0]
    live_count = jnp.sum(live)

    def live_rms(field):
        return jnp.sqrt(jnp.sum(live * lax.optimization_barrier(jnp.sum(field * field, axis=1))) / (live_count * D))
    statistics = jnp.stack([live_rms(outputs), live_rms(branch_a), live_rms(branch_m)])
    return (outputs, grads[0], grads[1], grads[2], grads[3], grads[4], grads[5], grads[6], grads[7], grads[8], grads[9], grads[10], grads[11], statistics)
```

```python
import jax
import jax.numpy as jnp
from jax import lax
from jax.experimental import pallas as pl
from jax.experimental.pallas import tpu as pltpu
from jax.sharding import PartitionSpec as P

HEADS = 16
HEAD_DIM = 64
LONG_DEV = 128
SHORT_LEN = 128
UNITS = 1


bucket_edges = (1, 2, 3, 4, 5, 6, 7, 8, 12, 16, 23, 32, 46, 64, 91)
norm_eps = 1e-06
balance_coef = 0.01
zloss_coef = 0.001
masked_score = -1e30
highest = lax.Precision.HIGHEST


def rms_norm(values, gain):
    return values * lax.rsqrt(jnp.mean(values * values, axis=-1, keepdims=True) + norm_eps) * gain


def geglu(gate_pre, up_pre):
    return jax.nn.gelu(gate_pre, approximate=True) * up_pre


def geglu_back(gate_pre, up_pre, d_act):
    unused, back = jax.vjp(geglu, gate_pre, up_pre)
    d_gate, d_up = back(d_act)
    return (d_gate.astype(jnp.bfloat16), d_up.astype(jnp.bfloat16))


def rel_buckets(query_pos, key_pos):
    relative = key_pos[None, :] - query_pos[:, None]
    magnitude = jnp.abs(relative)
    edges = jnp.array(bucket_edges, jnp.int32)
    level = jnp.sum((magnitude[:, :, None] >= edges[None, None, :]).astype(jnp.int32), axis=2)
    return level + jnp.where(relative > 0, len(bucket_edges) + 1, 0)


def bucket_table(query_pos, key_pos, count):
    buckets = rel_buckets(query_pos, key_pos)
    return (buckets[None, :, :] == jnp.arange(count, dtype=jnp.int32)[:, None, None]).astype(
        jnp.float32
    )


def score_block(query, keys, bias, valid):
    raw = jnp.einsum("bqhe,bkhe->bhqk", query, keys, preferred_element_type=jnp.float32)
    raw = raw * query.shape[-1] ** (-0.5) + bias[None]
    return jnp.where(valid[:, None, None, :], raw, masked_score)


def attend_forward(query, keys, values, bias, valid):
    scores = score_block(query, keys, bias, valid)
    row_max = jnp.max(scores, axis=-1, keepdims=True)
    exp_terms = jnp.exp(scores - row_max)
    row_total = jnp.sum(exp_terms, axis=-1, keepdims=True)
    probs = (exp_terms / row_total).astype(jnp.bfloat16)
    mixed = jnp.einsum("bhqk,bkhe->bqhe", probs, values, preferred_element_type=jnp.float32)
    return (mixed.astype(jnp.bfloat16), row_max + jnp.log(row_total))


def attend_backward(query, keys, values, bias, valid, log_norm, d_mixed):
    scale = query.shape[-1] ** (-0.5)
    scores = score_block(query, keys, bias, valid)
    probs = jnp.exp(scores - log_norm)
    d_values = jnp.einsum(
        "bhqk,bqhe->bkhe", probs.astype(jnp.bfloat16), d_mixed, preferred_element_type=jnp.float32
    )
    d_probs = jnp.einsum("bqhe,bkhe->bhqk", d_mixed, values, preferred_element_type=jnp.float32)
    spread = jnp.sum(probs * d_probs, axis=-1, keepdims=True)
    d_scores = (probs * (d_probs - spread)).astype(jnp.bfloat16)
    d_query = (
        jnp.einsum("bhqk,bkhe->bqhe", d_scores, keys, preferred_element_type=jnp.float32) * scale
    )
    d_keys = (
        jnp.einsum("bhqk,bqhe->bkhe", d_scores, query, preferred_element_type=jnp.float32) * scale
    )
    return (d_query, d_keys, d_values, d_scores)


MESH_ID = pl.DeviceIdType.MESH

SUM_PARTS = (
    (5120, 0, ("x", "y", "z"), 0),
    (5120, 5120, ("y", "z", "x"), 0),
    (6144, 10240, ("z", "x", "y"), 0),
    (512, 0, ("y", "x", "z"), 1),
)
SUM_ROWS = (16384, 512)


def torus_place():
    row = lax.axis_index("row")
    col = lax.axis_index("col")
    core = lax.rem(col, 2)
    x = lax.rem(lax.div(col, 2), 4)
    z = lax.div(col, 8)
    return row, z, x, core


def axis_peer(axis, step):
    row, z, x, core = torus_place()
    if axis == "y":
        row = lax.rem(row + step, 4)
    elif axis == "x":
        x = lax.rem(x + step, 4)
    elif axis == "z":
        z = lax.rem(z + step, 4)
    else:
        core = 1 - core
    return (row, (z * 4 + x) * 2 + core)


def sum_kernel(*refs):
    inputs = refs[0:2]
    results = refs[2:4]
    held = refs[4:6]
    other = refs[6:8]
    slots = refs[8:8 + 3 * len(SUM_PARTS)]
    load_sem, core_send, core_recv, hop_send, hop_recv, gather_send, gather_recv, copy_sem, last_send, last_recv = refs[
        8 + 3 * len(SUM_PARTS):
    ]
    row, z, x, core = torus_place()
    place = {"x": x, "y": row, "z": z}
    barrier = pltpu.get_barrier_semaphore()
    pl.semaphore_signal(barrier, inc=1, device_id=axis_peer("core", 1), device_id_type=MESH_ID)
    for axis in ("x", "y", "z"):
        for step in (1, 2, 3):
            pl.semaphore_signal(barrier, inc=1, device_id=axis_peer(axis, step), device_id_type=MESH_ID)
    loads = []
    for p, (rows, first, order, kind) in enumerate(SUM_PARTS):
        mine = pl.multiple_of(core * SUM_ROWS[kind] + first, 256)
        load = pltpu.make_async_copy(
            inputs[kind].at[pl.ds(mine, rows)], held[kind].at[pl.ds(first, rows)], load_sem.at[p]
        )
        load.start()
        loads.append(load)
    pl.semaphore_wait(barrier, 10)
    swaps = []
    for p, (rows, first, order, kind) in enumerate(SUM_PARTS):
        yours = pl.multiple_of((1 - core) * SUM_ROWS[kind] + first, 256)
        swap = pltpu.make_async_remote_copy(
            inputs[kind].at[pl.ds(yours, rows)],
            other[kind].at[pl.ds(first, rows)],
            core_send.at[p],
            core_recv.at[p],
            device_id=axis_peer("core", 1),
            device_id_type=MESH_ID,
        )
        swap.start()
        swaps.append(swap)

    def add_rows(kind, start, rows, terms):
        if kind == 1:
            tile = min(rows, 128)
        else:
            tile = 80 if rows % 80 == 0 else 96
            tile = tile * 4 if rows % (tile * 4) == 0 else tile

        def body(i, carry):
            offset = pl.multiple_of(i * tile, 8 if kind == 1 else 16)
            here = pl.ds(pl.multiple_of(start + offset, 8 if kind == 1 else 16), tile)
            total = held[kind][here, :].astype(jnp.float32)
            for ref, base in terms:
                total = total + ref[pl.ds(pl.multiple_of(base + offset, 8 if kind == 1 else 16), tile), :].astype(jnp.float32)
            held[kind][here, :] = total.astype(held[kind].dtype)
            return carry

        lax.fori_loop(0, rows // tile, body, 0)

    def start_hop(p, level):
        rows, first, order, kind = SUM_PARTS[p]
        size = rows // 4 ** (level + 1)
        base = first
        for done in range(level):
            base = base + place[order[done]] * (rows // 4 ** (done + 1))
        axis = order[level]
        hops = []
        for step in (1, 2, 3):
            block = lax.rem(place[axis] + step, 4)
            hop = pltpu.make_async_remote_copy(
                held[kind].at[pl.ds(pl.multiple_of(base + block * size, 8 if kind == 1 else 16), size)],
                slots[p * 3 + level].at[pl.ds((step - 1) * size, size)],
                hop_send.at[p, level, step - 1],
                hop_recv.at[p, level, step - 1],
                device_id=axis_peer(axis, step),
                device_id_type=MESH_ID,
            )
            hop.start()
            hops.append(hop)
        return hops

    def end_hop(p, level, hops):
        rows, first, order, kind = SUM_PARTS[p]
        size = rows // 4 ** (level + 1)
        base = first
        for done in range(level + 1):
            base = base + place[order[done]] * (rows // 4 ** (done + 1))
        for hop in hops:
            hop.wait()
        add_rows(kind, base, size, [(slots[p * 3 + level], step * size) for step in range(3)])

    count = len(SUM_PARTS)
    flight = [None] * count
    for p in range(count):
        rows, first, order, kind = SUM_PARTS[p]
        loads[p].wait()
        swaps[p].wait()
        add_rows(kind, first, rows, [(other[kind], first)])
        flight[p] = start_hop(p, 0)
    for level in (1, 2):
        for p in range(count):
            end_hop(p, level - 1, flight[p])
            flight[p] = start_hop(p, level)

    def place_of(p, levels):
        rows, first, order, kind = SUM_PARTS[p]
        base = first
        for done in range(levels):
            base = base + place[order[done]] * (rows // 4 ** (done + 1))
        return base

    def gather(p, level):
        rows, first, order, kind = SUM_PARTS[p]
        size = rows // 4 ** (level + 1)
        align = 8 if kind == 1 else 16
        here = pl.multiple_of(place_of(p, level + 1), align)
        there = pl.multiple_of(place_of(p, level + 1) + core * SUM_ROWS[kind], align)
        source = held[kind].at[pl.ds(here, size)] if level == 2 else results[kind].at[pl.ds(there, size)]
        moves = []
        for step in (1, 2, 3):
            move = pltpu.make_async_remote_copy(
                source,
                results[kind].at[pl.ds(there, size)],
                gather_send.at[p, level, step - 1],
                gather_recv.at[p, level, step - 1],
                device_id=axis_peer(order[level], step),
                device_id_type=MESH_ID,
            )
            move.start()
            moves.append(move)
        if level == 2:
            keep = pltpu.make_async_copy(source, results[kind].at[pl.ds(there, size)], copy_sem.at[p])
            keep.start()
            keep.wait()
        return moves

    for p in range(count):
        end_hop(p, 2, flight[p])
        flight[p] = gather(p, 2)
    for level in (1, 0):
        for p in range(count):
            for move in flight[p]:
                move.wait()
            flight[p] = gather(p, level)
    lasts = []
    for p in range(count):
        rows, first, order, kind = SUM_PARTS[p]
        size = rows // 4
        for index in range(4):
            if index > 0:
                flight[p][index - 1].wait()
            block = lax.rem(place[order[0]] + 4 - index, 4)
            there = pl.ds(pl.multiple_of(first + block * size + core * SUM_ROWS[kind], 8 if kind == 1 else 16), size)
            last = pltpu.make_async_remote_copy(
                results[kind].at[there],
                results[kind].at[there],
                last_send.at[p, index],
                last_recv.at[p, index],
                device_id=axis_peer("core", 1),
                device_id_type=MESH_ID,
            )
            last.start()
            lasts.append(last)
    for last in lasts:
        last.wait()


def sum_over_devices(weights, small):
    scratch = [
        pltpu.VMEM((SUM_ROWS[0], 128), jnp.bfloat16),
        pltpu.VMEM((SUM_ROWS[1], 128), jnp.float32),
        pltpu.VMEM((SUM_ROWS[0], 128), jnp.bfloat16),
        pltpu.VMEM((SUM_ROWS[1], 128), jnp.float32),
    ]
    for rows, first, order, kind in SUM_PARTS:
        for level in range(3):
            scratch.append(
                pltpu.VMEM((3 * rows // 4 ** (level + 1), 128), jnp.float32 if kind == 1 else jnp.bfloat16)
            )
    count = len(SUM_PARTS)
    dma = pltpu.SemaphoreType.DMA
    scratch += [
        dma((count,)),
        dma((count,)),
        dma((count,)),
        dma((count, 3, 3)),
        dma((count, 3, 3)),
        dma((count, 3, 3)),
        dma((count, 3, 3)),
        dma((count,)),
        dma((count, 4)),
        dma((count, 4)),
    ]
    return pl.pallas_call(
        sum_kernel,
        out_shape=(
            jax.ShapeDtypeStruct((2 * SUM_ROWS[0], 128), jnp.bfloat16),
            jax.ShapeDtypeStruct((2 * SUM_ROWS[1], 128), jnp.float32),
        ),
        in_specs=[pl.BlockSpec(memory_space=pl.ANY)] * 2,
        out_specs=[pl.BlockSpec(memory_space=pl.ANY)] * 2,
        scratch_shapes=scratch,
        compiler_params=pltpu.CompilerParams(
            collective_id=4, has_side_effects=True, vmem_limit_bytes=48 * 1024 * 1024
        ),
        name="sum_over_devices",
    )(weights, small)


def pack_small(parts):
    rows = []
    for part in parts:
        flat = part.reshape(-1)
        pad = -flat.shape[0] % 1024
        rows.append(jnp.pad(flat, (0, pad)).reshape(-1, 128))
    packed = jnp.concatenate(rows, axis=0)
    return jnp.pad(packed, ((0, 2 * SUM_ROWS[1] - packed.shape[0]), (0, 0)))


def per_device(
    tokens_in,
    out_cot,
    long_lengths,
    short_lengths,
    routes,
    gain_attn,
    w_query,
    w_key,
    w_value,
    w_out,
    rel_bias,
    gain_moe,
    router,
    w_gate,
    w_up,
    w_down,
):
    tok_dev, width = tokens_in.shape
    experts = router.shape[1]
    local_experts = w_gate.shape[0]
    buckets_count = rel_bias.shape[0]
    topk = routes.shape[1]
    long_rows = UNITS * LONG_DEV
    long_len = LONG_DEV * lax.axis_size("row")
    capacity = (10 * tok_dev + 4 * experts - 1) // (4 * experts)

    def heads(rows, count, length):
        return rows.reshape(count, length, HEADS, HEAD_DIM)

    inputs = tokens_in.astype(jnp.float32)
    normed_a, norm_a_back = jax.vjp(rms_norm, inputs, gain_attn)
    normed_ab = normed_a.astype(jnp.bfloat16)
    query = jnp.dot(normed_ab, w_query, preferred_element_type=jnp.float32).astype(jnp.bfloat16)
    keys = jnp.dot(normed_ab, w_key, preferred_element_type=jnp.float32).astype(jnp.bfloat16)
    values = jnp.dot(normed_ab, w_value, preferred_element_type=jnp.float32).astype(jnp.bfloat16)
    long_kg, long_vg = (
        lax.all_gather(keys[:long_rows].reshape(UNITS, LONG_DEV, width), "row", axis=1, tiled=True),
        lax.all_gather(
            values[:long_rows].reshape(UNITS, LONG_DEV, width), "row", axis=1, tiled=True
        ),
    )
    long_q = heads(query[:long_rows], UNITS, LONG_DEV)
    long_k = heads(long_kg, UNITS, long_len)
    long_v = heads(long_vg, UNITS, long_len)
    short_q = heads(query[long_rows:], UNITS, SHORT_LEN)
    short_k = heads(keys[long_rows:], UNITS, SHORT_LEN)
    short_v = heads(values[long_rows:], UNITS, SHORT_LEN)
    long_qpos = lax.axis_index("row") * LONG_DEV + jnp.arange(LONG_DEV, dtype=jnp.int32)
    long_kpos = jnp.arange(long_len, dtype=jnp.int32)
    short_pos = jnp.arange(SHORT_LEN, dtype=jnp.int32)
    long_hot = bucket_table(long_qpos, long_kpos, buckets_count)
    short_hot = bucket_table(short_pos, short_pos, buckets_count)
    long_bias = jnp.einsum("nqk,nh->hqk", long_hot, rel_bias, precision=highest)
    short_bias = jnp.einsum("nqk,nh->hqk", short_hot, rel_bias, precision=highest)
    long_valid = long_kpos[None, :] < long_lengths[:, None]
    short_valid = short_pos[None, :] < short_lengths[:, None]
    long_o, long_norm = attend_forward(long_q, long_k, long_v, long_bias, long_valid)
    short_o, short_norm = attend_forward(short_q, short_k, short_v, short_bias, short_valid)
    mixed = jnp.concatenate([long_o.reshape(long_rows, width), short_o.reshape(-1, width)], axis=0)
    branch_a = jnp.dot(mixed, w_out, preferred_element_type=jnp.float32)
    resid = inputs + branch_a
    normed_m, norm_m_back = jax.vjp(rms_norm, resid, gain_moe)
    normed_mb = normed_m.astype(jnp.bfloat16)
    logits = jnp.dot(normed_m, router, precision=highest, preferred_element_type=jnp.float32)
    row_max = jnp.max(logits, axis=1, keepdims=True)
    exp_terms = jnp.exp(logits - row_max)
    row_total = jnp.sum(exp_terms, axis=1, keepdims=True)
    probs = exp_terms / row_total
    router_norm = row_max[:, 0] + jnp.log(row_total[:, 0])
    expert_ids = jnp.arange(experts, dtype=jnp.int32)
    route_match = routes[:, :, None] == expert_ids[None, None, :]
    route_hot = route_match.astype(jnp.float32)
    picked = jnp.sum(probs[:, None, :] * route_hot, axis=2)
    picked_sum = jnp.sum(picked, axis=1, keepdims=True)
    gates = picked / picked_sum
    fraction = jnp.sum(route_hot, axis=(0, 1)) / (topk * tok_dev)
    flat_hot = route_match.astype(jnp.int32).reshape(-1, experts)
    earlier = jnp.cumsum(flat_hot, axis=0) - flat_hot
    slots = jnp.sum(earlier * flat_hot, axis=1).reshape(tok_dev, topk)
    place = routes * capacity + slots
    slot_ids = jnp.arange(experts * capacity, dtype=jnp.int32)
    place_hot = (jnp.transpose(place)[:, :, None] == slot_ids[None, None, :]).astype(jnp.bfloat16)
    buffer = jnp.einsum(
        "ktp,td->pd", place_hot, normed_mb, preferred_element_type=jnp.float32
    ).astype(jnp.bfloat16)
    received = lax.all_to_all(
        buffer.reshape(experts, capacity, width), "col", split_axis=0, concat_axis=0, tiled=True
    )
    received = received.reshape(-1, local_experts, capacity, width)
    gate_full, up_full, down_full = (
        lax.all_gather(w_gate, "row", axis=2, tiled=True),
        lax.all_gather(w_up, "row", axis=2, tiled=True),
        lax.all_gather(w_down, "row", axis=1, tiled=True),
    )
    gate_pre = jnp.einsum("sjcd,jdf->sjcf", received, gate_full, preferred_element_type=jnp.float32)
    up_pre = jnp.einsum("sjcd,jdf->sjcf", received, up_full, preferred_element_type=jnp.float32)
    act_b = geglu(gate_pre, up_pre).astype(jnp.bfloat16)
    expert_out = jnp.einsum("sjcf,jfd->sjcd", act_b, down_full, preferred_element_type=jnp.float32)
    returned = lax.all_to_all(
        expert_out.astype(jnp.bfloat16), "col", split_axis=0, concat_axis=0, tiled=True
    ).reshape(experts * capacity, width)
    chosen = jnp.einsum("ktp,pd->tkd", place_hot, returned, preferred_element_type=jnp.float32)
    branch_m = jnp.sum(gates[:, :, None] * chosen, axis=1)
    outputs = resid + branch_m
    long_live = (long_qpos[None, :] < long_lengths[:, None]).reshape(-1)
    short_live = (short_pos[None, :] < short_lengths[:, None]).reshape(-1)
    live = jnp.concatenate([long_live, short_live]).astype(jnp.float32)

    def live_squares(field):
        return jnp.sum(live * jnp.sum(field * field, axis=1))

    tallies = jnp.stack(
        [live_squares(outputs), live_squares(branch_a), live_squares(branch_m), jnp.sum(live)]
    )
    d_out = out_cot.astype(jnp.float32)
    weighted = (gates[:, :, None] * d_out[:, None, :]).astype(jnp.bfloat16)
    d_returned = jnp.einsum(
        "ktp,tkd->pd", place_hot, weighted, preferred_element_type=jnp.float32
    ).astype(jnp.bfloat16)
    d_gates = jnp.sum(chosen * d_out[:, None, :], axis=2)
    d_picked = d_gates / picked_sum - jnp.sum(d_gates * picked, axis=1, keepdims=True) / (
        picked_sum * picked_sum
    )
    d_probs = (
        jnp.sum(d_picked[:, :, None] * route_hot, axis=1)
        + balance_coef * experts * fraction[None, :]
    )
    d_logits = (
        probs * (d_probs - jnp.sum(d_probs * probs, axis=1, keepdims=True))
        + 2.0 * zloss_coef * router_norm[:, None] * probs
    )
    d_router = jnp.einsum(
        "td,te->de", normed_m, d_logits, precision=highest, preferred_element_type=jnp.float32
    )
    d_normed = jnp.einsum(
        "te,de->td", d_logits, router, precision=highest, preferred_element_type=jnp.float32
    )
    d_received = lax.all_to_all(
        d_returned.reshape(experts, capacity, width), "col", split_axis=0, concat_axis=0, tiled=True
    )
    d_received = d_received.reshape(-1, local_experts, capacity, width)
    d_act = jnp.einsum("sjcd,jfd->sjcf", d_received, down_full, preferred_element_type=jnp.float32)
    d_gate_b, d_up_b = geglu_back(gate_pre, up_pre, d_act)
    d_down_full = jnp.einsum(
        "sjcf,sjcd->jfd", act_b, d_received, preferred_element_type=jnp.float32
    )
    d_gate_full = jnp.einsum(
        "sjcd,sjcf->jdf", received, d_gate_b, preferred_element_type=jnp.float32
    )
    d_up_full = jnp.einsum("sjcd,sjcf->jdf", received, d_up_b, preferred_element_type=jnp.float32)
    d_rows = jnp.einsum("sjcf,jdf->sjcd", d_gate_b, gate_full, preferred_element_type=jnp.float32)
    d_rows = d_rows + jnp.einsum(
        "sjcf,jdf->sjcd", d_up_b, up_full, preferred_element_type=jnp.float32
    )
    d_gate_w, d_up_w, d_down_w = (
        lax.psum_scatter(
            d_gate_full.astype(jnp.bfloat16), "row", scatter_dimension=2, tiled=True
        ).astype(jnp.float32),
        lax.psum_scatter(
            d_up_full.astype(jnp.bfloat16), "row", scatter_dimension=2, tiled=True
        ).astype(jnp.float32),
        lax.psum_scatter(
            d_down_full.astype(jnp.bfloat16), "row", scatter_dimension=1, tiled=True
        ).astype(jnp.float32),
    )
    d_sent = lax.all_to_all(
        d_rows.astype(jnp.bfloat16), "col", split_axis=0, concat_axis=0, tiled=True
    ).reshape(experts * capacity, width)
    d_normed = d_normed + jnp.einsum(
        "ktp,pd->td", place_hot, d_sent, preferred_element_type=jnp.float32
    )
    d_resid_norm, d_gain_m = norm_m_back(d_normed)
    d_resid = d_out + d_resid_norm
    d_branch = d_resid.astype(jnp.bfloat16)
    d_w_out = jnp.einsum("td,te->de", mixed, d_branch, preferred_element_type=jnp.float32)
    d_mixed = jnp.einsum("te,de->td", d_branch, w_out, preferred_element_type=jnp.float32).astype(
        jnp.bfloat16
    )
    long_dq, long_dk, long_dv, long_ds = attend_backward(
        long_q,
        long_k,
        long_v,
        long_bias,
        long_valid,
        long_norm,
        heads(d_mixed[:long_rows], UNITS, LONG_DEV),
    )
    short_dq, short_dk, short_dv, short_ds = attend_backward(
        short_q,
        short_k,
        short_v,
        short_bias,
        short_valid,
        short_norm,
        heads(d_mixed[long_rows:], UNITS, SHORT_LEN),
    )
    own_dk, own_dv = (
        lax.psum_scatter(
            long_dk.reshape(UNITS, long_len, width).astype(jnp.bfloat16),
            "row",
            scatter_dimension=1,
            tiled=True,
        ).astype(jnp.float32),
        lax.psum_scatter(
            long_dv.reshape(UNITS, long_len, width).astype(jnp.bfloat16),
            "row",
            scatter_dimension=1,
            tiled=True,
        ).astype(jnp.float32),
    )
    d_bias = jnp.einsum(
        "bhqk,nqk->nh", long_ds, long_hot.astype(jnp.bfloat16), preferred_element_type=jnp.float32
    )
    d_bias = d_bias + jnp.einsum(
        "bhqk,nqk->nh", short_ds, short_hot.astype(jnp.bfloat16), preferred_element_type=jnp.float32
    )
    d_query = jnp.concatenate(
        [long_dq.reshape(long_rows, width), short_dq.reshape(-1, width)], axis=0
    ).astype(jnp.bfloat16)
    d_keys = jnp.concatenate(
        [own_dk.reshape(long_rows, width), short_dk.reshape(-1, width)], axis=0
    ).astype(jnp.bfloat16)
    d_values = jnp.concatenate(
        [own_dv.reshape(long_rows, width), short_dv.reshape(-1, width)], axis=0
    ).astype(jnp.bfloat16)
    d_w_query = jnp.einsum("td,te->de", normed_ab, d_query, preferred_element_type=jnp.float32)
    d_w_key = jnp.einsum("td,te->de", normed_ab, d_keys, preferred_element_type=jnp.float32)
    d_w_value = jnp.einsum("td,te->de", normed_ab, d_values, preferred_element_type=jnp.float32)
    d_normed_a = jnp.einsum("te,de->td", d_query, w_query, preferred_element_type=jnp.float32)
    d_normed_a = d_normed_a + jnp.einsum(
        "te,de->td", d_keys, w_key, preferred_element_type=jnp.float32
    )
    d_normed_a = d_normed_a + jnp.einsum(
        "te,de->td", d_values, w_value, preferred_element_type=jnp.float32
    )
    d_inputs_norm, d_gain_a = norm_a_back(d_normed_a)
    d_inputs = d_resid + d_inputs_norm
    grads = jnp.stack([d_w_query, d_w_key, d_w_value, d_w_out]).astype(jnp.bfloat16)
    grads = grads.reshape(4, width, 8, 128).transpose(0, 2, 1, 3).reshape(-1, 128)
    small = pack_small([jnp.transpose(d_router), d_gain_a, d_gain_m, d_bias, tallies])
    grads, small = sum_over_devices(grads, small)
    grads = grads.reshape(4, 8, width, 128).transpose(0, 2, 1, 3).reshape(4, width, width)
    grads = grads.astype(jnp.float32)
    summed = (
        small[256:264].reshape(-1),
        grads[0],
        grads[1],
        grads[2],
        grads[3],
        small[272:276].reshape(buckets_count, HEADS),
        small[264:272].reshape(-1),
        jnp.transpose(small[0:256].reshape(experts, width)),
        small[280],
    )
    totals = summed[8]
    statistics = jnp.stack(
        [
            jnp.sqrt(totals[0] / (totals[3] * width)),
            jnp.sqrt(totals[1] / (totals[3] * width)),
            jnp.sqrt(totals[2] / (totals[3] * width)),
        ]
    )
    return (
        outputs,
        d_inputs,
        summed[0],
        summed[1],
        summed[2],
        summed[3],
        summed[4],
        summed[5],
        summed[6],
        summed[7],
        d_gate_w,
        d_up_w,
        d_down_w,
        statistics,
    )


def solution(mesh):
    placed = (
        P(("row", "col"), None),
        P(("row", "col"), None),
        P("col"),
        P(("row", "col")),
        P(("row", "col"), None),
        P(),
        P(),
        P(),
        P(),
        P(),
        P(),
        P(),
        P(),
        P("col", None, "row"),
        P("col", None, "row"),
        P("col", "row", None),
    )
    return jax.shard_map(
        per_device,
        mesh=mesh,
        in_specs=placed,
        out_specs=(
            P(("row", "col"), None),
            P(("row", "col"), None),
            P(),
            P(),
            P(),
            P(),
            P(),
            P(),
            P(),
            P(),
            P("col", None, "row"),
            P("col", None, "row"),
            P("col", "row", None),
            P(),
        ),
        check_vma=False,
    )
```

```python
import functools

import numpy as np
import jax
import jax.numpy as jnp
from jax import lax
from jax.experimental import pallas as pl
from jax.experimental.pallas import tpu as pltpu
from jax.sharding import PartitionSpec as P

HEADS = 16
HEAD_DIM = 64
WIDTH = 1024
ROWS = 256
LONG = 128
EXPERTS = 32
SLOTS = 20
FOLDED = 80
QUARTER = 256
PIECES = EXPERTS * FOLDED
TABLE = 640
SHARD = 704
HALF = 2 * SHARD

bucket_edges = (1, 2, 3, 4, 5, 6, 7, 8, 12, 16, 23, 32, 46, 64, 91)
norm_eps = 1e-06
balance_coef = 0.01
zloss_coef = 0.001
masked_score = -1e30
highest = lax.Precision.HIGHEST
MESH_ID = pl.DeviceIdType.MESH
F32 = jnp.float32
BF16 = jnp.bfloat16
VMEM_SPEC = pl.BlockSpec(memory_space=pltpu.VMEM)
HBM_SPEC = pl.BlockSpec(memory_space=pl.ANY)
SMEM_SPEC = pl.BlockSpec(memory_space=pltpu.SMEM)
DMA = pltpu.SemaphoreType.DMA


def piece_ids():
    row = np.arange(PIECES)
    slot = (row // FOLDED) * SLOTS + row % SLOTS
    quarter = (row % FOLDED) // SLOTS
    return np.stack([slot, quarter]).astype(np.float32)


def unfold_matrix():
    out = np.arange(320)
    quarter, message, slot = out // 80, (out % 80) // SLOTS, out % SLOTS
    hot = np.zeros((320, 320), np.float32)
    hot[out, message * FOLDED + quarter * SLOTS + slot] = 1
    return hot


def nt(left, right, precision=None):
    return lax.dot_general(
        left, right, (((1,), (1,)), ((), ())), preferred_element_type=F32, precision=precision
    )


def tn(left, right):
    return lax.dot_general(left, right, (((0,), (0,)), ((), ())), preferred_element_type=F32)


def nn(left, right, precision=None):
    return jnp.dot(left, right, preferred_element_type=F32, precision=precision)


def iota(shape, dim):
    return lax.broadcasted_iota(jnp.int32, shape, dim)


def block(index, size):
    return pl.ds(pl.multiple_of(index * size, size), size)


def bucket_hot(relative):
    magnitude = jnp.abs(relative)
    level = jnp.zeros_like(relative)
    for edge in bucket_edges:
        level = level + (magnitude >= edge).astype(jnp.int32)
    level = level + jnp.where(relative > 0, len(bucket_edges) + 1, 0)
    return (iota((32, relative.shape[1]), 0) == level).astype(F32)


def route_places(routes_t):
    hots = [(iota((EXPERTS, ROWS), 0) == routes_t[k : k + 1, :]).astype(F32) for k in range(2)]
    both = hots[0] + hots[1]
    before = (iota((ROWS, ROWS), 0) < iota((ROWS, ROWS), 1)).astype(BF16)
    earlier = nn(both.astype(BF16), before)
    slots = [jnp.sum(earlier * hot, axis=0, keepdims=True) for hot in hots]
    places = [routes_t[k : k + 1, :].astype(F32) * SLOTS + slots[k] for k in range(2)]
    return hots, both, slots, places


def slot_hot(slots_row):
    return (iota((128, ROWS), 0).astype(F32) == slots_row).astype(F32)


def live_column(long_len, short_len, row):
    position = iota((ROWS, 1), 0)
    is_long = position < LONG
    here = jnp.where(is_long, position + row * LONG, position - LONG)
    limit = jnp.where(is_long, long_len, short_len)
    return (here < limit).astype(F32)


def forward_kernel(
    long_len, short_len, tokens, cot, routes_t, gain_a, gain_m, rel_bias_t, router_t, ids, wq, wk, wv, wo,
    x_slots, o_slots, g_slots, query, long_kv, short_kv, mixed, norm_l, norm_s, resid, probs_t, rnorm_t,
    normed, buffer_o, buffer_x, gate_out, table_l, table_s,
    o_send, o_recv, x_send, x_recv, g_send, g_recv, own_sem, kv_send, kv_recv, t_send, t_recv,
):
    row = lax.axis_index("row")
    col = lax.axis_index("col")
    mate = 3 - row
    barrier = pltpu.get_barrier_semaphore()
    for step in (1, 2, 3):
        pl.semaphore_signal(barrier, inc=1, device_id=(lax.rem(row + step, 4), col), device_id_type=MESH_ID)

    def greet(step, carry):
        pl.semaphore_signal(barrier, inc=1, device_id=(row, lax.rem(col + step, EXPERTS)), device_id_type=MESH_ID)
        return carry

    lax.fori_loop(1, EXPERTS, greet, 0)

    hots, both, slots, places = route_places(routes_t[...])

    def message(buffer, slots_ref, send, recv, dest, source):
        return pltpu.make_async_remote_copy(
            buffer.at[block(dest, FOLDED)],
            slots_ref.at[0, block(source, FOLDED)],
            send.at[dest],
            recv.at[source],
            device_id=(row, dest),
            device_id_type=MESH_ID,
        )

    def dispatch(source, buffer, slots_ref, send, recv, own):
        def one_group(i, carry):
            group = lax.rem(lax.div(col, 4) + i, 8)
            rows = block(group, 320)
            slot_id = ids[rows, 0:1]
            quarter = ids[rows, 1:2]
            match = (slot_id == places[0]) | (slot_id == places[1])
            total = jnp.zeros((320, QUARTER), F32)
            for q in range(4):
                hot = jnp.where(match & (quarter == q), 1.0, 0.0).astype(BF16)
                total = total + nn(hot, source[:, q * QUARTER : (q + 1) * QUARTER])
            buffer[rows, :] = total.astype(BF16)
            for j in range(4):
                dest = group * 4 + j

                @pl.when(dest != col)
                def _():
                    message(buffer, slots_ref, send, recv, dest, col).start()

                @pl.when(dest == col)
                def _():
                    pltpu.make_async_copy(
                        buffer.at[block(dest, FOLDED)], slots_ref.at[0, block(dest, FOLDED)], own
                    ).start()

            return carry

        lax.fori_loop(0, 8, one_group, 0)

    def wait_source(buffer, slots_ref, send, recv, own, source):
        @pl.when(source != col)
        def _():
            message(buffer, slots_ref, send, recv, col, source).wait_recv()

        @pl.when(source == col)
        def _():
            pltpu.make_async_copy(
                buffer.at[block(col, FOLDED)], slots_ref.at[0, block(col, FOLDED)], own
            ).wait()

    def wait_sends(buffer, slots_ref, send, recv):
        def one(step, carry):
            message(buffer, slots_ref, send, recv, lax.rem(col + step, EXPERTS), col).wait_send()
            return carry

        lax.fori_loop(1, EXPERTS, one, 0)

    pl.semaphore_wait(barrier, EXPERTS + 2)

    def norm_rows(i, carry):
        rows = block(i, 64)
        x = tokens[rows, :].astype(F32)
        scale = lax.rsqrt(jnp.mean(x * x, axis=1, keepdims=True) + norm_eps)
        normed[rows, :] = (x * scale * gain_a[...]).astype(BF16)
        return carry

    lax.fori_loop(0, 4, norm_rows, 0)

    def project_kv(i, carry):
        lanes = block(i, 256)
        for offset, weight in ((0, wk), (WIDTH, wv)):
            part = nn(normed[...], weight[:, lanes]).astype(BF16)
            out = pl.ds(pl.multiple_of(i * 256 + offset, 256), 256)
            long_kv[row, :, out] = part[:LONG]
            short_kv[:, out] = part[LONG:]
        return carry

    lax.fori_loop(0, 4, project_kv, 0)

    def kv_move(step):
        return pltpu.make_async_remote_copy(
            long_kv.at[row],
            long_kv.at[row],
            kv_send.at[step - 1],
            kv_recv.at[step - 1],
            device_id=(lax.rem(row + step, 4), col),
            device_id_type=MESH_ID,
        )

    def kv_arrival(step):
        source = lax.rem(row + 4 - step, 4)
        return pltpu.make_async_remote_copy(
            long_kv.at[source],
            long_kv.at[source],
            kv_send.at[step - 1],
            kv_recv.at[step - 1],
            device_id=(source, col),
            device_id_type=MESH_ID,
        )

    for step in (1, 2, 3):
        kv_move(step).start()

    dispatch(cot, buffer_o, o_slots, o_send, o_recv, own_sem.at[0])

    def project_q(i, carry):
        lanes = block(i, 256)
        query[:, lanes] = nn(normed[...], wq[:, lanes]).astype(BF16)
        return carry

    lax.fori_loop(0, 4, project_q, 0)

    place_l = iota((1, TABLE), 1)
    place_l = jnp.where(place_l < 512, place_l, place_l - TABLE) - row * LONG
    place_s = iota((1, 256), 1)
    place_s = jnp.where(place_s < 128, place_s, place_s - 256)
    table_l[...] = nn(rel_bias_t[...], bucket_hot(place_l), highest)
    table_s[...] = nn(rel_bias_t[...], bucket_hot(place_s), highest)

    lane = iota((1, 128), 1)

    def attend(q2, k2, v2, table, head, keep, count, width):
        bias = pltpu.roll(
            jnp.broadcast_to(table[pl.ds(head, 1), :], (128, width)), 0, 1, stride=1, stride_axis=0
        )[:, :count]
        scores = jnp.where(keep, nt(q2, k2) * 0.125 + bias, masked_score)
        row_max = jnp.max(scores, axis=1, keepdims=True)
        terms = jnp.exp(scores - row_max)
        total = jnp.sum(terms, axis=1, keepdims=True)
        return nn((terms / total).astype(BF16), v2), row_max + jnp.log(total)

    def attend_pairs(q_first, keys_of, table, keep, count, width, norm_out):
        def one_pair(pair, carry):
            lanes = block(pair, 128)
            values = pl.ds(pl.multiple_of(pair * 128 + WIDTH, 128), 128)
            q2 = query[q_first : q_first + 128, lanes]
            k2, v2 = keys_of(lanes), keys_of(values)
            outs = []
            norms = norm_out[...]
            for side in range(2):
                here = (lane >= 64) if side else (lane < 64)
                out, norm = attend(
                    jnp.where(here, q2, jnp.zeros_like(q2)), k2, v2, table, pair * 2 + side, keep, count, width
                )
                outs.append(out)
                norms = jnp.where(lane == pair * 2 + side, norm, norms)
            norm_out[...] = norms
            mixed[q_first : q_first + 128, lanes] = jnp.where(lane < 64, outs[0], outs[1]).astype(BF16)
            return carry

        lax.fori_loop(0, HEADS // 2, one_pair, 0)

    norm_l[...] = jnp.zeros_like(norm_l)
    norm_s[...] = jnp.zeros_like(norm_s)
    attend_pairs(LONG, lambda lanes: short_kv[:, lanes], table_s, iota((1, 128), 1) < short_len[0], 128, 256, norm_s)

    def wait_o(source, carry):
        wait_source(buffer_o, o_slots, o_send, o_recv, own_sem.at[0], source)
        return carry

    lax.fori_loop(0, EXPERTS, wait_o, 0)

    def to_mate(source, target, index):
        return pltpu.make_async_remote_copy(
            source, target, t_send.at[index], t_recv.at[index], device_id=(mate, col), device_id_type=MESH_ID
        )

    for step in (1, 2, 3):
        kv_arrival(step).wait_recv()
    o_move = to_mate(o_slots.at[0], o_slots.at[1], 8)
    o_move.start()
    attend_pairs(
        0,
        lambda lanes: long_kv[:, :, lanes].reshape(512, 128),
        table_l,
        iota((1, 512), 1) < long_len[0],
        512,
        TABLE,
        norm_l,
    )

    def project_out(i, carry):
        lanes = block(i, 256)
        resid[:, lanes] = tokens[:, lanes].astype(F32) + nn(mixed[...], wo[:, lanes])
        return carry

    lax.fori_loop(0, 4, project_out, 0)

    def norm_again(i, carry):
        rows = block(i, 64)
        x = resid[rows, :]
        scale = lax.rsqrt(jnp.mean(x * x, axis=1, keepdims=True) + norm_eps)
        normed[rows, :] = (x * scale * gain_m[...]).astype(BF16)
        return carry

    lax.fori_loop(0, 4, norm_again, 0)
    dispatch(normed, buffer_x, x_slots, x_send, x_recv, own_sem.at[1])

    x = resid[...]
    scale = lax.rsqrt(jnp.mean(x * x, axis=1, keepdims=True) + norm_eps)
    logits = nt(router_t[...], x * scale * gain_m[...], highest)
    row_max = jnp.max(logits, axis=0, keepdims=True)
    terms = jnp.exp(logits - row_max)
    total = jnp.sum(terms, axis=0, keepdims=True)
    probs = terms / total
    probs_t[...] = probs
    rnorm_t[...] = row_max + jnp.log(total)
    picked = [jnp.sum(probs * hot, axis=0, keepdims=True) for hot in hots]
    picked_sum = picked[0] + picked[1]
    gate_slots = jnp.zeros((EXPERTS, 128), F32)
    for k in range(2):
        gate_slots = gate_slots + nt(hots[k] * (picked[k] / picked_sum), slot_hot(slots[k]), highest)
    for e in range(EXPERTS):
        gate_out[e] = jnp.broadcast_to(gate_slots[e : e + 1, :], (8, 128))

    def gate_message(dest, source):
        return pltpu.make_async_remote_copy(
            gate_out.at[dest],
            g_slots.at[0, source],
            g_send.at[dest],
            g_recv.at[source],
            device_id=(row, dest),
            device_id_type=MESH_ID,
        )

    def send_gates(step, carry):
        gate_message(lax.rem(col + step, EXPERTS), col).start()
        return carry

    lax.fori_loop(1, EXPERTS, send_gates, 0)
    own_gates = pltpu.make_async_copy(gate_out.at[col], g_slots.at[0, col], own_sem.at[2])
    own_gates.start()

    def x_move(group):
        rows = block(group, 320)
        return to_mate(x_slots.at[0, rows], x_slots.at[1, rows], group)

    def forward_x(i, carry):
        group = lax.rem(lax.div(col, 4) + 8 - i, 8)
        for j in range(4):
            wait_source(buffer_x, x_slots, x_send, x_recv, own_sem.at[1], group * 4 + j)
        x_move(group).start()
        return carry

    lax.fori_loop(0, 8, forward_x, 0)

    def wait_gates(step, carry):
        gate_message(col, lax.rem(col + step, EXPERTS)).wait_recv()
        return carry

    lax.fori_loop(1, EXPERTS, wait_gates, 0)
    own_gates.wait()
    g_move = to_mate(g_slots.at[0], g_slots.at[1], 9)
    g_move.start()

    for step in (1, 2, 3):
        kv_move(step).wait_send()
    wait_sends(buffer_o, o_slots, o_send, o_recv)
    wait_sends(buffer_x, x_slots, x_send, x_recv)

    def wait_gate_sends(step, carry):
        gate_message(lax.rem(col + step, EXPERTS), col).wait_send()
        return carry

    lax.fori_loop(1, EXPERTS, wait_gate_sends, 0)
    o_move.wait()

    def wait_x(group, carry):
        x_move(group).wait()
        return carry

    lax.fori_loop(0, 8, wait_x, 0)
    g_move.wait()


def forward(long_lengths, short_lengths, tokens, cot, routes_t, gain_a, gain_m, rel_bias_t, router_t, ids, wq, wk, wv, wo):
    def out(shape, dtype):
        return jax.ShapeDtypeStruct(shape, dtype)

    return pl.pallas_call(
        forward_kernel,
        out_shape=(
            out((2, PIECES, QUARTER), BF16),
            out((2, PIECES, QUARTER), BF16),
            out((2, EXPERTS, 8, 128), F32),
            out((ROWS, WIDTH), BF16),
            out((4, LONG, 2 * WIDTH), BF16),
            out((LONG, 2 * WIDTH), BF16),
            out((ROWS, WIDTH), BF16),
            out((128, 128), F32),
            out((128, 128), F32),
            out((ROWS, WIDTH), F32),
            out((EXPERTS, ROWS), F32),
            out((1, ROWS), F32),
        ),
        in_specs=[SMEM_SPEC] * 2 + [VMEM_SPEC] * 12,
        out_specs=[HBM_SPEC] * 3 + [VMEM_SPEC] * 9,
        scratch_shapes=[
            pltpu.VMEM((ROWS, WIDTH), BF16),
            pltpu.VMEM((PIECES, QUARTER), BF16),
            pltpu.VMEM((PIECES, QUARTER), BF16),
            pltpu.VMEM((EXPERTS, 8, 128), F32),
            pltpu.VMEM((HEADS, TABLE), F32),
            pltpu.VMEM((HEADS, 256), F32),
            DMA((EXPERTS,)),
            DMA((EXPERTS,)),
            DMA((EXPERTS,)),
            DMA((EXPERTS,)),
            DMA((EXPERTS,)),
            DMA((EXPERTS,)),
            DMA((3,)),
            DMA((3,)),
            DMA((3,)),
            DMA((10,)),
            DMA((10,)),
        ],
        compiler_params=pltpu.CompilerParams(
            collective_id=1, has_side_effects=True, vmem_limit_bytes=56 * 1024 * 1024
        ),
        name="forward_and_dispatch",
    )(long_lengths, short_lengths, tokens, cot, routes_t, gain_a, gain_m, rel_bias_t, router_t, ids, wq, wk, wv, wo)


def expert_kernel(
    x_slots, o_slots, g_slots, unfold, fold, row_hot, slot_of, wg_own, wu_own, wd_own, wg_mate, wu_mate, wd_mate,
    dx_back, dg_back, outs, wg_grad, wu_grad, wd_grad, wg_send, wu_send, wd_send,
    stage, xs, os, dys, wg, wu, wd, act, dg, du, part, arrived, gate_part, gate_arrived, gate_out, grad_stage, grad_half,
    stage_sem, weight_sem, t_send, t_recv, m_send, m_recv, r_send, r_recv, own_sem, out_sem,
):
    row = lax.axis_index("row")
    col = lax.axis_index("col")
    mate = 3 - row
    barrier = pltpu.get_barrier_semaphore()
    pl.semaphore_signal(barrier, inc=1, device_id=(mate, col), device_id_type=MESH_ID)

    def greet(step, carry):
        pl.semaphore_signal(barrier, inc=1, device_id=(row, lax.rem(col + step, EXPERTS)), device_id_type=MESH_ID)
        return carry

    lax.fori_loop(1, EXPERTS, greet, 0)

    def load(source, which, index):
        return pltpu.make_async_copy(source.at[which], stage.at[index], stage_sem.at[index])

    load(x_slots, 1, 0).start()
    load(o_slots, 1, 1).start()
    weights = []
    for i, (own, other, held) in enumerate(((wg_own, wg_mate, wg), (wu_own, wu_mate, wu), (wd_own, wd_mate, wd))):
        for j, source in enumerate((own, other)):
            copy = pltpu.make_async_copy(source, held.at[pl.ds(j * SHARD, SHARD)], weight_sem.at[i, j])
            copy.start()
            weights.append(copy)

    def spread(index, target, first):
        def one(group, carry):
            wide = nn(unfold[...], stage[index, block(group, 320), :]).astype(BF16)
            rows = pl.ds(pl.multiple_of(first + group * 80, 16), 80)
            for q in range(4):
                target[rows, q * QUARTER : (q + 1) * QUARTER] = wide[q * 80 : (q + 1) * 80]
            return carry

        lax.fori_loop(0, 8, one, 0)

    def gate_column(which):
        gates = jnp.concatenate([g_slots[which, e, 0:1, :] for e in range(EXPERTS)], axis=0)
        wide = nn(row_hot[...], gates, highest)
        lanes = iota((640, 128), 1)
        return jnp.sum(jnp.where(lanes == slot_of[...], wide, 0.0), axis=1, keepdims=True)

    def hidden_tile(first, start, width):
        lanes = pl.ds(start, width)
        for part_rows in range(2):
            rows = pl.ds(first + part_rows * 320, 320)
            x = xs[rows, :]
            gate_pre = nt(x, wg[lanes, :])
            up_pre = nt(x, wu[lanes, :])
            d_act = nt(dys[rows, :], wd[lanes, :])
            square = gate_pre * gate_pre
            bend = jnp.tanh(0.7978845608028654 * gate_pre * (1.0 + 0.044715 * square))
            half = 0.5 * (1.0 + bend)
            gelu = gate_pre * half
            slope = half + 0.5 * gate_pre * (1.0 - bend * bend) * (
                0.7978845608028654 * (1.0 + 3.0 * 0.044715 * square)
            )
            act[rows, lanes] = (gelu * up_pre).astype(BF16)
            du[rows, lanes] = (d_act * gelu).astype(BF16)
            dg[rows, lanes] = (d_act * up_pre * slope).astype(BF16)

    def first_half(first):
        def one(i, carry):
            hidden_tile(first, pl.multiple_of(i * 256, 256), 256)
            return carry

        lax.fori_loop(0, 5, one, 0)
        hidden_tile(first, 1280, 128)

    def input_gradient(first, lanes):
        rows = pl.ds(first, 640)
        return nn(dg[rows, :], wg[:, lanes]) + nn(du[rows, :], wu[:, lanes])

    def to_mate(source, target, index):
        return pltpu.make_async_remote_copy(
            source, target, t_send.at[index], t_recv.at[index], device_id=(mate, col), device_id_type=MESH_ID
        )

    def output_part(first, which):
        def one(n, total):
            lanes = block(n, QUARTER)
            rows = pl.ds(first, 640)
            value = nn(act[rows, :], wd[:, lanes])
            stage[0, block(n, 640), :] = value.astype(BF16)
            return total + jnp.sum(value * os[rows, lanes].astype(F32), axis=1, keepdims=True)

        total = lax.fori_loop(0, 4, one, jnp.zeros((640, 1), F32))

        def fold_one(group, carry):
            tall = jnp.concatenate(
                [stage[0, pl.ds(pl.multiple_of(q * 640 + group * 80, 16), 80), :] for q in range(4)], axis=0
            )
            outs[which, block(group, 320), :] = nn(fold[...], tall).astype(BF16)
            return carry

        lax.fori_loop(0, 8, fold_one, 0)
        spread_out = jnp.where(iota((640, 128), 1) == slot_of[...], total, 0.0)
        return lax.dot_general(
            row_hot[...], spread_out, (((0,), (0,)), ((), ())), preferred_element_type=F32, precision=highest
        )

    load(x_slots, 1, 0).wait()
    spread(0, xs, 640)
    load(x_slots, 0, 0).start()
    load(o_slots, 1, 1).wait()
    spread(1, os, 640)
    load(o_slots, 0, 1).start()
    dys[640:1280, :] = (os[640:1280, :].astype(F32) * gate_column(1)).astype(BF16)
    load(x_slots, 0, 0).wait()
    spread(0, xs, 0)
    load(o_slots, 0, 1).wait()
    spread(1, os, 0)
    dys[0:640, :] = (os[0:640, :].astype(F32) * gate_column(0)).astype(BF16)
    for copy in weights:
        copy.wait()
    first_half(640)
    pl.semaphore_wait(barrier, EXPERTS)

    def part_move(n):
        return to_mate(part.at[block(n, 640)], arrived.at[block(n, 640)], n)

    def mate_gradient(n, carry):
        part[block(n, 640), :] = input_gradient(640, block(n, QUARTER)).astype(BF16)
        part_move(n).start()
        return carry

    lax.fori_loop(0, 4, mate_gradient, 0)
    gate_part[...] = output_part(640, 1)
    gate_move = to_mate(gate_part, gate_arrived, 4)
    gate_move.start()
    first_half(0)
    gates = output_part(0, 0)

    def own_gradient(n, carry):
        value = input_gradient(0, block(n, QUARTER))
        part_move(n).wait_recv()
        stage[1, block(n, 640), :] = (value + arrived[block(n, 640), :].astype(F32)).astype(BF16)
        return carry

    lax.fori_loop(0, 4, own_gradient, 0)
    gate_move.wait_recv()
    gates = gates + gate_arrived[...]
    for e in range(EXPERTS):
        gate_out[e] = jnp.broadcast_to(gates[e : e + 1, :], (8, 128))

    def message(dest, source):
        return pltpu.make_async_remote_copy(
            stage.at[0, block(dest, FOLDED)],
            dx_back.at[block(source, FOLDED)],
            m_send.at[dest],
            m_recv.at[source],
            device_id=(row, dest),
            device_id_type=MESH_ID,
        )

    def gate_message(dest, source):
        return pltpu.make_async_remote_copy(
            gate_out.at[dest],
            dg_back.at[source],
            r_send.at[dest],
            r_recv.at[source],
            device_id=(row, dest),
            device_id_type=MESH_ID,
        )

    own_dx = pltpu.make_async_copy(stage.at[0, block(col, FOLDED)], dx_back.at[block(col, FOLDED)], own_sem.at[0])
    own_dg = pltpu.make_async_copy(gate_out.at[col], dg_back.at[col], own_sem.at[1])

    def return_group(i, carry):
        group = lax.rem(lax.div(col, 4) + i, 8)
        tall = jnp.concatenate(
            [stage[1, pl.ds(pl.multiple_of(q * 640 + group * 80, 16), 80), :] for q in range(4)], axis=0
        )
        stage[0, block(group, 320), :] = nn(fold[...], tall).astype(BF16)
        for j in range(4):
            dest = group * 4 + j

            @pl.when(dest != col)
            def _():
                message(dest, col).start()
                gate_message(dest, col).start()

            @pl.when(dest == col)
            def _():
                own_dx.start()
                own_dg.start()

        return carry

    lax.fori_loop(0, 8, return_group, 0)

    grads = ((dg, xs, wg_grad, wg_send), (du, xs, wu_grad, wu_send), (act, dys, wd_grad, wd_send))

    def grad_copies(slot, start, width, result, send):
        copies = []
        if start < SHARD:
            rows = min(width, SHARD - start)
            copies.append((grad_stage.at[slot, pl.ds(0, rows)], result.at[pl.ds(start, rows)], out_sem.at[slot, 0]))
        if start + width > SHARD:
            skip = max(0, SHARD - start)
            copies.append(
                (
                    grad_half.at[slot, pl.ds(skip, width - skip)],
                    send.at[pl.ds(start + skip - SHARD, width - skip)],
                    out_sem.at[slot, 1],
                )
            )
        return [pltpu.make_async_copy(*copy) for copy in copies]

    pending = [[], []]
    turn = 0
    for left, right, result, send in grads:
        for start in range(0, HALF, 256):
            width = min(256, HALF - start)
            slot = turn % 2
            turn += 1
            for copy in pending[slot]:
                copy.wait()
            value = tn(left[:, start : start + width], right[...])
            if start < SHARD:
                grad_stage[slot, 0:width, :] = value
            if start + width > SHARD:
                grad_half[slot, 0:width, :] = value.astype(BF16)
            pending[slot] = grad_copies(slot, start, width, result, send)
            for copy in pending[slot]:
                copy.start()
    for copies in pending:
        for copy in copies:
            copy.wait()

    def wait_source(step, carry):
        source = lax.rem(col + step, EXPERTS)
        message(col, source).wait_recv()
        gate_message(col, source).wait_recv()
        message(source, col).wait_send()
        gate_message(source, col).wait_send()
        return carry

    lax.fori_loop(1, EXPERTS, wait_source, 0)
    own_dx.wait()
    own_dg.wait()

    def wait_parts(n, carry):
        part_move(n).wait_send()
        return carry

    lax.fori_loop(0, 4, wait_parts, 0)
    gate_move.wait_send()


def experts(x_slots, o_slots, g_slots, consts, own, other):
    def out(shape, dtype):
        return jax.ShapeDtypeStruct(shape, dtype)

    hidden = (2 * 640, HALF)
    return pl.pallas_call(
        expert_kernel,
        out_shape=(
            out((PIECES, QUARTER), BF16),
            out((EXPERTS, 8, 128), F32),
            out((2, PIECES, QUARTER), BF16),
        )
        + (out((SHARD, WIDTH), F32),) * 3
        + (out((SHARD, WIDTH), BF16),) * 3,
        in_specs=[HBM_SPEC] * 2 + [VMEM_SPEC] * 5 + [HBM_SPEC] * 6,
        out_specs=[HBM_SPEC] * 2 + [VMEM_SPEC] + [HBM_SPEC] * 6,
        scratch_shapes=[
            pltpu.VMEM((2, PIECES, QUARTER), BF16),
            pltpu.VMEM((1280, WIDTH), BF16),
            pltpu.VMEM((1280, WIDTH), BF16),
            pltpu.VMEM((1280, WIDTH), BF16),
            pltpu.VMEM((HALF, WIDTH), BF16),
            pltpu.VMEM((HALF, WIDTH), BF16),
            pltpu.VMEM((HALF, WIDTH), BF16),
            pltpu.VMEM(hidden, BF16),
            pltpu.VMEM(hidden, BF16),
            pltpu.VMEM(hidden, BF16),
            pltpu.VMEM((PIECES, QUARTER), BF16),
            pltpu.VMEM((PIECES, QUARTER), BF16),
            pltpu.VMEM((EXPERTS, 128), F32),
            pltpu.VMEM((EXPERTS, 128), F32),
            pltpu.VMEM((EXPERTS, 8, 128), F32),
            pltpu.VMEM((2, 256, WIDTH), F32),
            pltpu.VMEM((2, 256, WIDTH), BF16),
            DMA((2,)),
            DMA((3, 2)),
            DMA((5,)),
            DMA((5,)),
            DMA((EXPERTS,)),
            DMA((EXPERTS,)),
            DMA((EXPERTS,)),
            DMA((EXPERTS,)),
            DMA((2,)),
            DMA((2, 2)),
        ],
        compiler_params=pltpu.CompilerParams(
            collective_id=2, has_side_effects=True, vmem_limit_bytes=60 * 1024 * 1024
        ),
        name="experts",
    )(x_slots, o_slots, g_slots, *consts, *own, *other)


def backward_kernel(
    long_len, short_len, tokens, cot, routes, routes_t, gain_a, gain_m, rel_bias_t, router_t, ids_t, wq, wk, wv, wo,
    resid, probs_t, rnorm_t, query, long_kv, short_kv, mixed, norm_l, norm_s, dx_back, dg_back, outs,
    block_out, tokens_grad, grads, small,
    total, branch, d_mixed, normed, flipped, d_query, d_kv, d_long, d_arrived, table_l, table_s, diag_l, diag_s,
    turned, out_arrived, out_sum, out_back,
    t_send, t_recv, kv_send, kv_recv, m_send, m_recv, own_sem,
):
    row = lax.axis_index("row")
    col = lax.axis_index("col")
    mate = 3 - row
    barrier = pltpu.get_barrier_semaphore()
    for step in (1, 2, 3):
        pl.semaphore_signal(barrier, inc=1, device_id=(lax.rem(row + step, 4), col), device_id_type=MESH_ID)

    def greet(step, carry):
        pl.semaphore_signal(barrier, inc=1, device_id=(row, lax.rem(col + step, EXPERTS)), device_id_type=MESH_ID)
        return carry

    lax.fori_loop(1, EXPERTS, greet, 0)
    pl.semaphore_wait(barrier, EXPERTS + 2)

    out_move = pltpu.make_async_remote_copy(
        outs.at[1], out_arrived, t_send, t_recv, device_id=(mate, col), device_id_type=MESH_ID
    )
    out_move.start()

    def message(dest, source):
        return pltpu.make_async_remote_copy(
            out_sum.at[block(dest, FOLDED)],
            out_back.at[block(source, FOLDED)],
            m_send.at[dest],
            m_recv.at[source],
            device_id=(row, dest),
            device_id_type=MESH_ID,
        )

    own_out = pltpu.make_async_copy(out_sum.at[block(col, FOLDED)], out_back.at[block(col, FOLDED)], own_sem)

    hot_rows = [(iota((ROWS, EXPERTS), 1) == routes[:, k : k + 1]).astype(F32) for k in range(2)]
    before = (iota((ROWS, ROWS), 1) < iota((ROWS, ROWS), 0)).astype(BF16)
    earlier = nn(before, (hot_rows[0] + hot_rows[1]).astype(BF16))
    place = [
        routes[:, k : k + 1].astype(F32) * SLOTS + jnp.sum(earlier * hot_rows[k], axis=1, keepdims=True)
        for k in range(2)
    ]

    def gather_back(source):
        total[...] = jnp.zeros_like(total)

        def one(i, carry):
            here = block(i, 512)
            slot_id, quarter = ids_t[0:1, here], ids_t[1:2, here]
            match = (slot_id == place[0]) | (slot_id == place[1])
            values = source[here, :]
            for q in range(4):
                hot = jnp.where(match & (quarter == q), 1.0, 0.0).astype(BF16)
                total[:, q * QUARTER : (q + 1) * QUARTER] += nn(hot, values)
            return carry

        lax.fori_loop(0, PIECES // 512, one, 0)

    gather_back(dx_back)

    hots, both, slots, unused = route_places(routes_t[...])
    probs = probs_t[...]
    picked = [jnp.sum(probs * hot, axis=0, keepdims=True) for hot in hots]
    picked_sum = picked[0] + picked[1]
    gate_slots = jnp.concatenate([dg_back[e, 0:1, :] for e in range(EXPERTS)], axis=0)
    d_gates = [
        jnp.sum(hots[k] * nn(gate_slots, slot_hot(slots[k]), highest), axis=0, keepdims=True) for k in range(2)
    ]
    shared = (d_gates[0] * picked[0] + d_gates[1] * picked[1]) / (picked_sum * picked_sum)
    fraction = jnp.sum(both, axis=1, keepdims=True) / (2 * ROWS)
    d_probs = balance_coef * EXPERTS * fraction
    for k in range(2):
        d_probs = d_probs + (d_gates[k] / picked_sum - shared) * hots[k]
    d_logits = probs * (d_probs - jnp.sum(d_probs * probs, axis=0, keepdims=True))
    d_logits = d_logits + 2.0 * zloss_coef * rnorm_t[...] * probs

    x = resid[...]
    scale = lax.rsqrt(jnp.mean(x * x, axis=1, keepdims=True) + norm_eps)
    router_grad = nn(d_logits, x * scale * gain_m[...], highest)
    small[...] = jnp.zeros_like(small)
    for i in range(8):
        small[i * 32 : (i + 1) * 32, :] = router_grad[:, i * 128 : (i + 1) * 128]
    d_normed = total[...] + nn(d_logits.T, router_t[...], highest)
    gain_grad = jnp.sum(d_normed * (x * scale), axis=0, keepdims=True)
    for i in range(8):
        small[264 + i : 265 + i, :] = gain_grad[:, i * 128 : (i + 1) * 128]
    d_normed = d_normed * gain_m[...]
    shrink = jnp.mean(d_normed * x, axis=1, keepdims=True)
    d_resid = cot[...].astype(F32) + scale * d_normed - x * (scale * scale * scale * shrink)
    tokens_grad[...] = d_resid
    branch[...] = d_resid.astype(BF16)

    def flip(source):
        def one(i, carry):
            flipped[block(i, 128), :] = source[:, block(i, 128)].T
            return carry

        lax.fori_loop(0, 8, one, 0)

    def weight_gradient(which, value_of):
        def one(n, carry):
            out = nn(flipped[...], value_of(n)).astype(BF16)
            first = which * 8192 + n * 2048
            grads[pl.ds(pl.multiple_of(first, 1024), 1024), :] = out[:, 0:128]
            grads[pl.ds(pl.multiple_of(first + 1024, 1024), 1024), :] = out[:, 128:256]
            return carry

        lax.fori_loop(0, 4, one, 0)

    def back_mixed(n, carry):
        rows = block(n, 256)
        d_mixed[:, rows] = nt(branch[...], wo[rows, :]).astype(BF16)
        return carry

    lax.fori_loop(0, 4, back_mixed, 0)

    place_l = iota((1, TABLE), 1)
    place_l = jnp.where(place_l < 512, place_l, place_l - TABLE) - row * LONG
    place_s = iota((1, 256), 1)
    place_s = jnp.where(place_s < 128, place_s, place_s - 256)
    table_l[...] = nn(rel_bias_t[...], bucket_hot(place_l), highest)
    table_s[...] = nn(rel_bias_t[...], bucket_hot(place_s), highest)
    turned[...] = (iota((128, 128), 0) + iota((128, 128), 1) == 127).astype(BF16)
    lane = iota((1, 128), 1)

    def attend_back(first, keys_of, store_kv, table, diag, keep, count, width, norm_in):
        def one_pair(pair, carry):
            lanes = block(pair, 128)
            values = pl.ds(pl.multiple_of(pair * 128 + WIDTH, 128), 128)
            q2 = query[first : first + 128, lanes]
            m2 = d_mixed[first : first + 128, lanes]
            k2, v2 = keys_of(lanes), keys_of(values)
            d_k = jnp.zeros((count, 128), F32)
            d_v = jnp.zeros((count, 128), F32)
            d_q = []
            for side in range(2):
                head = pair * 2 + side
                here = (lane >= 64) if side else (lane < 64)
                q1 = jnp.where(here, q2, jnp.zeros_like(q2))
                m1 = jnp.where(here, m2, jnp.zeros_like(m2))
                norm = jnp.sum(jnp.where(lane == head, norm_in[...], 0.0), axis=1, keepdims=True)
                bias = pltpu.roll(
                    jnp.broadcast_to(table[pl.ds(head, 1), :], (128, width)), 0, 1, stride=1, stride_axis=0
                )[:, :count]
                scores = jnp.where(keep, nt(q1, k2) * 0.125 + bias, masked_score)
                probs = jnp.exp(scores - norm)
                d_probs = nt(m1, v2)
                shift = jnp.sum(probs * d_probs, axis=1, keepdims=True)
                d_scores = (probs * (d_probs - shift)).astype(BF16)
                d_v = d_v + tn(probs.astype(BF16), m1)
                d_k = d_k + tn(d_scores, q1)
                d_q.append(nn(d_scores, k2))
                reverse = nn(turned[...], d_scores)
                reverse = jnp.concatenate([reverse, jnp.zeros((128, width - count), F32)], axis=1)
                reverse = pltpu.roll(reverse, 0, 1, stride=1, stride_axis=0)
                diag[pl.ds(head, 1), :] = jnp.sum(reverse, axis=0, keepdims=True)
            d_query[first : first + 128, lanes] = (jnp.where(lane < 64, d_q[0], d_q[1]) * 0.125).astype(BF16)
            store_kv(lanes, d_k * 0.125)
            store_kv(values, d_v)
            return carry

        lax.fori_loop(0, HEADS // 2, one_pair, 0)

    def store_long(lanes, value):
        d_long[:, :, lanes] = value.astype(BF16).reshape(4, LONG, 128)

    def store_short(lanes, value):
        d_kv[LONG:, lanes] = value.astype(BF16)

    attend_back(
        0,
        lambda lanes: long_kv[:, :, lanes].reshape(512, 128),
        store_long,
        table_l,
        diag_l,
        iota((1, 512), 1) < long_len[0],
        512,
        TABLE,
        norm_l,
    )

    def kv_move(step):
        dest = lax.rem(row + step, 4)
        return pltpu.make_async_remote_copy(
            d_long.at[dest],
            d_arrived.at[step - 1],
            kv_send.at[step - 1],
            kv_recv.at[step - 1],
            device_id=(dest, col),
            device_id_type=MESH_ID,
        )

    for step in (1, 2, 3):
        kv_move(step).start()

    out_move.wait_recv()

    def return_group(i, carry):
        group = lax.rem(lax.div(col, 4) + i, 8)
        rows = block(group, 320)
        out_sum[rows, :] = (outs[0, rows, :].astype(F32) + out_arrived[rows, :].astype(F32)).astype(BF16)
        for j in range(4):
            dest = group * 4 + j

            @pl.when(dest != col)
            def _():
                message(dest, col).start()

            @pl.when(dest == col)
            def _():
                own_out.start()

        return carry

    lax.fori_loop(0, 8, return_group, 0)

    attend_back(
        LONG,
        lambda lanes: short_kv[:, lanes],
        store_short,
        table_s,
        diag_s,
        iota((1, 128), 1) < short_len[0],
        128,
        256,
        norm_s,
    )
    flip(mixed)
    weight_gradient(3, lambda n: branch[:, block(n, 256)])
    back_l = bucket_hot(iota((1, TABLE), 1) - 127 - row * LONG)
    back_s = bucket_hot(iota((1, 256), 1) - 127)
    small[272:288, 0:32] = nt(diag_l[...], back_l, highest) + nt(diag_s[...], back_s, highest)

    def norm_rows(i, carry):
        rows = block(i, 64)
        x = tokens[rows, :].astype(F32)
        scale = lax.rsqrt(jnp.mean(x * x, axis=1, keepdims=True) + norm_eps)
        normed[rows, :] = (x * scale * gain_a[...]).astype(BF16)
        return carry

    lax.fori_loop(0, 4, norm_rows, 0)
    flip(normed)
    weight_gradient(0, lambda n: d_query[:, block(n, 256)])
    for step in (1, 2, 3):
        kv_move(step).wait()

    def add_kv(i, carry):
        lanes = block(i, 256)
        value = d_long[row, :, lanes].astype(F32)
        for step in range(3):
            value = value + d_arrived[step, :, lanes].astype(F32)
        d_kv[0:LONG, lanes] = value.astype(BF16)
        return carry

    lax.fori_loop(0, 8, add_kv, 0)
    weight_gradient(1, lambda n: d_kv[:, block(n, 256)])
    weight_gradient(2, lambda n: d_kv[:, pl.ds(pl.multiple_of(n * 256 + WIDTH, 256), 256)])

    def back_normed(n, carry):
        rows = block(n, 256)
        value = nt(d_query[...], wq[rows, :]) + nt(d_kv[:, 0:WIDTH], wk[rows, :])
        total[:, rows] = value + nt(d_kv[:, WIDTH:], wv[rows, :])
        return carry

    lax.fori_loop(0, 4, back_normed, 0)
    x = tokens[...].astype(F32)
    scale = lax.rsqrt(jnp.mean(x * x, axis=1, keepdims=True) + norm_eps)
    d_normed = total[...]
    gain_grad = jnp.sum(d_normed * (x * scale), axis=0, keepdims=True)
    for i in range(8):
        small[256 + i : 257 + i, :] = gain_grad[:, i * 128 : (i + 1) * 128]
    d_normed = d_normed * gain_a[...]
    shrink = jnp.mean(d_normed * x, axis=1, keepdims=True)
    tokens_grad[...] = tokens_grad[...] + scale * d_normed - x * (scale * scale * scale * shrink)

    def wait_source(step, carry):
        source = lax.rem(col + step, EXPERTS)
        message(col, source).wait_recv()
        message(source, col).wait_send()
        return carry

    lax.fori_loop(1, EXPERTS, wait_source, 0)
    own_out.wait()
    out_move.wait_send()
    total[...] = jnp.zeros_like(total)
    gates = [picked[k] / picked_sum for k in range(2)]
    gates = [jnp.broadcast_to(gate, (128, ROWS)).T[:, 0:1] for gate in gates]

    def combine(i, carry):
        here = block(i, 512)
        slot_id, quarter = ids_t[0:1, here], ids_t[1:2, here]
        weight = jnp.where(slot_id == place[0], gates[0], 0.0) + jnp.where(slot_id == place[1], gates[1], 0.0)
        high = weight.astype(BF16)
        rest = (weight - high.astype(F32)).astype(BF16)
        values = out_back[here, :]
        for q in range(4):
            here_q = quarter == q
            part = nn(jnp.where(here_q, high, jnp.zeros_like(high)), values)
            part = part + nn(jnp.where(here_q, rest, jnp.zeros_like(rest)), values)
            total[:, q * QUARTER : (q + 1) * QUARTER] += part
        return carry

    lax.fori_loop(0, PIECES // 512, combine, 0)
    branch_m = total[...]
    live = live_column(long_len[0], short_len[0], row)
    resid_now = resid[...]
    result = resid_now + branch_m
    block_out[...] = result
    branch_a = resid_now - tokens[...].astype(F32)
    tallies = [
        jnp.sum(live * jnp.sum(field * field, axis=1, keepdims=True), axis=0, keepdims=True)
        for field in (result, branch_a, branch_m)
    ]
    tallies.append(jnp.sum(live, axis=0, keepdims=True))
    packed = jnp.zeros((8, 128), F32)
    for i, tally in enumerate(tallies):
        packed = jnp.where(iota((8, 128), 1) == i, tally, packed)
    small[288:296, :] = packed


def backward(*args):
    def out(shape, dtype):
        return jax.ShapeDtypeStruct(shape, dtype)

    return pl.pallas_call(
        backward_kernel,
        out_shape=(
            out((ROWS, WIDTH), F32),
            out((ROWS, WIDTH), F32),
            out((2 * SUM_ROWS[0], 128), BF16),
            out((2 * SUM_ROWS[1], 128), F32),
        ),
        in_specs=[SMEM_SPEC] * 2 + [VMEM_SPEC] * (len(args) - 2),
        out_specs=[VMEM_SPEC] * 4,
        scratch_shapes=[
            pltpu.VMEM((ROWS, WIDTH), F32),
            pltpu.VMEM((ROWS, WIDTH), BF16),
            pltpu.VMEM((ROWS, WIDTH), BF16),
            pltpu.VMEM((ROWS, WIDTH), BF16),
            pltpu.VMEM((WIDTH, ROWS), BF16),
            pltpu.VMEM((ROWS, WIDTH), BF16),
            pltpu.VMEM((ROWS, 2 * WIDTH), BF16),
            pltpu.VMEM((4, LONG, 2 * WIDTH), BF16),
            pltpu.VMEM((3, LONG, 2 * WIDTH), BF16),
            pltpu.VMEM((HEADS, TABLE), F32),
            pltpu.VMEM((HEADS, 256), F32),
            pltpu.VMEM((HEADS, TABLE), F32),
            pltpu.VMEM((HEADS, 256), F32),
            pltpu.VMEM((128, 128), BF16),
            pltpu.VMEM((PIECES, QUARTER), BF16),
            pltpu.VMEM((PIECES, QUARTER), BF16),
            pltpu.VMEM((PIECES, QUARTER), BF16),
            DMA,
            DMA,
            DMA((3,)),
            DMA((3,)),
            DMA((EXPERTS,)),
            DMA((EXPERTS,)),
            DMA,
        ],
        compiler_params=pltpu.CompilerParams(
            collective_id=3, has_side_effects=True, vmem_limit_bytes=60 * 1024 * 1024
        ),
        name="backward_local",
    )(*args)


SUM_PARTS = (
    (5120, 0, ("x", "y", "z"), 0),
    (5120, 5120, ("y", "z", "x"), 0),
    (6144, 10240, ("z", "x", "y"), 0),
    (512, 0, ("y", "x", "z"), 1),
)
SUM_ROWS = (16384, 512)


def torus_place():
    row = lax.axis_index("row")
    col = lax.axis_index("col")
    core = lax.rem(col, 2)
    x = lax.rem(lax.div(col, 2), 4)
    z = lax.div(col, 8)
    return row, z, x, core


def axis_peer(axis, step):
    row, z, x, core = torus_place()
    if axis == "y":
        row = lax.rem(row + step, 4)
    elif axis == "x":
        x = lax.rem(x + step, 4)
    elif axis == "z":
        z = lax.rem(z + step, 4)
    else:
        core = 1 - core
    return (row, (z * 4 + x) * 2 + core)


def sum_kernel(*refs):
    inputs = refs[0:2]
    results = refs[2:4]
    held = refs[4:6]
    other = refs[6:8]
    slots = refs[8:8 + 3 * len(SUM_PARTS)]
    load_sem, core_send, core_recv, hop_send, hop_recv, gather_send, gather_recv, copy_sem, last_send, last_recv = refs[
        8 + 3 * len(SUM_PARTS):
    ]
    row, z, x, core = torus_place()
    place = {"x": x, "y": row, "z": z}
    barrier = pltpu.get_barrier_semaphore()
    pl.semaphore_signal(barrier, inc=1, device_id=axis_peer("core", 1), device_id_type=MESH_ID)
    for axis in ("x", "y", "z"):
        for step in (1, 2, 3):
            pl.semaphore_signal(barrier, inc=1, device_id=axis_peer(axis, step), device_id_type=MESH_ID)
    loads = []
    for p, (rows, first, order, kind) in enumerate(SUM_PARTS):
        mine = pl.multiple_of(core * SUM_ROWS[kind] + first, 256)
        load = pltpu.make_async_copy(
            inputs[kind].at[pl.ds(mine, rows)], held[kind].at[pl.ds(first, rows)], load_sem.at[p]
        )
        load.start()
        loads.append(load)
    pl.semaphore_wait(barrier, 10)
    swaps = []
    for p, (rows, first, order, kind) in enumerate(SUM_PARTS):
        yours = pl.multiple_of((1 - core) * SUM_ROWS[kind] + first, 256)
        swap = pltpu.make_async_remote_copy(
            inputs[kind].at[pl.ds(yours, rows)],
            other[kind].at[pl.ds(first, rows)],
            core_send.at[p],
            core_recv.at[p],
            device_id=axis_peer("core", 1),
            device_id_type=MESH_ID,
        )
        swap.start()
        swaps.append(swap)

    def add_rows(kind, start, rows, terms):
        if kind == 1:
            tile = min(rows, 128)
        else:
            tile = 80 if rows % 80 == 0 else 96
            tile = tile * 4 if rows % (tile * 4) == 0 else tile

        def body(i, carry):
            offset = pl.multiple_of(i * tile, 8 if kind == 1 else 16)
            here = pl.ds(pl.multiple_of(start + offset, 8 if kind == 1 else 16), tile)
            total = held[kind][here, :].astype(jnp.float32)
            for ref, base in terms:
                total = total + ref[pl.ds(pl.multiple_of(base + offset, 8 if kind == 1 else 16), tile), :].astype(jnp.float32)
            held[kind][here, :] = total.astype(held[kind].dtype)
            return carry

        lax.fori_loop(0, rows // tile, body, 0)

    def start_hop(p, level):
        rows, first, order, kind = SUM_PARTS[p]
        size = rows // 4 ** (level + 1)
        base = first
        for done in range(level):
            base = base + place[order[done]] * (rows // 4 ** (done + 1))
        axis = order[level]
        hops = []
        for step in (1, 2, 3):
            block = lax.rem(place[axis] + step, 4)
            hop = pltpu.make_async_remote_copy(
                held[kind].at[pl.ds(pl.multiple_of(base + block * size, 8 if kind == 1 else 16), size)],
                slots[p * 3 + level].at[pl.ds((step - 1) * size, size)],
                hop_send.at[p, level, step - 1],
                hop_recv.at[p, level, step - 1],
                device_id=axis_peer(axis, step),
                device_id_type=MESH_ID,
            )
            hop.start()
            hops.append(hop)
        return hops

    def end_hop(p, level, hops):
        rows, first, order, kind = SUM_PARTS[p]
        size = rows // 4 ** (level + 1)
        base = first
        for done in range(level + 1):
            base = base + place[order[done]] * (rows // 4 ** (done + 1))
        for hop in hops:
            hop.wait()
        add_rows(kind, base, size, [(slots[p * 3 + level], step * size) for step in range(3)])

    count = len(SUM_PARTS)
    flight = [None] * count
    for p in range(count):
        rows, first, order, kind = SUM_PARTS[p]
        loads[p].wait()
        swaps[p].wait()
        add_rows(kind, first, rows, [(other[kind], first)])
        flight[p] = start_hop(p, 0)
    for level in (1, 2):
        for p in range(count):
            end_hop(p, level - 1, flight[p])
            flight[p] = start_hop(p, level)

    def place_of(p, levels):
        rows, first, order, kind = SUM_PARTS[p]
        base = first
        for done in range(levels):
            base = base + place[order[done]] * (rows // 4 ** (done + 1))
        return base

    def gather(p, level):
        rows, first, order, kind = SUM_PARTS[p]
        size = rows // 4 ** (level + 1)
        align = 8 if kind == 1 else 16
        here = pl.multiple_of(place_of(p, level + 1), align)
        there = pl.multiple_of(place_of(p, level + 1) + core * SUM_ROWS[kind], align)
        source = held[kind].at[pl.ds(here, size)] if level == 2 else results[kind].at[pl.ds(there, size)]
        moves = []
        for step in (1, 2, 3):
            move = pltpu.make_async_remote_copy(
                source,
                results[kind].at[pl.ds(there, size)],
                gather_send.at[p, level, step - 1],
                gather_recv.at[p, level, step - 1],
                device_id=axis_peer(order[level], step),
                device_id_type=MESH_ID,
            )
            move.start()
            moves.append(move)
        if level == 2:
            keep = pltpu.make_async_copy(source, results[kind].at[pl.ds(there, size)], copy_sem.at[p])
            keep.start()
            keep.wait()
        return moves

    for p in range(count):
        end_hop(p, 2, flight[p])
        flight[p] = gather(p, 2)
    for level in (1, 0):
        for p in range(count):
            for move in flight[p]:
                move.wait()
            flight[p] = gather(p, level)
    lasts = []
    for p in range(count):
        rows, first, order, kind = SUM_PARTS[p]
        size = rows // 4
        for index in range(4):
            if index > 0:
                flight[p][index - 1].wait()
            block = lax.rem(place[order[0]] + 4 - index, 4)
            there = pl.ds(pl.multiple_of(first + block * size + core * SUM_ROWS[kind], 8 if kind == 1 else 16), size)
            last = pltpu.make_async_remote_copy(
                results[kind].at[there],
                results[kind].at[there],
                last_send.at[p, index],
                last_recv.at[p, index],
                device_id=axis_peer("core", 1),
                device_id_type=MESH_ID,
            )
            last.start()
            lasts.append(last)
    for last in lasts:
        last.wait()


def sum_over_devices(weights, small):
    scratch = [
        pltpu.VMEM((SUM_ROWS[0], 128), jnp.bfloat16),
        pltpu.VMEM((SUM_ROWS[1], 128), jnp.float32),
        pltpu.VMEM((SUM_ROWS[0], 128), jnp.bfloat16),
        pltpu.VMEM((SUM_ROWS[1], 128), jnp.float32),
    ]
    for rows, first, order, kind in SUM_PARTS:
        for level in range(3):
            scratch.append(
                pltpu.VMEM((3 * rows // 4 ** (level + 1), 128), jnp.float32 if kind == 1 else jnp.bfloat16)
            )
    count = len(SUM_PARTS)
    dma = pltpu.SemaphoreType.DMA
    scratch += [
        dma((count,)),
        dma((count,)),
        dma((count,)),
        dma((count, 3, 3)),
        dma((count, 3, 3)),
        dma((count, 3, 3)),
        dma((count, 3, 3)),
        dma((count,)),
        dma((count, 4)),
        dma((count, 4)),
    ]
    return pl.pallas_call(
        sum_kernel,
        out_shape=(
            jax.ShapeDtypeStruct((2 * SUM_ROWS[0], 128), jnp.bfloat16),
            jax.ShapeDtypeStruct((2 * SUM_ROWS[1], 128), jnp.float32),
        ),
        in_specs=[pl.BlockSpec(memory_space=pl.ANY)] * 2,
        out_specs=[pl.BlockSpec(memory_space=pl.ANY)] * 2,
        scratch_shapes=scratch,
        compiler_params=pltpu.CompilerParams(
            collective_id=4, has_side_effects=True, vmem_limit_bytes=48 * 1024 * 1024
        ),
        name="sum_over_devices",
    )(weights, small)


def per_device(
    tokens_in, out_cot, long_lengths, short_lengths, routes, gain_attn, w_query, w_key, w_value, w_out, rel_bias,
    gain_moe, router, w_gate, w_up, w_down,
):
    pairs = [(0, 1), (1, 0), (2, 3), (3, 2)]
    own = (jnp.swapaxes(w_gate[0], 0, 1), jnp.swapaxes(w_up[0], 0, 1), w_down[0])
    other = tuple(lax.ppermute(weight, "row", pairs) for weight in own)
    routes_t = jnp.swapaxes(routes, 0, 1)
    router_t = jnp.swapaxes(router, 0, 1)
    rel_bias_t = jnp.swapaxes(rel_bias, 0, 1)
    gain_a, gain_m = gain_attn.reshape(1, WIDTH), gain_moe.reshape(1, WIDTH)
    ids = piece_ids()
    x_slots, o_slots, g_slots, query, long_kv, short_kv, mixed, norm_l, norm_s, resid, probs_t, rnorm_t = forward(
        long_lengths, short_lengths, tokens_in, out_cot, routes_t, gain_a, gain_m, rel_bias_t, router_t,
        jnp.asarray(ids.T), w_query, w_key, w_value, w_out,
    )
    unfold = unfold_matrix()
    row_of = np.arange(640) // SLOTS
    consts = (
        jnp.asarray(unfold, BF16),
        jnp.asarray(unfold.T, BF16),
        jnp.asarray((row_of[:, None] == np.arange(EXPERTS)[None, :]).astype(np.float32)),
        jnp.asarray((np.arange(640) % SLOTS).astype(np.int32)[:, None]),
    )
    dx_back, dg_back, outs, wg_grad, wu_grad, wd_grad, wg_send, wu_send, wd_send = experts(
        x_slots, o_slots, g_slots, consts, own, other
    )
    arrived = [lax.ppermute(part, "row", pairs) for part in (wg_send, wu_send, wd_send)]
    block_out, tokens_grad, grads, small = backward(
        long_lengths, short_lengths, tokens_in, out_cot, routes, routes_t, gain_a, gain_m, rel_bias_t, router_t,
        jnp.asarray(ids), w_query, w_key, w_value, w_out, resid, probs_t, rnorm_t, query, long_kv, short_kv, mixed,
        norm_l, norm_s, dx_back, dg_back, outs,
    )
    grads, small = sum_over_devices(grads, small)
    grads = grads.reshape(4, 8, WIDTH, 128).transpose(0, 2, 1, 3).reshape(4, WIDTH, WIDTH).astype(F32)
    expert_grads = [
        mine + part.astype(F32) for mine, part in zip((wg_grad, wu_grad, wd_grad), arrived)
    ]
    totals = small[288]
    statistics = jnp.sqrt(totals[0:3] / (totals[3] * WIDTH))
    router_grad = small[0:256].reshape(8, EXPERTS, 128).transpose(1, 0, 2).reshape(EXPERTS, WIDTH)
    return (
        block_out,
        tokens_grad,
        small[256:264].reshape(WIDTH),
        grads[0],
        grads[1],
        grads[2],
        grads[3],
        jnp.swapaxes(small[272:288, 0:32], 0, 1),
        small[264:272].reshape(WIDTH),
        jnp.swapaxes(router_grad, 0, 1),
        jnp.swapaxes(expert_grads[0], 0, 1)[None],
        jnp.swapaxes(expert_grads[1], 0, 1)[None],
        expert_grads[2][None],
        statistics,
    )


def solution(mesh):
    tokens = P(("row", "col"), None)
    whole = P()
    wide = P("col", None, "row")
    tall = P("col", "row", None)
    return jax.shard_map(
        per_device,
        mesh=mesh,
        in_specs=(tokens, tokens, P("col"), P(("row", "col")), tokens) + (whole,) * 8 + (wide, wide, tall),
        out_specs=(tokens, tokens) + (whole,) * 8 + (wide, wide, tall, whole),
        check_vma=False,
    )
```

```python
import functools

import numpy as np
import jax
import jax.numpy as jnp
from jax import lax
from jax.experimental import pallas as pl
from jax.experimental.pallas import tpu as pltpu
from jax.sharding import PartitionSpec as P

HEADS = 16
HEAD_DIM = 64
WIDTH = 1024
ROWS = 256
LONG = 128
EXPERTS = 32
SLOTS = 20
FOLDED = 80
QUARTER = 256
PIECES = EXPERTS * FOLDED
TABLE = 640
SHARD = 704
PADDED = 768
EARLY_DOWN = 352
GRAD_ROWS = 3 * SHARD
GRAD_EARLY = 528
GRAD_LATE = GRAD_ROWS - 2 * GRAD_EARLY

bucket_edges = (1, 2, 3, 4, 5, 6, 7, 8, 12, 16, 23, 32, 46, 64, 91)
norm_eps = 1e-06
balance_coef = 0.01
zloss_coef = 0.001
masked_score = -1e30
highest = lax.Precision.HIGHEST
MESH_ID = pl.DeviceIdType.MESH
F32 = jnp.float32
BF16 = jnp.bfloat16
VMEM_SPEC = pl.BlockSpec(memory_space=pltpu.VMEM)
HBM_SPEC = pl.BlockSpec(memory_space=pl.ANY)
SMEM_SPEC = pl.BlockSpec(memory_space=pltpu.SMEM)
DMA = pltpu.SemaphoreType.DMA


def piece_ids():
    row = np.arange(PIECES)
    slot = (row // FOLDED) * SLOTS + row % SLOTS
    quarter = (row % FOLDED) // SLOTS
    return np.stack([slot, quarter]).astype(np.float32)


def unfold_matrix():
    out = np.arange(320)
    quarter, message, slot = out // 80, (out % 80) // SLOTS, out % SLOTS
    hot = np.zeros((320, 320), np.float32)
    hot[out, message * FOLDED + quarter * SLOTS + slot] = 1
    return hot


def nt(left, right, precision=None):
    return lax.dot_general(
        left, right, (((1,), (1,)), ((), ())), preferred_element_type=F32, precision=precision
    )


def tn(left, right):
    return lax.dot_general(left, right, (((0,), (0,)), ((), ())), preferred_element_type=F32)


def nn(left, right, precision=None):
    return jnp.dot(left, right, preferred_element_type=F32, precision=precision)


def iota(shape, dim):
    return lax.broadcasted_iota(jnp.int32, shape, dim)


def block(index, size):
    return pl.ds(pl.multiple_of(index * size, size), size)


def bucket_hot(relative):
    magnitude = jnp.abs(relative)
    level = jnp.zeros_like(relative)
    for edge in bucket_edges:
        level = level + (magnitude >= edge).astype(jnp.int32)
    level = level + jnp.where(relative > 0, len(bucket_edges) + 1, 0)
    return (iota((32, relative.shape[1]), 0) == level).astype(F32)


def route_places(routes_t):
    hots = [(iota((EXPERTS, ROWS), 0) == routes_t[k : k + 1, :]).astype(F32) for k in range(2)]
    both = hots[0] + hots[1]
    before = (iota((ROWS, ROWS), 0) < iota((ROWS, ROWS), 1)).astype(BF16)
    earlier = nn(both.astype(BF16), before)
    slots = [jnp.sum(earlier * hot, axis=0, keepdims=True) for hot in hots]
    places = [routes_t[k : k + 1, :].astype(F32) * SLOTS + slots[k] for k in range(2)]
    return hots, both, slots, places


def slot_hot(slots_row):
    return (iota((128, ROWS), 0).astype(F32) == slots_row).astype(F32)


def live_column(long_len, short_len, row):
    position = iota((ROWS, 1), 0)
    is_long = position < LONG
    here = jnp.where(is_long, position + row * LONG, position - LONG)
    limit = jnp.where(is_long, long_len, short_len)
    return (here < limit).astype(F32)


def forward_kernel(
    long_len, short_len, tokens, cot, routes_t, gain_a, gain_m, rel_bias_t, router_t, ids, wq, wk, wv, wo, wg_own, wu_own, wd_own,
    x_slots, o_slots, g_slots, wg_mate, wu_mate, wd_mate, query, long_kv, short_kv, mixed, norm_l, norm_s, resid, probs_t, rnorm_t,
    normed, buffer_o, buffer_x, gate_out, table_l, table_s,
    o_send, o_recv, x_send, x_recv, g_send, g_recv, own_sem, kv_send, kv_recv, t_send, t_recv, w_send, w_recv,
):
    row = lax.axis_index("row")
    col = lax.axis_index("col")
    mate = 3 - row
    barrier = pltpu.get_barrier_semaphore()
    for step in (1, 2, 3):
        pl.semaphore_signal(barrier, inc=1, device_id=(lax.rem(row + step, 4), col), device_id_type=MESH_ID)

    def greet(step, carry):
        pl.semaphore_signal(barrier, inc=1, device_id=(row, lax.rem(col + step, EXPERTS)), device_id_type=MESH_ID)
        return carry

    lax.fori_loop(1, EXPERTS, greet, 0)

    hots, both, slots, places = route_places(routes_t[...])

    def message(buffer, slots_ref, send, recv, dest, source):
        return pltpu.make_async_remote_copy(
            buffer.at[block(dest, FOLDED)],
            slots_ref.at[0, block(source, FOLDED)],
            send.at[dest],
            recv.at[source],
            device_id=(row, dest),
            device_id_type=MESH_ID,
        )

    def dispatch(source, buffer, slots_ref, send, recv, own):
        def one_group(i, carry):
            group = lax.rem(lax.div(col, 4) + i, 8)
            rows = block(group, 320)
            slot_id = ids[rows, 0:1]
            quarter = ids[rows, 1:2]
            match = (slot_id == places[0]) | (slot_id == places[1])
            total = jnp.zeros((320, QUARTER), F32)
            for q in range(4):
                hot = jnp.where(match & (quarter == q), 1.0, 0.0).astype(BF16)
                total = total + nn(hot, source[:, q * QUARTER : (q + 1) * QUARTER])
            buffer[rows, :] = total.astype(BF16)
            for j in range(4):
                dest = group * 4 + j

                @pl.when(dest != col)
                def _():
                    message(buffer, slots_ref, send, recv, dest, col).start()

                @pl.when(dest == col)
                def _():
                    pltpu.make_async_copy(
                        buffer.at[block(dest, FOLDED)], slots_ref.at[0, block(dest, FOLDED)], own
                    ).start()

            return carry

        lax.fori_loop(0, 8, one_group, 0)

    def wait_source(buffer, slots_ref, send, recv, own, source):
        @pl.when(source != col)
        def _():
            message(buffer, slots_ref, send, recv, col, source).wait_recv()

        @pl.when(source == col)
        def _():
            pltpu.make_async_copy(
                buffer.at[block(col, FOLDED)], slots_ref.at[0, block(col, FOLDED)], own
            ).wait()

    def wait_sends(buffer, slots_ref, send, recv):
        def one(step, carry):
            message(buffer, slots_ref, send, recv, lax.rem(col + step, EXPERTS), col).wait_send()
            return carry

        lax.fori_loop(1, EXPERTS, one, 0)

    pl.semaphore_wait(barrier, EXPERTS + 2)

    def norm_rows(i, carry):
        rows = block(i, 64)
        x = tokens[rows, :].astype(F32)
        scale = lax.rsqrt(jnp.mean(x * x, axis=1, keepdims=True) + norm_eps)
        normed[rows, :] = (x * scale * gain_a[...]).astype(BF16)
        return carry

    lax.fori_loop(0, 4, norm_rows, 0)

    def project_kv(i, carry):
        lanes = block(i, 256)
        for offset, weight in ((0, wk), (WIDTH, wv)):
            part = nn(normed[...], weight[:, lanes]).astype(BF16)
            out = pl.ds(pl.multiple_of(i * 256 + offset, 256), 256)
            long_kv[row, :, out] = part[:LONG]
            short_kv[:, out] = part[LONG:]
        return carry

    lax.fori_loop(0, 4, project_kv, 0)

    def kv_move(step):
        return pltpu.make_async_remote_copy(
            long_kv.at[row],
            long_kv.at[row],
            kv_send.at[step - 1],
            kv_recv.at[step - 1],
            device_id=(lax.rem(row + step, 4), col),
            device_id_type=MESH_ID,
        )

    def kv_arrival(step):
        source = lax.rem(row + 4 - step, 4)
        return pltpu.make_async_remote_copy(
            long_kv.at[source],
            long_kv.at[source],
            kv_send.at[step - 1],
            kv_recv.at[step - 1],
            device_id=(source, col),
            device_id_type=MESH_ID,
        )

    for step in (1, 2, 3):
        kv_move(step).start()

    partner = row + 1 - 2 * lax.rem(row, 2)
    weight_moves = [
        pltpu.make_async_remote_copy(
            source, target, w_send.at[i], w_recv.at[i], device_id=(partner, col), device_id_type=MESH_ID
        )
        for i, (source, target) in enumerate(
            ((wg_own, wg_mate), (wu_own, wu_mate), (wd_own.at[pl.ds(0, EARLY_DOWN)], wd_mate))
        )
    ]
    for move in weight_moves:
        move.start()

    dispatch(cot, buffer_o, o_slots, o_send, o_recv, own_sem.at[0])

    def project_q(i, carry):
        lanes = block(i, 256)
        query[:, lanes] = nn(normed[...], wq[:, lanes]).astype(BF16)
        return carry

    lax.fori_loop(0, 4, project_q, 0)

    place_l = iota((1, TABLE), 1)
    place_l = jnp.where(place_l < 512, place_l, place_l - TABLE) - row * LONG
    place_s = iota((1, 256), 1)
    place_s = jnp.where(place_s < 128, place_s, place_s - 256)
    table_l[...] = nn(rel_bias_t[...], bucket_hot(place_l), highest)
    table_s[...] = nn(rel_bias_t[...], bucket_hot(place_s), highest)

    lane = iota((1, 128), 1)

    def attend(q2, k2, v2, table, head, keep, count, width):
        bias = pltpu.roll(
            jnp.broadcast_to(table[pl.ds(head, 1), :], (128, width)), 0, 1, stride=1, stride_axis=0
        )[:, :count]
        scores = jnp.where(keep, nt(q2, k2) * 0.125 + bias, masked_score)
        row_max = jnp.max(scores, axis=1, keepdims=True)
        terms = jnp.exp(scores - row_max)
        total = jnp.sum(terms, axis=1, keepdims=True)
        return nn((terms / total).astype(BF16), v2), row_max + jnp.log(total)

    def attend_pairs(q_first, keys_of, table, keep, count, width, norm_out):
        def one_pair(pair, carry):
            lanes = block(pair, 128)
            values = pl.ds(pl.multiple_of(pair * 128 + WIDTH, 128), 128)
            q2 = query[q_first : q_first + 128, lanes]
            k2, v2 = keys_of(lanes), keys_of(values)
            outs = []
            norms = norm_out[...]
            for side in range(2):
                here = (lane >= 64) if side else (lane < 64)
                out, norm = attend(
                    jnp.where(here, q2, jnp.zeros_like(q2)), k2, v2, table, pair * 2 + side, keep, count, width
                )
                outs.append(out)
                norms = jnp.where(lane == pair * 2 + side, norm, norms)
            norm_out[...] = norms
            mixed[q_first : q_first + 128, lanes] = jnp.where(lane < 64, outs[0], outs[1]).astype(BF16)
            return carry

        lax.fori_loop(0, HEADS // 2, one_pair, 0)

    norm_l[...] = jnp.zeros_like(norm_l)
    norm_s[...] = jnp.zeros_like(norm_s)
    attend_pairs(LONG, lambda lanes: short_kv[:, lanes], table_s, iota((1, 128), 1) < short_len[0], 128, 256, norm_s)

    def wait_o(source, carry):
        wait_source(buffer_o, o_slots, o_send, o_recv, own_sem.at[0], source)
        return carry

    lax.fori_loop(0, EXPERTS, wait_o, 0)

    def to_mate(source, target, index):
        return pltpu.make_async_remote_copy(
            source, target, t_send.at[index], t_recv.at[index], device_id=(mate, col), device_id_type=MESH_ID
        )

    for step in (1, 2, 3):
        kv_arrival(step).wait_recv()
    o_move = to_mate(o_slots.at[0], o_slots.at[1], 8)
    o_move.start()
    attend_pairs(
        0,
        lambda lanes: long_kv[:, :, lanes].reshape(512, 128),
        table_l,
        iota((1, 512), 1) < long_len[0],
        512,
        TABLE,
        norm_l,
    )

    def project_out(i, carry):
        lanes = block(i, 256)
        resid[:, lanes] = tokens[:, lanes].astype(F32) + nn(mixed[...], wo[:, lanes])
        return carry

    lax.fori_loop(0, 4, project_out, 0)

    def norm_again(i, carry):
        rows = block(i, 64)
        x = resid[rows, :]
        scale = lax.rsqrt(jnp.mean(x * x, axis=1, keepdims=True) + norm_eps)
        normed[rows, :] = (x * scale * gain_m[...]).astype(BF16)
        return carry

    lax.fori_loop(0, 4, norm_again, 0)
    dispatch(normed, buffer_x, x_slots, x_send, x_recv, own_sem.at[1])

    x = resid[...]
    scale = lax.rsqrt(jnp.mean(x * x, axis=1, keepdims=True) + norm_eps)
    logits = nt(router_t[...], x * scale * gain_m[...], highest)
    row_max = jnp.max(logits, axis=0, keepdims=True)
    terms = jnp.exp(logits - row_max)
    total = jnp.sum(terms, axis=0, keepdims=True)
    probs = terms / total
    probs_t[...] = probs
    rnorm_t[...] = row_max + jnp.log(total)
    picked = [jnp.sum(probs * hot, axis=0, keepdims=True) for hot in hots]
    picked_sum = picked[0] + picked[1]
    gate_slots = jnp.zeros((EXPERTS, 128), F32)
    for k in range(2):
        gate_slots = gate_slots + nt(hots[k] * (picked[k] / picked_sum), slot_hot(slots[k]), highest)
    for e in range(EXPERTS):
        gate_out[e] = jnp.broadcast_to(gate_slots[e : e + 1, :], (8, 128))

    def gate_message(dest, source):
        return pltpu.make_async_remote_copy(
            gate_out.at[dest],
            g_slots.at[0, source],
            g_send.at[dest],
            g_recv.at[source],
            device_id=(row, dest),
            device_id_type=MESH_ID,
        )

    def send_gates(step, carry):
        gate_message(lax.rem(col + step, EXPERTS), col).start()
        return carry

    lax.fori_loop(1, EXPERTS, send_gates, 0)
    own_gates = pltpu.make_async_copy(gate_out.at[col], g_slots.at[0, col], own_sem.at[2])
    own_gates.start()

    def x_move(group):
        rows = block(group, 320)
        return to_mate(x_slots.at[0, rows], x_slots.at[1, rows], group)

    def forward_x(i, carry):
        group = lax.rem(lax.div(col, 4) + 8 - i, 8)
        for j in range(4):
            wait_source(buffer_x, x_slots, x_send, x_recv, own_sem.at[1], group * 4 + j)
        x_move(group).start()
        return carry

    lax.fori_loop(0, 8, forward_x, 0)

    def wait_gates(step, carry):
        gate_message(col, lax.rem(col + step, EXPERTS)).wait_recv()
        return carry

    lax.fori_loop(1, EXPERTS, wait_gates, 0)
    own_gates.wait()
    g_move = to_mate(g_slots.at[0], g_slots.at[1], 9)
    g_move.start()

    for step in (1, 2, 3):
        kv_move(step).wait_send()
    wait_sends(buffer_o, o_slots, o_send, o_recv)
    wait_sends(buffer_x, x_slots, x_send, x_recv)

    def wait_gate_sends(step, carry):
        gate_message(lax.rem(col + step, EXPERTS), col).wait_send()
        return carry

    lax.fori_loop(1, EXPERTS, wait_gate_sends, 0)
    o_move.wait()

    def wait_x(group, carry):
        x_move(group).wait()
        return carry

    lax.fori_loop(0, 8, wait_x, 0)
    g_move.wait()
    for move in weight_moves:
        move.wait()


def forward(long_lengths, short_lengths, tokens, cot, routes_t, gain_a, gain_m, rel_bias_t, router_t, ids, wq, wk, wv, wo, wg, wu, wd):
    def out(shape, dtype):
        return jax.ShapeDtypeStruct(shape, dtype)

    return pl.pallas_call(
        forward_kernel,
        out_shape=(
            out((2, PIECES, QUARTER), BF16),
            out((2, PIECES, QUARTER), BF16),
            out((2, EXPERTS, 8, 128), F32),
            out((SHARD, WIDTH), BF16),
            out((SHARD, WIDTH), BF16),
            out((EARLY_DOWN, WIDTH), BF16),
            out((ROWS, WIDTH), BF16),
            out((4, LONG, 2 * WIDTH), BF16),
            out((LONG, 2 * WIDTH), BF16),
            out((ROWS, WIDTH), BF16),
            out((128, 128), F32),
            out((128, 128), F32),
            out((ROWS, WIDTH), F32),
            out((EXPERTS, ROWS), F32),
            out((1, ROWS), F32),
        ),
        in_specs=[SMEM_SPEC] * 2 + [VMEM_SPEC] * 12 + [HBM_SPEC] * 3,
        out_specs=[HBM_SPEC] * 6 + [VMEM_SPEC] * 9,
        scratch_shapes=[
            pltpu.VMEM((ROWS, WIDTH), BF16),
            pltpu.VMEM((PIECES, QUARTER), BF16),
            pltpu.VMEM((PIECES, QUARTER), BF16),
            pltpu.VMEM((EXPERTS, 8, 128), F32),
            pltpu.VMEM((HEADS, TABLE), F32),
            pltpu.VMEM((HEADS, 256), F32),
            DMA((EXPERTS,)),
            DMA((EXPERTS,)),
            DMA((EXPERTS,)),
            DMA((EXPERTS,)),
            DMA((EXPERTS,)),
            DMA((EXPERTS,)),
            DMA((3,)),
            DMA((3,)),
            DMA((3,)),
            DMA((10,)),
            DMA((10,)),
            DMA((3,)),
            DMA((3,)),
        ],
        compiler_params=pltpu.CompilerParams(
            collective_id=1, has_side_effects=True, vmem_limit_bytes=56 * 1024 * 1024
        ),
        name="forward_and_dispatch",
    )(
        long_lengths, short_lengths, tokens, cot, routes_t, gain_a, gain_m, rel_bias_t, router_t, ids, wq, wk, wv, wo,
        wg, wu, wd,
    )


def expert_kernel(
    x_slots, o_slots, g_slots, unfold, fold, row_hot, slot_of, wg_own, wu_own, wd_own, wg_mate, wu_mate, wd_mate,
    dx_back, dg_back, outs, grad_own, grad_send,
    stage, xs, os, dys, wg, wu, wd, act, dg, du, part, arrived, dxs, gate_part, gate_arrived, gate_out, grad_stage,
    grad_half, stage_sem, weight_sem, late_send, late_recv, t_send, t_recv, m_send, m_recv, r_send, r_recv, own_sem,
    out_sem,
):
    row = lax.axis_index("row")
    col = lax.axis_index("col")
    mate = 3 - row
    partner = row + 1 - 2 * lax.rem(row, 2)
    barrier = pltpu.get_barrier_semaphore()
    pl.semaphore_signal(barrier, inc=1, device_id=(mate, col), device_id_type=MESH_ID)
    pl.semaphore_signal(barrier, inc=1, device_id=(partner, col), device_id_type=MESH_ID)

    def greet(step, carry):
        pl.semaphore_signal(barrier, inc=1, device_id=(row, lax.rem(col + step, EXPERTS)), device_id_type=MESH_ID)
        return carry

    lax.fori_loop(1, EXPERTS, greet, 0)

    def load(source, which, index):
        return pltpu.make_async_copy(source.at[which], stage.at[index], stage_sem.at[index])

    load(x_slots, 1, 0).start()
    load(o_slots, 1, 1).start()
    weights = [[], []]
    for j, sources in enumerate(((wg_own, wu_own, wd_own), (wg_mate, wu_mate, wd_mate))):
        for i, (source, held) in enumerate(zip(sources, (wg, wu, wd))):
            copy = pltpu.make_async_copy(
                source, held.at[pl.ds(j * PADDED, source.shape[0])], weight_sem.at[i, j]
            )
            copy.start()
            weights[j].append(copy)
    for held in (wg, wu, wd):
        for j in range(2):
            held[j * PADDED + SHARD : (j + 1) * PADDED, :] = jnp.zeros((PADDED - SHARD, WIDTH), BF16)
    pl.semaphore_wait(barrier, EXPERTS + 1)
    late = pltpu.make_async_remote_copy(
        wd_own.at[pl.ds(EARLY_DOWN, SHARD - EARLY_DOWN)],
        wd.at[pl.ds(PADDED + EARLY_DOWN, SHARD - EARLY_DOWN)],
        late_send,
        late_recv,
        device_id=(partner, col),
        device_id_type=MESH_ID,
    )
    late.start()

    def spread(index, target, first):
        def one(group, carry):
            wide = nn(unfold[...], stage[index, block(group, 320), :]).astype(BF16)
            rows = pl.ds(pl.multiple_of(first + group * 80, 16), 80)
            for q in range(4):
                target[rows, q * QUARTER : (q + 1) * QUARTER] = wide[q * 80 : (q + 1) * 80]
            return carry

        lax.fori_loop(0, 8, one, 0)

    def gate_column(which):
        gates = jnp.concatenate([g_slots[which, e, 0:1, :] for e in range(EXPERTS)], axis=0)
        wide = nn(row_hot[...], gates, highest)
        lanes = iota((640, 128), 1)
        return jnp.sum(jnp.where(lanes == slot_of[...], wide, 0.0), axis=1, keepdims=True)

    def take_tokens(which, first):
        load(x_slots, which, 0).wait()
        spread(0, xs, first)
        load(o_slots, which, 1).wait()
        spread(1, os, first)
        rows = pl.ds(first, 640)
        dys[rows, :] = (os[rows, :].astype(F32) * gate_column(which)).astype(BF16)

    def hidden_half(first, half):
        lanes = slice(half * PADDED, (half + 1) * PADDED)
        rows = slice(first, first + 640)
        gate_pre = nt(xs[rows, :], wg[lanes, :])
        up_pre = nt(xs[rows, :], wu[lanes, :])
        d_act = nt(dys[rows, :], wd[lanes, :])
        square = gate_pre * gate_pre
        bend = jnp.tanh(0.7978845608028654 * gate_pre * (1.0 + 0.044715 * square))
        level = 0.5 * (1.0 + bend)
        gelu = gate_pre * level
        slope = level + 0.5 * gate_pre * (1.0 - bend * bend) * (
            0.7978845608028654 * (1.0 + 3.0 * 0.044715 * square)
        )
        act[rows, lanes] = (gelu * up_pre).astype(BF16)
        du[rows, lanes] = (d_act * gelu).astype(BF16)
        dg[rows, lanes] = (d_act * up_pre * slope).astype(BF16)

    def input_gradient(first):
        rows = pl.ds(first, 320)
        return nn(dg[rows, :], wg[...]) + nn(du[rows, :], wu[...])

    def to_mate(source, target, index):
        return pltpu.make_async_remote_copy(
            source, target, t_send.at[index], t_recv.at[index], device_id=(mate, col), device_id_type=MESH_ID
        )

    def fold_group(source, group):
        rows = pl.ds(pl.multiple_of(group * 80, 16), 80)
        tall = jnp.concatenate([source[rows, q * QUARTER : (q + 1) * QUARTER] for q in range(4)], axis=0)
        return nn(fold[...], tall).astype(BF16)

    def output_part(first, which):
        totals = []
        for i in range(2):
            rows = slice(first + i * 320, first + (i + 1) * 320)
            value = nn(act[rows, :], wd[...])
            dxs[i * 320 : (i + 1) * 320, :] = value.astype(BF16)
            totals.append(jnp.sum(value * os[rows, :].astype(F32), axis=1, keepdims=True))
        total = jnp.concatenate(totals, axis=0)

        def fold_one(group, carry):
            outs[which, block(group, 320), :] = fold_group(dxs, group)
            return carry

        lax.fori_loop(0, 8, fold_one, 0)
        wide = jnp.where(iota((640, 128), 1) == slot_of[...], total, 0.0)
        return lax.dot_general(
            row_hot[...], wide, (((0,), (0,)), ((), ())), preferred_element_type=F32, precision=highest
        )

    def part_move(i):
        rows = pl.ds(i * 320, 320)
        return to_mate(part.at[rows], arrived.at[rows], i)

    take_tokens(1, 640)
    load(x_slots, 0, 0).start()
    load(o_slots, 0, 1).start()
    for copy in weights[0]:
        copy.wait()
    hidden_half(640, 0)
    take_tokens(0, 0)
    for copy in weights[1]:
        copy.wait()
    late.wait_recv()
    hidden_half(640, 1)
    for i in range(2):
        part[i * 320 : (i + 1) * 320, :] = input_gradient(640 + i * 320).astype(BF16)
        part_move(i).start()
    hidden_half(0, 0)
    hidden_half(0, 1)
    gate_part[...] = output_part(640, 1)
    gate_move = to_mate(gate_part, gate_arrived, 2)
    gate_move.start()
    gates = output_part(0, 0)

    def message(dest, source):
        return pltpu.make_async_remote_copy(
            stage.at[0, block(dest, FOLDED)],
            dx_back.at[block(source, FOLDED)],
            m_send.at[dest],
            m_recv.at[source],
            device_id=(row, dest),
            device_id_type=MESH_ID,
        )

    def gate_message(dest, source):
        return pltpu.make_async_remote_copy(
            gate_out.at[dest],
            dg_back.at[source],
            r_send.at[dest],
            r_recv.at[source],
            device_id=(row, dest),
            device_id_type=MESH_ID,
        )

    own_dx = pltpu.make_async_copy(stage.at[0, block(col, FOLDED)], dx_back.at[block(col, FOLDED)], own_sem.at[0])
    own_dg = pltpu.make_async_copy(gate_out.at[col], dg_back.at[col], own_sem.at[1])
    for i in range(2):
        rows = slice(i * 320, (i + 1) * 320)
        value = input_gradient(i * 320)
        part_move(i).wait_recv()
        dxs[rows, :] = (value + arrived[rows, :].astype(F32)).astype(BF16)

        def return_group(k, carry, i=i):
            group = i * 4 + lax.rem(lax.div(col, 4) + k, 4)
            stage[0, block(group, 320), :] = fold_group(dxs, group)
            for j in range(4):
                dest = group * 4 + j

                @pl.when(dest != col)
                def _():
                    message(dest, col).start()

                @pl.when(dest == col)
                def _():
                    own_dx.start()

            return carry

        lax.fori_loop(0, 4, return_group, 0)
    gate_move.wait_recv()
    gates = gates + gate_arrived[...]
    for e in range(EXPERTS):
        gate_out[e] = jnp.broadcast_to(gates[e : e + 1, :], (8, 128))

    def send_gates(step, carry):
        gate_message(lax.rem(col + step, EXPERTS), col).start()
        return carry

    lax.fori_loop(1, EXPERTS, send_gates, 0)
    own_dg.start()

    pending = [None, None]
    turn = 0
    for which, (left, right) in enumerate(((dg, xs), (du, xs), (act, dys))):
        for half in (1, 0):
            for n in range(2):
                lanes = slice(n * 512, (n + 1) * 512)
                value = tn(left[:, half * PADDED : (half + 1) * PADDED], right[:, lanes])[0:SHARD]
                slot = turn % 2
                turn += 1
                if pending[slot] is not None:
                    pending[slot].wait()
                if half == 0:
                    grad_stage[slot] = value
                    source, target = grad_stage.at[slot], grad_own
                else:
                    grad_half[slot] = value.astype(BF16)
                    source, target = grad_half.at[slot], grad_send
                pending[slot] = pltpu.make_async_copy(
                    source, target.at[pl.ds(which * SHARD, SHARD), pl.ds(n * 512, 512)], out_sem.at[slot]
                )
                pending[slot].start()
    for copy in pending:
        copy.wait()

    def wait_source(step, carry):
        source = lax.rem(col + step, EXPERTS)
        message(col, source).wait_recv()
        gate_message(col, source).wait_recv()
        message(source, col).wait_send()
        gate_message(source, col).wait_send()
        return carry

    lax.fori_loop(1, EXPERTS, wait_source, 0)
    own_dx.wait()
    own_dg.wait()
    for i in range(2):
        part_move(i).wait_send()
    gate_move.wait_send()
    late.wait_send()


def experts(x_slots, o_slots, g_slots, consts, own, other):
    def out(shape, dtype):
        return jax.ShapeDtypeStruct(shape, dtype)

    hidden = (2 * 640, 2 * PADDED)
    return pl.pallas_call(
        expert_kernel,
        out_shape=(
            out((PIECES, QUARTER), BF16),
            out((EXPERTS, 8, 128), F32),
            out((2, PIECES, QUARTER), BF16),
            out((GRAD_ROWS, WIDTH), F32),
            out((GRAD_ROWS, WIDTH), BF16),
        ),
        in_specs=[HBM_SPEC] * 2 + [VMEM_SPEC] * 5 + [HBM_SPEC] * 6,
        out_specs=[HBM_SPEC] * 2 + [VMEM_SPEC] + [HBM_SPEC] * 2,
        scratch_shapes=[
            pltpu.VMEM((2, PIECES, QUARTER), BF16),
            pltpu.VMEM((1280, WIDTH), BF16),
            pltpu.VMEM((1280, WIDTH), BF16),
            pltpu.VMEM((1280, WIDTH), BF16),
            pltpu.VMEM((2 * PADDED, WIDTH), BF16),
            pltpu.VMEM((2 * PADDED, WIDTH), BF16),
            pltpu.VMEM((2 * PADDED, WIDTH), BF16),
            pltpu.VMEM(hidden, BF16),
            pltpu.VMEM(hidden, BF16),
            pltpu.VMEM(hidden, BF16),
            pltpu.VMEM((640, WIDTH), BF16),
            pltpu.VMEM((640, WIDTH), BF16),
            pltpu.VMEM((640, WIDTH), BF16),
            pltpu.VMEM((EXPERTS, 128), F32),
            pltpu.VMEM((EXPERTS, 128), F32),
            pltpu.VMEM((EXPERTS, 8, 128), F32),
            pltpu.VMEM((2, SHARD, 512), F32),
            pltpu.VMEM((2, SHARD, 512), BF16),
            DMA((2,)),
            DMA((3, 2)),
            DMA,
            DMA,
            DMA((3,)),
            DMA((3,)),
            DMA((EXPERTS,)),
            DMA((EXPERTS,)),
            DMA((EXPERTS,)),
            DMA((EXPERTS,)),
            DMA((2,)),
            DMA((2,)),
        ],
        compiler_params=pltpu.CompilerParams(
            collective_id=2, has_side_effects=True, vmem_limit_bytes=62 * 1024 * 1024
        ),
        name="experts",
    )(x_slots, o_slots, g_slots, *consts, *own, *other)


def backward_kernel(
    long_len, short_len, tokens, cot, routes, routes_t, gain_a, gain_m, rel_bias_t, router_t, ids_t, wq, wk, wv, wo,
    resid, probs_t, rnorm_t, query, long_kv, short_kv, mixed, norm_l, norm_s, dx_back, dg_back, outs, grad_send,
    block_out, tokens_grad, grads, small, grad_mate,
    total, branch, d_mixed, normed, flipped, d_query, d_kv, d_long, d_arrived, table_l, table_s, diag_l, diag_s,
    turned, out_arrived, out_sum, out_back,
    t_send, t_recv, kv_send, kv_recv, m_send, m_recv, own_sem, w_send, w_recv,
):
    row = lax.axis_index("row")
    col = lax.axis_index("col")
    mate = 3 - row
    barrier = pltpu.get_barrier_semaphore()
    for step in (1, 2, 3):
        pl.semaphore_signal(barrier, inc=1, device_id=(lax.rem(row + step, 4), col), device_id_type=MESH_ID)

    def greet(step, carry):
        pl.semaphore_signal(barrier, inc=1, device_id=(row, lax.rem(col + step, EXPERTS)), device_id_type=MESH_ID)
        return carry

    lax.fori_loop(1, EXPERTS, greet, 0)
    pl.semaphore_wait(barrier, EXPERTS + 2)

    out_move = pltpu.make_async_remote_copy(
        outs.at[1], out_arrived, t_send, t_recv, device_id=(mate, col), device_id_type=MESH_ID
    )
    out_move.start()

    partner = row + 1 - 2 * lax.rem(row, 2)

    def weight_move(index):
        rows = pl.ds(index * GRAD_EARLY, GRAD_EARLY)
        return pltpu.make_async_remote_copy(
            grad_send.at[rows],
            grad_mate.at[rows],
            w_send.at[index],
            w_recv.at[index],
            device_id=(partner, col),
            device_id_type=MESH_ID,
        )

    weight_move(0).start()

    def message(dest, source):
        return pltpu.make_async_remote_copy(
            out_sum.at[block(dest, FOLDED)],
            out_back.at[block(source, FOLDED)],
            m_send.at[dest],
            m_recv.at[source],
            device_id=(row, dest),
            device_id_type=MESH_ID,
        )

    own_out = pltpu.make_async_copy(out_sum.at[block(col, FOLDED)], out_back.at[block(col, FOLDED)], own_sem)

    hot_rows = [(iota((ROWS, EXPERTS), 1) == routes[:, k : k + 1]).astype(F32) for k in range(2)]
    before = (iota((ROWS, ROWS), 1) < iota((ROWS, ROWS), 0)).astype(BF16)
    earlier = nn(before, (hot_rows[0] + hot_rows[1]).astype(BF16))
    place = [
        routes[:, k : k + 1].astype(F32) * SLOTS + jnp.sum(earlier * hot_rows[k], axis=1, keepdims=True)
        for k in range(2)
    ]

    def gather_back(source):
        total[...] = jnp.zeros_like(total)

        def one(i, carry):
            here = block(i, 512)
            slot_id, quarter = ids_t[0:1, here], ids_t[1:2, here]
            match = (slot_id == place[0]) | (slot_id == place[1])
            values = source[here, :]
            for q in range(4):
                hot = jnp.where(match & (quarter == q), 1.0, 0.0).astype(BF16)
                total[:, q * QUARTER : (q + 1) * QUARTER] += nn(hot, values)
            return carry

        lax.fori_loop(0, PIECES // 512, one, 0)

    gather_back(dx_back)

    hots, both, slots, unused = route_places(routes_t[...])
    probs = probs_t[...]
    picked = [jnp.sum(probs * hot, axis=0, keepdims=True) for hot in hots]
    picked_sum = picked[0] + picked[1]
    gate_slots = jnp.concatenate([dg_back[e, 0:1, :] for e in range(EXPERTS)], axis=0)
    d_gates = [
        jnp.sum(hots[k] * nn(gate_slots, slot_hot(slots[k]), highest), axis=0, keepdims=True) for k in range(2)
    ]
    shared = (d_gates[0] * picked[0] + d_gates[1] * picked[1]) / (picked_sum * picked_sum)
    fraction = jnp.sum(both, axis=1, keepdims=True) / (2 * ROWS)
    d_probs = balance_coef * EXPERTS * fraction
    for k in range(2):
        d_probs = d_probs + (d_gates[k] / picked_sum - shared) * hots[k]
    d_logits = probs * (d_probs - jnp.sum(d_probs * probs, axis=0, keepdims=True))
    d_logits = d_logits + 2.0 * zloss_coef * rnorm_t[...] * probs

    x = resid[...]
    scale = lax.rsqrt(jnp.mean(x * x, axis=1, keepdims=True) + norm_eps)
    router_grad = nn(d_logits, x * scale * gain_m[...], highest)
    small[...] = jnp.zeros_like(small)
    for i in range(8):
        small[i * 32 : (i + 1) * 32, :] = router_grad[:, i * 128 : (i + 1) * 128]
    d_normed = total[...] + nn(d_logits.T, router_t[...], highest)
    gain_grad = jnp.sum(d_normed * (x * scale), axis=0, keepdims=True)
    for i in range(8):
        small[264 + i : 265 + i, :] = gain_grad[:, i * 128 : (i + 1) * 128]
    d_normed = d_normed * gain_m[...]
    shrink = jnp.mean(d_normed * x, axis=1, keepdims=True)
    d_resid = cot[...].astype(F32) + scale * d_normed - x * (scale * scale * scale * shrink)
    tokens_grad[...] = d_resid
    branch[...] = d_resid.astype(BF16)

    def flip(source):
        def one(i, carry):
            flipped[block(i, 128), :] = source[:, block(i, 128)].T
            return carry

        lax.fori_loop(0, 8, one, 0)

    def weight_gradient(which, value_of):
        def one(n, carry):
            out = nn(flipped[...], value_of(n)).astype(BF16)
            first = which * 8192 + n * 2048
            grads[pl.ds(pl.multiple_of(first, 1024), 1024), :] = out[:, 0:128]
            grads[pl.ds(pl.multiple_of(first + 1024, 1024), 1024), :] = out[:, 128:256]
            return carry

        lax.fori_loop(0, 4, one, 0)

    def back_mixed(n, carry):
        rows = block(n, 256)
        d_mixed[:, rows] = nt(branch[...], wo[rows, :]).astype(BF16)
        return carry

    lax.fori_loop(0, 4, back_mixed, 0)

    place_l = iota((1, TABLE), 1)
    place_l = jnp.where(place_l < 512, place_l, place_l - TABLE) - row * LONG
    place_s = iota((1, 256), 1)
    place_s = jnp.where(place_s < 128, place_s, place_s - 256)
    table_l[...] = nn(rel_bias_t[...], bucket_hot(place_l), highest)
    table_s[...] = nn(rel_bias_t[...], bucket_hot(place_s), highest)
    turned[...] = (iota((128, 128), 0) + iota((128, 128), 1) == 127).astype(BF16)
    lane = iota((1, 128), 1)

    def attend_back(first, keys_of, store_kv, table, diag, keep, count, width, norm_in):
        def one_pair(pair, carry):
            lanes = block(pair, 128)
            values = pl.ds(pl.multiple_of(pair * 128 + WIDTH, 128), 128)
            q2 = query[first : first + 128, lanes]
            m2 = d_mixed[first : first + 128, lanes]
            k2, v2 = keys_of(lanes), keys_of(values)
            d_k = jnp.zeros((count, 128), F32)
            d_v = jnp.zeros((count, 128), F32)
            d_q = []
            for side in range(2):
                head = pair * 2 + side
                here = (lane >= 64) if side else (lane < 64)
                q1 = jnp.where(here, q2, jnp.zeros_like(q2))
                m1 = jnp.where(here, m2, jnp.zeros_like(m2))
                norm = jnp.sum(jnp.where(lane == head, norm_in[...], 0.0), axis=1, keepdims=True)
                bias = pltpu.roll(
                    jnp.broadcast_to(table[pl.ds(head, 1), :], (128, width)), 0, 1, stride=1, stride_axis=0
                )[:, :count]
                scores = jnp.where(keep, nt(q1, k2) * 0.125 + bias, masked_score)
                probs = jnp.exp(scores - norm)
                d_probs = nt(m1, v2)
                shift = jnp.sum(probs * d_probs, axis=1, keepdims=True)
                d_scores = (probs * (d_probs - shift)).astype(BF16)
                d_v = d_v + tn(probs.astype(BF16), m1)
                d_k = d_k + tn(d_scores, q1)
                d_q.append(nn(d_scores, k2))
                reverse = nn(turned[...], d_scores)
                reverse = jnp.concatenate([reverse, jnp.zeros((128, width - count), F32)], axis=1)
                reverse = pltpu.roll(reverse, 0, 1, stride=1, stride_axis=0)
                diag[pl.ds(head, 1), :] = jnp.sum(reverse, axis=0, keepdims=True)
            d_query[first : first + 128, lanes] = (jnp.where(lane < 64, d_q[0], d_q[1]) * 0.125).astype(BF16)
            store_kv(lanes, d_k * 0.125)
            store_kv(values, d_v)
            return carry

        lax.fori_loop(0, HEADS // 2, one_pair, 0)

    def store_long(lanes, value):
        d_long[:, :, lanes] = value.astype(BF16).reshape(4, LONG, 128)

    def store_short(lanes, value):
        d_kv[LONG:, lanes] = value.astype(BF16)

    attend_back(
        0,
        lambda lanes: long_kv[:, :, lanes].reshape(512, 128),
        store_long,
        table_l,
        diag_l,
        iota((1, 512), 1) < long_len[0],
        512,
        TABLE,
        norm_l,
    )

    def kv_move(step):
        dest = lax.rem(row + step, 4)
        return pltpu.make_async_remote_copy(
            d_long.at[dest],
            d_arrived.at[step - 1],
            kv_send.at[step - 1],
            kv_recv.at[step - 1],
            device_id=(dest, col),
            device_id_type=MESH_ID,
        )

    for step in (1, 2, 3):
        kv_move(step).start()
    weight_move(1).start()

    out_move.wait_recv()

    def return_group(i, carry):
        group = lax.rem(lax.div(col, 4) + i, 8)
        rows = block(group, 320)
        out_sum[rows, :] = (outs[0, rows, :].astype(F32) + out_arrived[rows, :].astype(F32)).astype(BF16)
        for j in range(4):
            dest = group * 4 + j

            @pl.when(dest != col)
            def _():
                message(dest, col).start()

            @pl.when(dest == col)
            def _():
                own_out.start()

        return carry

    lax.fori_loop(0, 8, return_group, 0)

    attend_back(
        LONG,
        lambda lanes: short_kv[:, lanes],
        store_short,
        table_s,
        diag_s,
        iota((1, 128), 1) < short_len[0],
        128,
        256,
        norm_s,
    )
    flip(mixed)
    weight_gradient(3, lambda n: branch[:, block(n, 256)])
    back_l = bucket_hot(iota((1, TABLE), 1) - 127 - row * LONG)
    back_s = bucket_hot(iota((1, 256), 1) - 127)
    small[272:288, 0:32] = nt(diag_l[...], back_l, highest) + nt(diag_s[...], back_s, highest)

    def norm_rows(i, carry):
        rows = block(i, 64)
        x = tokens[rows, :].astype(F32)
        scale = lax.rsqrt(jnp.mean(x * x, axis=1, keepdims=True) + norm_eps)
        normed[rows, :] = (x * scale * gain_a[...]).astype(BF16)
        return carry

    lax.fori_loop(0, 4, norm_rows, 0)
    flip(normed)
    weight_gradient(0, lambda n: d_query[:, block(n, 256)])
    for step in (1, 2, 3):
        kv_move(step).wait()

    def add_kv(i, carry):
        lanes = block(i, 256)
        value = d_long[row, :, lanes].astype(F32)
        for step in range(3):
            value = value + d_arrived[step, :, lanes].astype(F32)
        d_kv[0:LONG, lanes] = value.astype(BF16)
        return carry

    lax.fori_loop(0, 8, add_kv, 0)
    weight_gradient(1, lambda n: d_kv[:, block(n, 256)])
    weight_gradient(2, lambda n: d_kv[:, pl.ds(pl.multiple_of(n * 256 + WIDTH, 256), 256)])

    def back_normed(n, carry):
        rows = block(n, 256)
        value = nt(d_query[...], wq[rows, :]) + nt(d_kv[:, 0:WIDTH], wk[rows, :])
        total[:, rows] = value + nt(d_kv[:, WIDTH:], wv[rows, :])
        return carry

    lax.fori_loop(0, 4, back_normed, 0)
    x = tokens[...].astype(F32)
    scale = lax.rsqrt(jnp.mean(x * x, axis=1, keepdims=True) + norm_eps)
    d_normed = total[...]
    gain_grad = jnp.sum(d_normed * (x * scale), axis=0, keepdims=True)
    for i in range(8):
        small[256 + i : 257 + i, :] = gain_grad[:, i * 128 : (i + 1) * 128]
    d_normed = d_normed * gain_a[...]
    shrink = jnp.mean(d_normed * x, axis=1, keepdims=True)
    tokens_grad[...] = tokens_grad[...] + scale * d_normed - x * (scale * scale * scale * shrink)

    def wait_source(step, carry):
        source = lax.rem(col + step, EXPERTS)
        message(col, source).wait_recv()
        message(source, col).wait_send()
        return carry

    lax.fori_loop(1, EXPERTS, wait_source, 0)
    own_out.wait()
    out_move.wait_send()
    total[...] = jnp.zeros_like(total)
    gates = [picked[k] / picked_sum for k in range(2)]
    gates = [jnp.broadcast_to(gate, (128, ROWS)).T[:, 0:1] for gate in gates]

    def combine(i, carry):
        here = block(i, 512)
        slot_id, quarter = ids_t[0:1, here], ids_t[1:2, here]
        weight = jnp.where(slot_id == place[0], gates[0], 0.0) + jnp.where(slot_id == place[1], gates[1], 0.0)
        high = weight.astype(BF16)
        rest = (weight - high.astype(F32)).astype(BF16)
        values = out_back[here, :]
        for q in range(4):
            here_q = quarter == q
            part = nn(jnp.where(here_q, high, jnp.zeros_like(high)), values)
            part = part + nn(jnp.where(here_q, rest, jnp.zeros_like(rest)), values)
            total[:, q * QUARTER : (q + 1) * QUARTER] += part
        return carry

    lax.fori_loop(0, PIECES // 512, combine, 0)
    branch_m = total[...]
    live = live_column(long_len[0], short_len[0], row)
    resid_now = resid[...]
    result = resid_now + branch_m
    block_out[...] = result
    branch_a = resid_now - tokens[...].astype(F32)
    tallies = [
        jnp.sum(live * jnp.sum(field * field, axis=1, keepdims=True), axis=0, keepdims=True)
        for field in (result, branch_a, branch_m)
    ]
    tallies.append(jnp.sum(live, axis=0, keepdims=True))
    packed = jnp.zeros((8, 128), F32)
    for i, tally in enumerate(tallies):
        packed = jnp.where(iota((8, 128), 1) == i, tally, packed)
    small[288:296, :] = packed
    weight_move(0).wait()
    weight_move(1).wait()


def backward(*args):
    def out(shape, dtype):
        return jax.ShapeDtypeStruct(shape, dtype)

    return pl.pallas_call(
        backward_kernel,
        out_shape=(
            out((ROWS, WIDTH), F32),
            out((ROWS, WIDTH), F32),
            out((2 * SUM_ROWS[0], 128), BF16),
            out((2 * SUM_ROWS[1], 128), F32),
            out((2 * GRAD_EARLY, WIDTH), BF16),
        ),
        in_specs=[SMEM_SPEC] * 2 + [VMEM_SPEC] * (len(args) - 3) + [HBM_SPEC],
        out_specs=[VMEM_SPEC] * 4 + [HBM_SPEC],
        scratch_shapes=[
            pltpu.VMEM((ROWS, WIDTH), F32),
            pltpu.VMEM((ROWS, WIDTH), BF16),
            pltpu.VMEM((ROWS, WIDTH), BF16),
            pltpu.VMEM((ROWS, WIDTH), BF16),
            pltpu.VMEM((WIDTH, ROWS), BF16),
            pltpu.VMEM((ROWS, WIDTH), BF16),
            pltpu.VMEM((ROWS, 2 * WIDTH), BF16),
            pltpu.VMEM((4, LONG, 2 * WIDTH), BF16),
            pltpu.VMEM((3, LONG, 2 * WIDTH), BF16),
            pltpu.VMEM((HEADS, TABLE), F32),
            pltpu.VMEM((HEADS, 256), F32),
            pltpu.VMEM((HEADS, TABLE), F32),
            pltpu.VMEM((HEADS, 256), F32),
            pltpu.VMEM((128, 128), BF16),
            pltpu.VMEM((PIECES, QUARTER), BF16),
            pltpu.VMEM((PIECES, QUARTER), BF16),
            pltpu.VMEM((PIECES, QUARTER), BF16),
            DMA,
            DMA,
            DMA((3,)),
            DMA((3,)),
            DMA((EXPERTS,)),
            DMA((EXPERTS,)),
            DMA,
            DMA((2,)),
            DMA((2,)),
        ],
        compiler_params=pltpu.CompilerParams(
            collective_id=3, has_side_effects=True, vmem_limit_bytes=60 * 1024 * 1024
        ),
        name="backward_local",
    )(*args)


SUM_PARTS = (
    (5120, 0, ("x", "y", "z"), 0),
    (5120, 5120, ("y", "z", "x"), 0),
    (6144, 10240, ("z", "x", "y"), 0),
    (512, 0, ("y", "x", "z"), 1),
)
SUM_ROWS = (16384, 512)


def torus_place():
    row = lax.axis_index("row")
    col = lax.axis_index("col")
    core = lax.rem(col, 2)
    x = lax.rem(lax.div(col, 2), 4)
    z = lax.div(col, 8)
    return row, z, x, core


def axis_peer(axis, step):
    row, z, x, core = torus_place()
    if axis == "y":
        row = lax.rem(row + step, 4)
    elif axis == "x":
        x = lax.rem(x + step, 4)
    elif axis == "z":
        z = lax.rem(z + step, 4)
    else:
        core = 1 - core
    return (row, (z * 4 + x) * 2 + core)


def sum_kernel(*refs):
    inputs = refs[0:2]
    grad_send = refs[2]
    results = refs[3:5]
    grad_mate = refs[5]
    refs = refs[6:]
    held = refs[0:2]
    other = refs[2:4]
    slots = refs[4 : 4 + 3 * len(SUM_PARTS)]
    load_sem, core_send, core_recv, hop_send, hop_recv, gather_send, gather_recv, copy_sem, last_send, last_recv, w_send, w_recv = refs[
        4 + 3 * len(SUM_PARTS) :
    ]
    row, z, x, core = torus_place()
    place = {"x": x, "y": row, "z": z}
    barrier = pltpu.get_barrier_semaphore()
    pl.semaphore_signal(barrier, inc=1, device_id=axis_peer("core", 1), device_id_type=MESH_ID)
    for axis in ("x", "y", "z"):
        for step in (1, 2, 3):
            pl.semaphore_signal(barrier, inc=1, device_id=axis_peer(axis, step), device_id_type=MESH_ID)
    loads = []
    for p, (rows, first, order, kind) in enumerate(SUM_PARTS):
        mine = pl.multiple_of(core * SUM_ROWS[kind] + first, 256)
        load = pltpu.make_async_copy(
            inputs[kind].at[pl.ds(mine, rows)], held[kind].at[pl.ds(first, rows)], load_sem.at[p]
        )
        load.start()
        loads.append(load)
    pl.semaphore_wait(barrier, 10)
    swaps = []
    for p, (rows, first, order, kind) in enumerate(SUM_PARTS):
        yours = pl.multiple_of((1 - core) * SUM_ROWS[kind] + first, 256)
        swap = pltpu.make_async_remote_copy(
            inputs[kind].at[pl.ds(yours, rows)],
            other[kind].at[pl.ds(first, rows)],
            core_send.at[p],
            core_recv.at[p],
            device_id=axis_peer("core", 1),
            device_id_type=MESH_ID,
        )
        swap.start()
        swaps.append(swap)

    def add_rows(kind, start, rows, terms):
        if kind == 1:
            tile = min(rows, 128)
        else:
            tile = 80 if rows % 80 == 0 else 96
            tile = tile * 4 if rows % (tile * 4) == 0 else tile

        def body(i, carry):
            offset = pl.multiple_of(i * tile, 8 if kind == 1 else 16)
            here = pl.ds(pl.multiple_of(start + offset, 8 if kind == 1 else 16), tile)
            total = held[kind][here, :].astype(jnp.float32)
            for ref, base in terms:
                total = total + ref[pl.ds(pl.multiple_of(base + offset, 8 if kind == 1 else 16), tile), :].astype(jnp.float32)
            held[kind][here, :] = total.astype(held[kind].dtype)
            return carry

        lax.fori_loop(0, rows // tile, body, 0)

    def start_hop(p, level):
        rows, first, order, kind = SUM_PARTS[p]
        size = rows // 4 ** (level + 1)
        base = first
        for done in range(level):
            base = base + place[order[done]] * (rows // 4 ** (done + 1))
        axis = order[level]
        hops = []
        for step in (1, 2, 3):
            block = lax.rem(place[axis] + step, 4)
            hop = pltpu.make_async_remote_copy(
                held[kind].at[pl.ds(pl.multiple_of(base + block * size, 8 if kind == 1 else 16), size)],
                slots[p * 3 + level].at[pl.ds((step - 1) * size, size)],
                hop_send.at[p, level, step - 1],
                hop_recv.at[p, level, step - 1],
                device_id=axis_peer(axis, step),
                device_id_type=MESH_ID,
            )
            hop.start()
            hops.append(hop)
        return hops

    def end_hop(p, level, hops):
        rows, first, order, kind = SUM_PARTS[p]
        size = rows // 4 ** (level + 1)
        base = first
        for done in range(level + 1):
            base = base + place[order[done]] * (rows // 4 ** (done + 1))
        for hop in hops:
            hop.wait()
        add_rows(kind, base, size, [(slots[p * 3 + level], step * size) for step in range(3)])

    count = len(SUM_PARTS)
    flight = [None] * count
    for p in range(count):
        rows, first, order, kind = SUM_PARTS[p]
        loads[p].wait()
        swaps[p].wait()
        add_rows(kind, first, rows, [(other[kind], first)])
        flight[p] = start_hop(p, 0)
    partner = row + 1 - 2 * lax.rem(row, 2)
    weight_move = pltpu.make_async_remote_copy(
        grad_send.at[pl.ds(2 * GRAD_EARLY, GRAD_LATE)],
        grad_mate,
        w_send,
        w_recv,
        device_id=(partner, lax.axis_index("col")),
        device_id_type=MESH_ID,
    )
    weight_move.start()
    for level in (1, 2):
        for p in range(count):
            end_hop(p, level - 1, flight[p])
            flight[p] = start_hop(p, level)

    def place_of(p, levels):
        rows, first, order, kind = SUM_PARTS[p]
        base = first
        for done in range(levels):
            base = base + place[order[done]] * (rows // 4 ** (done + 1))
        return base

    def gather(p, level):
        rows, first, order, kind = SUM_PARTS[p]
        size = rows // 4 ** (level + 1)
        align = 8 if kind == 1 else 16
        here = pl.multiple_of(place_of(p, level + 1), align)
        there = pl.multiple_of(place_of(p, level + 1) + core * SUM_ROWS[kind], align)
        source = held[kind].at[pl.ds(here, size)] if level == 2 else results[kind].at[pl.ds(there, size)]
        moves = []
        for step in (1, 2, 3):
            move = pltpu.make_async_remote_copy(
                source,
                results[kind].at[pl.ds(there, size)],
                gather_send.at[p, level, step - 1],
                gather_recv.at[p, level, step - 1],
                device_id=axis_peer(order[level], step),
                device_id_type=MESH_ID,
            )
            move.start()
            moves.append(move)
        if level == 2:
            keep = pltpu.make_async_copy(source, results[kind].at[pl.ds(there, size)], copy_sem.at[p])
            keep.start()
            keep.wait()
        return moves

    for p in range(count):
        end_hop(p, 2, flight[p])
        flight[p] = gather(p, 2)
    for level in (1, 0):
        for p in range(count):
            for move in flight[p]:
                move.wait()
            flight[p] = gather(p, level)
    lasts = []
    for p in range(count):
        rows, first, order, kind = SUM_PARTS[p]
        size = rows // 4
        for index in range(4):
            if index > 0:
                flight[p][index - 1].wait()
            block = lax.rem(place[order[0]] + 4 - index, 4)
            there = pl.ds(pl.multiple_of(first + block * size + core * SUM_ROWS[kind], 8 if kind == 1 else 16), size)
            last = pltpu.make_async_remote_copy(
                results[kind].at[there],
                results[kind].at[there],
                last_send.at[p, index],
                last_recv.at[p, index],
                device_id=axis_peer("core", 1),
                device_id_type=MESH_ID,
            )
            last.start()
            lasts.append(last)
    for last in lasts:
        last.wait()
    weight_move.wait()


def sum_over_devices(weights, small, grad_send):
    scratch = [
        pltpu.VMEM((SUM_ROWS[0], 128), jnp.bfloat16),
        pltpu.VMEM((SUM_ROWS[1], 128), jnp.float32),
        pltpu.VMEM((SUM_ROWS[0], 128), jnp.bfloat16),
        pltpu.VMEM((SUM_ROWS[1], 128), jnp.float32),
    ]
    for rows, first, order, kind in SUM_PARTS:
        for level in range(3):
            scratch.append(
                pltpu.VMEM((3 * rows // 4 ** (level + 1), 128), jnp.float32 if kind == 1 else jnp.bfloat16)
            )
    count = len(SUM_PARTS)
    dma = pltpu.SemaphoreType.DMA
    scratch += [
        dma((count,)),
        dma((count,)),
        dma((count,)),
        dma((count, 3, 3)),
        dma((count, 3, 3)),
        dma((count, 3, 3)),
        dma((count, 3, 3)),
        dma((count,)),
        dma((count, 4)),
        dma((count, 4)),
        dma,
        dma,
    ]
    return pl.pallas_call(
        sum_kernel,
        out_shape=(
            jax.ShapeDtypeStruct((2 * SUM_ROWS[0], 128), jnp.bfloat16),
            jax.ShapeDtypeStruct((2 * SUM_ROWS[1], 128), jnp.float32),
            jax.ShapeDtypeStruct((GRAD_LATE, WIDTH), jnp.bfloat16),
        ),
        in_specs=[pl.BlockSpec(memory_space=pl.ANY)] * 3,
        out_specs=[pl.BlockSpec(memory_space=pl.ANY)] * 3,
        scratch_shapes=scratch,
        compiler_params=pltpu.CompilerParams(
            collective_id=4, has_side_effects=True, vmem_limit_bytes=48 * 1024 * 1024
        ),
        name="sum_over_devices",
    )(weights, small, grad_send)


def finish_sums(grads):
    def kernel(grads_ref, *results):
        for which, result in enumerate(results):
            for i in range(8):
                result[:, i * 128 : (i + 1) * 128] = grads_ref[which, i].astype(F32)

    return pl.pallas_call(
        kernel,
        grid=(8,),
        out_shape=(jax.ShapeDtypeStruct((WIDTH, WIDTH), F32),) * 4,
        in_specs=[pl.BlockSpec((4, 8, 128, 128), lambda i: (0, 0, i, 0))],
        out_specs=(pl.BlockSpec((128, WIDTH), lambda i: (i, 0)),) * 4,
        name="finish_sums",
    )(grads.reshape(4, 8, WIDTH, 128))


def finish_experts(own, early, late):
    tile = 176
    early_steps = 2 * GRAD_EARLY // tile
    per_matrix = SHARD // tile

    def kernel(own_ref, early_ref, late_ref, *results):
        step = pl.program_id(0)
        total = own_ref[...] + jnp.where(step < early_steps, early_ref[...], late_ref[...]).astype(F32)
        for which, result in enumerate(results):

            @pl.when(step // per_matrix == which)
            def _():
                result[...] = total

    def spec(index):
        return pl.BlockSpec((tile, WIDTH), lambda i: (index(i), 0))

    def result_spec(which):
        return spec(lambda i: jnp.clip(i - which * per_matrix, 0, per_matrix - 1))

    return pl.pallas_call(
        kernel,
        grid=(GRAD_ROWS // tile,),
        out_shape=(jax.ShapeDtypeStruct((SHARD, WIDTH), F32),) * 3,
        in_specs=[
            spec(lambda i: i),
            spec(lambda i: jnp.minimum(i, early_steps - 1)),
            spec(lambda i: jnp.maximum(i - early_steps, 0)),
        ],
        out_specs=tuple(result_spec(which) for which in range(3)),
        name="finish_experts",
    )(own, early, late)


def per_device(
    tokens_in, out_cot, long_lengths, short_lengths, routes, gain_attn, w_query, w_key, w_value, w_out, rel_bias,
    gain_moe, router, w_gate, w_up, w_down,
):
    own = (jnp.swapaxes(w_gate[0], 0, 1), jnp.swapaxes(w_up[0], 0, 1), w_down[0])
    routes_t = jnp.swapaxes(routes, 0, 1)
    router_t = jnp.swapaxes(router, 0, 1)
    rel_bias_t = jnp.swapaxes(rel_bias, 0, 1)
    gain_a, gain_m = gain_attn.reshape(1, WIDTH), gain_moe.reshape(1, WIDTH)
    ids = piece_ids()
    sent = forward(
        long_lengths, short_lengths, tokens_in, out_cot, routes_t, gain_a, gain_m, rel_bias_t, router_t,
        jnp.asarray(ids.T), w_query, w_key, w_value, w_out, *own,
    )
    x_slots, o_slots, g_slots, *other = sent[:6]
    query, long_kv, short_kv, mixed, norm_l, norm_s, resid, probs_t, rnorm_t = sent[6:]
    unfold = unfold_matrix()
    row_of = np.arange(640) // SLOTS
    consts = (
        jnp.asarray(unfold, BF16),
        jnp.asarray(unfold.T, BF16),
        jnp.asarray((row_of[:, None] == np.arange(EXPERTS)[None, :]).astype(np.float32)),
        jnp.asarray((np.arange(640) % SLOTS).astype(np.int32)[:, None]),
    )
    dx_back, dg_back, outs, grad_own, grad_send = experts(x_slots, o_slots, g_slots, consts, own, other)
    block_out, tokens_grad, grads, small, grad_early = backward(
        long_lengths, short_lengths, tokens_in, out_cot, routes, routes_t, gain_a, gain_m, rel_bias_t, router_t,
        jnp.asarray(ids), w_query, w_key, w_value, w_out, resid, probs_t, rnorm_t, query, long_kv, short_kv, mixed,
        norm_l, norm_s, dx_back, dg_back, outs, grad_send,
    )
    grads, small, grad_late = sum_over_devices(grads, small, grad_send)
    grads = finish_sums(grads)
    expert_grads = finish_experts(grad_own, grad_early, grad_late)
    totals = small[288]
    statistics = jnp.sqrt(totals[0:3] / (totals[3] * WIDTH))
    router_grad = small[0:256].reshape(8, EXPERTS, 128).transpose(1, 0, 2).reshape(EXPERTS, WIDTH)
    return (
        block_out,
        tokens_grad,
        small[256:264].reshape(WIDTH),
        grads[0],
        grads[1],
        grads[2],
        grads[3],
        jnp.swapaxes(small[272:288, 0:32], 0, 1),
        small[264:272].reshape(WIDTH),
        jnp.swapaxes(router_grad, 0, 1),
        jnp.swapaxes(expert_grads[0], 0, 1)[None],
        jnp.swapaxes(expert_grads[1], 0, 1)[None],
        expert_grads[2][None],
        statistics,
    )


def solution(mesh):
    tokens = P(("row", "col"), None)
    whole = P()
    wide = P("col", None, "row")
    tall = P("col", "row", None)
    return jax.shard_map(
        per_device,
        mesh=mesh,
        in_specs=(tokens, tokens, P("col"), P(("row", "col")), tokens) + (whole,) * 8 + (wide, wide, tall),
        out_specs=(tokens, tokens) + (whole,) * 8 + (wide, wide, tall, whole),
        check_vma=False,
    )
```

```python
import functools

import numpy as np
import jax
import jax.numpy as jnp
from jax import lax
from jax.experimental import pallas as pl
from jax.experimental.pallas import tpu as pltpu
from jax.sharding import PartitionSpec as P

HEADS = 16
HEAD_DIM = 64
WIDTH = 1024
ROWS = 256
LONG = 128
EXPERTS = 32
SLOTS = 20
FOLDED = 80
QUARTER = 256
PIECES = EXPERTS * FOLDED
TABLE = 640
SHARD = 704
PADDED = 768
EARLY_DOWN = 352
FIRST_DOWN = 176
GRAD_ROWS = 3 * SHARD
GRAD_PIECES = (528, 208, 224, 224, 224)

bucket_edges = (1, 2, 3, 4, 5, 6, 7, 8, 12, 16, 23, 32, 46, 64, 91)
norm_eps = 1e-06
balance_coef = 0.01
zloss_coef = 0.001
masked_score = -1e30
highest = lax.Precision.HIGHEST
MESH_ID = pl.DeviceIdType.MESH
F32 = jnp.float32
BF16 = jnp.bfloat16
VMEM_SPEC = pl.BlockSpec(memory_space=pltpu.VMEM)
HBM_SPEC = pl.BlockSpec(memory_space=pl.ANY)
SMEM_SPEC = pl.BlockSpec(memory_space=pltpu.SMEM)
DMA = pltpu.SemaphoreType.DMA


def piece_ids():
    row = np.arange(PIECES)
    slot = (row // FOLDED) * SLOTS + row % SLOTS
    quarter = (row % FOLDED) // SLOTS
    return np.stack([slot, quarter]).astype(np.float32)


def unfold_matrix():
    out = np.arange(320)
    quarter, message, slot = out // 80, (out % 80) // SLOTS, out % SLOTS
    hot = np.zeros((320, 320), np.float32)
    hot[out, message * FOLDED + quarter * SLOTS + slot] = 1
    return hot


def nt(left, right, precision=None):
    return lax.dot_general(
        left, right, (((1,), (1,)), ((), ())), preferred_element_type=F32, precision=precision
    )


def tn(left, right):
    return lax.dot_general(left, right, (((0,), (0,)), ((), ())), preferred_element_type=F32)


def nn(left, right, precision=None):
    return jnp.dot(left, right, preferred_element_type=F32, precision=precision)


def iota(shape, dim):
    return lax.broadcasted_iota(jnp.int32, shape, dim)


def block(index, size):
    return pl.ds(pl.multiple_of(index * size, size), size)


def bucket_hot(relative):
    magnitude = jnp.abs(relative)
    level = jnp.zeros_like(relative)
    for edge in bucket_edges:
        level = level + (magnitude >= edge).astype(jnp.int32)
    level = level + jnp.where(relative > 0, len(bucket_edges) + 1, 0)
    return (iota((32, relative.shape[1]), 0) == level).astype(F32)


def route_places(routes_t):
    hots = [(iota((EXPERTS, ROWS), 0) == routes_t[k : k + 1, :]).astype(F32) for k in range(2)]
    both = hots[0] + hots[1]
    before = (iota((ROWS, ROWS), 0) < iota((ROWS, ROWS), 1)).astype(BF16)
    earlier = nn(both.astype(BF16), before)
    slots = [jnp.sum(earlier * hot, axis=0, keepdims=True) for hot in hots]
    places = [routes_t[k : k + 1, :].astype(F32) * SLOTS + slots[k] for k in range(2)]
    return hots, both, slots, places


def slot_hot(slots_row):
    return (iota((128, ROWS), 0).astype(F32) == slots_row).astype(F32)


def live_column(long_len, short_len, row):
    position = iota((ROWS, 1), 0)
    is_long = position < LONG
    here = jnp.where(is_long, position + row * LONG, position - LONG)
    limit = jnp.where(is_long, long_len, short_len)
    return (here < limit).astype(F32)


SUM_PARTS = (
    (4096, 0, ("x", "z", "y"), 0),
    (4096, 4096, ("z", "x", "y"), 0),
    (3072, 8192, ("x", "y", "z"), 0),
    (3072, 11264, ("z", "x", "y"), 0),
    (2048, 14336, ("y", "z", "x"), 0),
    (512, 0, ("y", "x", "z"), 1),
)
SUM_ROWS = (16384, 512)
SUM_COUNT = len(SUM_PARTS)


def torus_place():
    row = lax.axis_index("row")
    col = lax.axis_index("col")
    return row, lax.div(col, 8), lax.rem(lax.div(col, 2), 4), lax.rem(col, 2)


def axis_peer(axis, step):
    row, z, x, core = torus_place()
    if axis == "y":
        row = lax.rem(row + step, 4)
    elif axis == "x":
        x = lax.rem(x + step, 4)
    elif axis == "z":
        z = lax.rem(z + step, 4)
    else:
        core = 1 - core
    return (row, (z * 4 + x) * 2 + core)


class SumSteps:
    def __init__(self, sources, results, other, slots, sems):
        self.sources, self.results, self.other, self.slots = sources, results, other, slots
        (
            self.core_send, self.core_recv, self.hop_send, self.hop_recv, self.gather_send, self.gather_recv,
            self.copy_sem, self.last_send, self.last_recv,
        ) = sems
        row, z, x, self.core = torus_place()
        self.place = {"x": x, "y": row, "z": z}
        self.flight = {}

    def base(self, p, levels):
        rows, first, order, kind = SUM_PARTS[p]
        base = self.core * SUM_ROWS[kind] + first
        for done in range(levels):
            base = base + self.place[order[done]] * (rows // 4 ** (done + 1))
        return base

    def at(self, kind, start, rows):
        return pl.ds(pl.multiple_of(start, 8 if kind else 16), rows)

    def add(self, kind, start, rows, terms):
        if kind:
            tile = min(rows, 128)
        else:
            tile = next(t for t in (512, 384, 256, 192, 128, 64, 48, 32) if rows % t == 0)
        source = self.sources[kind]

        def body(i, carry):
            here = self.at(kind, start + i * tile, tile)
            total = source[here, :].astype(F32)
            for ref, first in terms:
                total = total + ref[self.at(kind, first + i * tile, tile), :].astype(F32)
            source[here, :] = total.astype(source.dtype)
            return carry

        lax.fori_loop(0, rows // tile, body, 0)

    def swap(self, p):
        rows, first, order, kind = SUM_PARTS[p]
        theirs = (1 - self.core) * SUM_ROWS[kind] + first
        move = pltpu.make_async_remote_copy(
            self.sources[kind].at[self.at(kind, theirs, rows)],
            self.other[kind].at[pl.ds(first, rows)],
            self.core_send.at[p],
            self.core_recv.at[p],
            device_id=axis_peer("core", 1),
            device_id_type=MESH_ID,
        )
        move.start()
        self.flight[p] = [move]

    def hop(self, p, level):
        rows, first, order, kind = SUM_PARTS[p]
        for move in self.flight[p]:
            move.wait()
        if level == 0:
            self.add(kind, self.base(p, 0), rows, [(self.other[kind], first)])
        else:
            self.end_hop(p, level - 1)
        size = rows // 4 ** (level + 1)
        axis = order[level]
        self.flight[p] = []
        for step in (1, 2, 3):
            block_of = lax.rem(self.place[axis] + step, 4)
            move = pltpu.make_async_remote_copy(
                self.sources[kind].at[self.at(kind, self.base(p, level) + block_of * size, size)],
                self.slots[p * 3 + level].at[pl.ds((step - 1) * size, size)],
                self.hop_send.at[p, level, step - 1],
                self.hop_recv.at[p, level, step - 1],
                device_id=axis_peer(axis, step),
                device_id_type=MESH_ID,
            )
            move.start()
            self.flight[p].append(move)

    def end_hop(self, p, level):
        rows, first, order, kind = SUM_PARTS[p]
        size = rows // 4 ** (level + 1)
        slots = self.slots[p * 3 + level]
        self.add(kind, self.base(p, level + 1), size, [(slots, step * size) for step in range(3)])

    def gather(self, p, level):
        rows, first, order, kind = SUM_PARTS[p]
        for move in self.flight[p]:
            move.wait()
        if level == 2:
            self.end_hop(p, 2)
        here = self.at(kind, self.base(p, level + 1), rows // 4 ** (level + 1))
        source = self.sources[kind].at[here] if level == 2 else self.results[kind].at[here]
        target = self.results[kind].at[here]
        self.flight[p] = []
        for step in (1, 2, 3):
            move = pltpu.make_async_remote_copy(
                source,
                target,
                self.gather_send.at[p, level, step - 1],
                self.gather_recv.at[p, level, step - 1],
                device_id=axis_peer(order[level], step),
                device_id_type=MESH_ID,
            )
            move.start()
            self.flight[p].append(move)
        if level == 2:
            keep = pltpu.make_async_copy(source, target, self.copy_sem.at[p])
            keep.start()
            self.flight[p].append(keep)

    def last(self, p):
        rows, first, order, kind = SUM_PARTS[p]
        size = rows // 4
        moves = []
        for index in range(4):
            if index > 0:
                self.flight[p][index - 1].wait()
            block_of = lax.rem(self.place[order[0]] + 4 - index, 4)
            here = self.results[kind].at[self.at(kind, self.base(p, 0) + block_of * size, size)]
            move = pltpu.make_async_remote_copy(
                here,
                here,
                self.last_send.at[p, index],
                self.last_recv.at[p, index],
                device_id=axis_peer("core", 1),
                device_id_type=MESH_ID,
            )
            move.start()
            moves.append(move)
        self.flight[p] = moves

    def end(self, p):
        for move in self.flight[p]:
            move.wait()


def sum_scratch():
    scratch = [
        pltpu.VMEM((SUM_ROWS[0], 128), BF16),
        pltpu.VMEM((SUM_ROWS[1], 128), F32),
    ]
    for rows, first, order, kind in SUM_PARTS:
        for level in range(3):
            scratch.append(pltpu.VMEM((3 * rows // 4 ** (level + 1), 128), F32 if kind else BF16))
    shapes = [(SUM_COUNT,)] * 2 + [(SUM_COUNT, 3, 3)] * 4 + [(SUM_COUNT,)] + [(SUM_COUNT, 4)] * 2
    return scratch + [DMA(shape) for shape in shapes]


def finish_sums(grads):
    def kernel(grads_ref, *results):
        for which, result in enumerate(results):
            for i in range(8):
                result[:, i * 128 : (i + 1) * 128] = grads_ref[i // 4, which, i % 4].astype(F32)

    return pl.pallas_call(
        kernel,
        grid=(4,),
        out_shape=(jax.ShapeDtypeStruct((WIDTH, WIDTH), F32),) * 4,
        in_specs=[pl.BlockSpec((2, 4, 4, 256, 128), lambda i: (0, 0, 0, i, 0))],
        out_specs=(pl.BlockSpec((256, WIDTH), lambda i: (i, 0)),) * 4,
        name="finish_sums",
    )(grads.reshape(2, 4, 4, WIDTH, 128))


def finish_experts(own, early, late):
    tile = 352
    per_matrix = SHARD // tile

    def kernel(own_ref, early_ref, late_ref, *results):
        step = pl.program_id(0)
        total = own_ref[...] + jnp.where(step < per_matrix, early_ref[...], late_ref[...]).astype(F32)
        for which, result in enumerate(results):

            @pl.when(step // per_matrix == which)
            def _():
                result[...] = total

    def spec(index):
        return pl.BlockSpec((tile, WIDTH), lambda i: (index(i), 0))

    def result_spec(which):
        return spec(lambda i: jnp.clip(i - which * per_matrix, 0, per_matrix - 1))

    return pl.pallas_call(
        kernel,
        grid=(GRAD_ROWS // tile,),
        out_shape=(jax.ShapeDtypeStruct((SHARD, WIDTH), F32),) * 3,
        in_specs=[
            spec(lambda i: i),
            spec(lambda i: jnp.minimum(i, per_matrix - 1)),
            spec(lambda i: jnp.maximum(i - per_matrix, 0)),
        ],
        out_specs=tuple(result_spec(which) for which in range(3)),
        name="finish_experts",
    )(own, early, late)


def forward_kernel(
    long_len, short_len, tokens, cot, routes_t, gain_a, gain_m, rel_bias_t, router_t, ids, wq, wk, wv, wo, wg_own, wu_own, wd_own,
    x_slots, o_slots, g_slots, wg_mate, wu_mate, wd_mate, query, long_kv, short_kv, mixed, norm_l, norm_s, resid, probs_t, rnorm_t,
    normed, buffer_o, buffer_x, gate_out, table_l, table_s,
    o_send, o_recv, x_send, x_recv, g_send, g_recv, own_sem, kv_send, kv_recv, t_send, t_recv, w_send, w_recv,
):
    row = lax.axis_index("row")
    col = lax.axis_index("col")
    mate = 3 - row
    barrier = pltpu.get_barrier_semaphore()
    for step in (1, 2, 3):
        pl.semaphore_signal(barrier, inc=1, device_id=(lax.rem(row + step, 4), col), device_id_type=MESH_ID)

    def greet(step, carry):
        pl.semaphore_signal(barrier, inc=1, device_id=(row, lax.rem(col + step, EXPERTS)), device_id_type=MESH_ID)
        return carry

    lax.fori_loop(1, EXPERTS, greet, 0)

    hots, both, slots, places = route_places(routes_t[...])

    def message(buffer, slots_ref, send, recv, dest, source):
        return pltpu.make_async_remote_copy(
            buffer.at[block(dest, FOLDED)],
            slots_ref.at[0, block(source, FOLDED)],
            send.at[dest],
            recv.at[source],
            device_id=(row, dest),
            device_id_type=MESH_ID,
        )

    def dispatch(source, buffer, slots_ref, send, recv, own):
        def one_group(i, carry):
            group = lax.rem(lax.div(col, 4) + i, 8)
            rows = block(group, 320)
            slot_id = ids[rows, 0:1]
            quarter = ids[rows, 1:2]
            match = (slot_id == places[0]) | (slot_id == places[1])
            total = jnp.zeros((320, QUARTER), F32)
            for q in range(4):
                hot = jnp.where(match & (quarter == q), 1.0, 0.0).astype(BF16)
                total = total + nn(hot, source[:, q * QUARTER : (q + 1) * QUARTER])
            buffer[rows, :] = total.astype(BF16)
            for j in range(4):
                dest = group * 4 + j

                @pl.when(dest != col)
                def _():
                    message(buffer, slots_ref, send, recv, dest, col).start()

                @pl.when(dest == col)
                def _():
                    pltpu.make_async_copy(
                        buffer.at[block(dest, FOLDED)], slots_ref.at[0, block(dest, FOLDED)], own
                    ).start()

            return carry

        lax.fori_loop(0, 8, one_group, 0)

    def wait_source(buffer, slots_ref, send, recv, own, source):
        @pl.when(source != col)
        def _():
            message(buffer, slots_ref, send, recv, col, source).wait_recv()

        @pl.when(source == col)
        def _():
            pltpu.make_async_copy(
                buffer.at[block(col, FOLDED)], slots_ref.at[0, block(col, FOLDED)], own
            ).wait()

    def wait_sends(buffer, slots_ref, send, recv):
        def one(step, carry):
            message(buffer, slots_ref, send, recv, lax.rem(col + step, EXPERTS), col).wait_send()
            return carry

        lax.fori_loop(1, EXPERTS, one, 0)

    pl.semaphore_wait(barrier, EXPERTS + 2)

    partner = row + 1 - 2 * lax.rem(row, 2)
    down_pieces = [pl.ds(0, FIRST_DOWN), pl.ds(FIRST_DOWN, EARLY_DOWN - FIRST_DOWN)]
    weight_moves = [
        pltpu.make_async_remote_copy(
            source, target, w_send.at[i], w_recv.at[i], device_id=(partner, col), device_id_type=MESH_ID
        )
        for i, (source, target) in enumerate(
            (
                (wd_own.at[down_pieces[0]], wd_mate.at[down_pieces[0]]),
                (wg_own, wg_mate),
                (wu_own, wu_mate),
                (wd_own.at[down_pieces[1]], wd_mate.at[down_pieces[1]]),
            )
        )
    ]
    weight_moves[0].start()

    def norm_rows(i, carry):
        rows = block(i, 64)
        x = tokens[rows, :].astype(F32)
        scale = lax.rsqrt(jnp.mean(x * x, axis=1, keepdims=True) + norm_eps)
        normed[rows, :] = (x * scale * gain_a[...]).astype(BF16)
        return carry

    lax.fori_loop(0, 4, norm_rows, 0)

    def project_kv(i, carry):
        lanes = block(i, 256)
        for offset, weight in ((0, wk), (WIDTH, wv)):
            part = nn(normed[...], weight[:, lanes]).astype(BF16)
            out = pl.ds(pl.multiple_of(i * 256 + offset, 256), 256)
            long_kv[row, :, out] = part[:LONG]
            short_kv[:, out] = part[LONG:]
        return carry

    lax.fori_loop(0, 4, project_kv, 0)

    def kv_move(step):
        return pltpu.make_async_remote_copy(
            long_kv.at[row],
            long_kv.at[row],
            kv_send.at[step - 1],
            kv_recv.at[step - 1],
            device_id=(lax.rem(row + step, 4), col),
            device_id_type=MESH_ID,
        )

    def kv_arrival(step):
        source = lax.rem(row + 4 - step, 4)
        return pltpu.make_async_remote_copy(
            long_kv.at[source],
            long_kv.at[source],
            kv_send.at[step - 1],
            kv_recv.at[step - 1],
            device_id=(source, col),
            device_id_type=MESH_ID,
        )

    for step in (1, 2, 3):
        kv_move(step).start()

    for move in weight_moves[1:]:
        move.start()

    dispatch(cot, buffer_o, o_slots, o_send, o_recv, own_sem.at[0])

    def project_q(i, carry):
        lanes = block(i, 256)
        query[:, lanes] = nn(normed[...], wq[:, lanes]).astype(BF16)
        return carry

    lax.fori_loop(0, 4, project_q, 0)

    place_l = iota((1, TABLE), 1)
    place_l = jnp.where(place_l < 512, place_l, place_l - TABLE) - row * LONG
    place_s = iota((1, 256), 1)
    place_s = jnp.where(place_s < 128, place_s, place_s - 256)
    table_l[...] = nn(rel_bias_t[...], bucket_hot(place_l), highest)
    table_s[...] = nn(rel_bias_t[...], bucket_hot(place_s), highest)

    lane = iota((1, 128), 1)

    def attend(q2, k2, v2, table, head, keep, count, width):
        bias = pltpu.roll(
            jnp.broadcast_to(table[pl.ds(head, 1), :], (128, width)), 0, 1, stride=1, stride_axis=0
        )[:, :count]
        scores = jnp.where(keep, nt(q2, k2) * 0.125 + bias, masked_score)
        row_max = jnp.max(scores, axis=1, keepdims=True)
        terms = jnp.exp(scores - row_max)
        total = jnp.sum(terms, axis=1, keepdims=True)
        return nn((terms / total).astype(BF16), v2), row_max + jnp.log(total)

    def attend_pairs(q_first, keys_of, table, keep, count, width, norm_out):
        def one_pair(pair, carry):
            lanes = block(pair, 128)
            values = pl.ds(pl.multiple_of(pair * 128 + WIDTH, 128), 128)
            q2 = query[q_first : q_first + 128, lanes]
            k2, v2 = keys_of(lanes), keys_of(values)
            outs = []
            norms = norm_out[...]
            for side in range(2):
                here = (lane >= 64) if side else (lane < 64)
                out, norm = attend(
                    jnp.where(here, q2, jnp.zeros_like(q2)), k2, v2, table, pair * 2 + side, keep, count, width
                )
                outs.append(out)
                norms = jnp.where(lane == pair * 2 + side, norm, norms)
            norm_out[...] = norms
            mixed[q_first : q_first + 128, lanes] = jnp.where(lane < 64, outs[0], outs[1]).astype(BF16)
            return carry

        lax.fori_loop(0, HEADS // 2, one_pair, 0)

    norm_l[...] = jnp.zeros_like(norm_l)
    norm_s[...] = jnp.zeros_like(norm_s)
    attend_pairs(LONG, lambda lanes: short_kv[:, lanes], table_s, iota((1, 128), 1) < short_len[0], 128, 256, norm_s)

    def wait_o(source, carry):
        wait_source(buffer_o, o_slots, o_send, o_recv, own_sem.at[0], source)
        return carry

    lax.fori_loop(0, EXPERTS, wait_o, 0)

    def to_mate(source, target, index):
        return pltpu.make_async_remote_copy(
            source, target, t_send.at[index], t_recv.at[index], device_id=(mate, col), device_id_type=MESH_ID
        )

    for step in (1, 2, 3):
        kv_arrival(step).wait_recv()
    o_move = to_mate(o_slots.at[0], o_slots.at[1], 8)
    o_move.start()
    attend_pairs(
        0,
        lambda lanes: long_kv[:, :, lanes].reshape(512, 128),
        table_l,
        iota((1, 512), 1) < long_len[0],
        512,
        TABLE,
        norm_l,
    )

    def project_out(i, carry):
        lanes = block(i, 256)
        resid[:, lanes] = tokens[:, lanes].astype(F32) + nn(mixed[...], wo[:, lanes])
        return carry

    lax.fori_loop(0, 4, project_out, 0)

    def norm_again(i, carry):
        rows = block(i, 64)
        x = resid[rows, :]
        scale = lax.rsqrt(jnp.mean(x * x, axis=1, keepdims=True) + norm_eps)
        normed[rows, :] = (x * scale * gain_m[...]).astype(BF16)
        return carry

    lax.fori_loop(0, 4, norm_again, 0)
    dispatch(normed, buffer_x, x_slots, x_send, x_recv, own_sem.at[1])

    x = resid[...]
    scale = lax.rsqrt(jnp.mean(x * x, axis=1, keepdims=True) + norm_eps)
    logits = nt(router_t[...], x * scale * gain_m[...], highest)
    row_max = jnp.max(logits, axis=0, keepdims=True)
    terms = jnp.exp(logits - row_max)
    total = jnp.sum(terms, axis=0, keepdims=True)
    probs = terms / total
    probs_t[...] = probs
    rnorm_t[...] = row_max + jnp.log(total)
    picked = [jnp.sum(probs * hot, axis=0, keepdims=True) for hot in hots]
    picked_sum = picked[0] + picked[1]
    gate_slots = jnp.zeros((EXPERTS, 128), F32)
    for k in range(2):
        gate_slots = gate_slots + nt(hots[k] * (picked[k] / picked_sum), slot_hot(slots[k]), highest)
    for e in range(EXPERTS):
        gate_out[e] = jnp.broadcast_to(gate_slots[e : e + 1, :], (8, 128))

    def gate_message(dest, source):
        return pltpu.make_async_remote_copy(
            gate_out.at[dest],
            g_slots.at[0, source],
            g_send.at[dest],
            g_recv.at[source],
            device_id=(row, dest),
            device_id_type=MESH_ID,
        )

    def send_gates(step, carry):
        gate_message(lax.rem(col + step, EXPERTS), col).start()
        return carry

    lax.fori_loop(1, EXPERTS, send_gates, 0)
    own_gates = pltpu.make_async_copy(gate_out.at[col], g_slots.at[0, col], own_sem.at[2])
    own_gates.start()

    def x_move(group):
        rows = block(group, 320)
        return to_mate(x_slots.at[0, rows], x_slots.at[1, rows], group)

    def forward_x(i, carry):
        group = lax.rem(lax.div(col, 4) + 8 - i, 8)
        for j in range(4):
            wait_source(buffer_x, x_slots, x_send, x_recv, own_sem.at[1], group * 4 + j)
        x_move(group).start()
        return carry

    lax.fori_loop(0, 8, forward_x, 0)

    def wait_gates(step, carry):
        gate_message(col, lax.rem(col + step, EXPERTS)).wait_recv()
        return carry

    lax.fori_loop(1, EXPERTS, wait_gates, 0)
    own_gates.wait()
    g_move = to_mate(g_slots.at[0], g_slots.at[1], 9)
    g_move.start()

    for step in (1, 2, 3):
        kv_move(step).wait_send()
    wait_sends(buffer_o, o_slots, o_send, o_recv)
    wait_sends(buffer_x, x_slots, x_send, x_recv)

    def wait_gate_sends(step, carry):
        gate_message(lax.rem(col + step, EXPERTS), col).wait_send()
        return carry

    lax.fori_loop(1, EXPERTS, wait_gate_sends, 0)
    o_move.wait()

    def wait_x(group, carry):
        x_move(group).wait()
        return carry

    lax.fori_loop(0, 8, wait_x, 0)
    g_move.wait()
    for move in weight_moves:
        move.wait()


def forward(long_lengths, short_lengths, tokens, cot, routes_t, gain_a, gain_m, rel_bias_t, router_t, ids, wq, wk, wv, wo, wg, wu, wd):
    def out(shape, dtype):
        return jax.ShapeDtypeStruct(shape, dtype)

    return pl.pallas_call(
        forward_kernel,
        out_shape=(
            out((2, PIECES, QUARTER), BF16),
            out((2, PIECES, QUARTER), BF16),
            out((2, EXPERTS, 8, 128), F32),
            out((SHARD, WIDTH), BF16),
            out((SHARD, WIDTH), BF16),
            out((EARLY_DOWN, WIDTH), BF16),
            out((ROWS, WIDTH), BF16),
            out((4, LONG, 2 * WIDTH), BF16),
            out((LONG, 2 * WIDTH), BF16),
            out((ROWS, WIDTH), BF16),
            out((128, 128), F32),
            out((128, 128), F32),
            out((ROWS, WIDTH), F32),
            out((EXPERTS, ROWS), F32),
            out((1, ROWS), F32),
        ),
        in_specs=[SMEM_SPEC] * 2 + [VMEM_SPEC] * 12 + [HBM_SPEC] * 3,
        out_specs=[HBM_SPEC] * 6 + [VMEM_SPEC] * 9,
        scratch_shapes=[
            pltpu.VMEM((ROWS, WIDTH), BF16),
            pltpu.VMEM((PIECES, QUARTER), BF16),
            pltpu.VMEM((PIECES, QUARTER), BF16),
            pltpu.VMEM((EXPERTS, 8, 128), F32),
            pltpu.VMEM((HEADS, TABLE), F32),
            pltpu.VMEM((HEADS, 256), F32),
            DMA((EXPERTS,)),
            DMA((EXPERTS,)),
            DMA((EXPERTS,)),
            DMA((EXPERTS,)),
            DMA((EXPERTS,)),
            DMA((EXPERTS,)),
            DMA((3,)),
            DMA((3,)),
            DMA((3,)),
            DMA((10,)),
            DMA((10,)),
            DMA((4,)),
            DMA((4,)),
        ],
        compiler_params=pltpu.CompilerParams(
            collective_id=1, has_side_effects=True, vmem_limit_bytes=56 * 1024 * 1024
        ),
        name="forward_and_dispatch",
    )(
        long_lengths, short_lengths, tokens, cot, routes_t, gain_a, gain_m, rel_bias_t, router_t, ids, wq, wk, wv, wo,
        wg, wu, wd,
    )


def expert_kernel(
    x_slots, o_slots, g_slots, unfold, fold, row_hot, slot_of, wg_own, wu_own, wd_own, wg_mate, wu_mate, wd_mate,
    dx_back, dg_back, outs, grad_own, grad_send, grad_mate,
    stage, xs, os, dys, wg, wu, wd, act, dg, du, part, arrived, dxs, gate_part, gate_arrived, gate_out, grad_stage,
    grad_half, grad_first, stage_sem, weight_sem, late_send, late_recv, first_send, first_recv, t_send, t_recv, m_send, m_recv, r_send, r_recv, own_sem,
    out_sem,
):
    row = lax.axis_index("row")
    col = lax.axis_index("col")
    mate = 3 - row
    partner = row + 1 - 2 * lax.rem(row, 2)
    barrier = pltpu.get_barrier_semaphore()
    pl.semaphore_signal(barrier, inc=1, device_id=(mate, col), device_id_type=MESH_ID)
    pl.semaphore_signal(barrier, inc=1, device_id=(partner, col), device_id_type=MESH_ID)

    def greet(step, carry):
        pl.semaphore_signal(barrier, inc=1, device_id=(row, lax.rem(col + step, EXPERTS)), device_id_type=MESH_ID)
        return carry

    lax.fori_loop(1, EXPERTS, greet, 0)

    def load(source, which, index):
        return pltpu.make_async_copy(source.at[which], stage.at[index], stage_sem.at[index])

    load(x_slots, 1, 0).start()
    load(o_slots, 1, 1).start()
    weights = [[], []]
    for j, sources in enumerate(((wg_own, wu_own, wd_own), (wg_mate, wu_mate, wd_mate))):
        for i, (source, held) in enumerate(zip(sources, (wg, wu, wd))):
            copy = pltpu.make_async_copy(
                source, held.at[pl.ds(j * PADDED, source.shape[0])], weight_sem.at[i, j]
            )
            copy.start()
            weights[j].append(copy)
    for held in (wg, wu, wd):
        for j in range(2):
            held[j * PADDED + SHARD : (j + 1) * PADDED, :] = jnp.zeros((PADDED - SHARD, WIDTH), BF16)
    pl.semaphore_wait(barrier, EXPERTS + 1)
    late = pltpu.make_async_remote_copy(
        wd_own.at[pl.ds(EARLY_DOWN, SHARD - EARLY_DOWN)],
        wd.at[pl.ds(PADDED + EARLY_DOWN, SHARD - EARLY_DOWN)],
        late_send,
        late_recv,
        device_id=(partner, col),
        device_id_type=MESH_ID,
    )
    late.start()

    def spread(index, target, first):
        def one(group, carry):
            wide = nn(unfold[...], stage[index, block(group, 320), :]).astype(BF16)
            rows = pl.ds(pl.multiple_of(first + group * 80, 16), 80)
            for q in range(4):
                target[rows, q * QUARTER : (q + 1) * QUARTER] = wide[q * 80 : (q + 1) * 80]
            return carry

        lax.fori_loop(0, 8, one, 0)

    def gate_column(which):
        gates = jnp.concatenate([g_slots[which, e, 0:1, :] for e in range(EXPERTS)], axis=0)
        wide = nn(row_hot[...], gates, highest)
        lanes = iota((640, 128), 1)
        return jnp.sum(jnp.where(lanes == slot_of[...], wide, 0.0), axis=1, keepdims=True)

    def take_tokens(which, first):
        load(x_slots, which, 0).wait()
        spread(0, xs, first)
        load(o_slots, which, 1).wait()
        spread(1, os, first)
        rows = pl.ds(first, 640)
        dys[rows, :] = (os[rows, :].astype(F32) * gate_column(which)).astype(BF16)

    def hidden_half(first, half):
        lanes = slice(half * PADDED, (half + 1) * PADDED)
        rows = slice(first, first + 640)
        gate_pre = nt(xs[rows, :], wg[lanes, :])
        up_pre = nt(xs[rows, :], wu[lanes, :])
        d_act = nt(dys[rows, :], wd[lanes, :])
        square = gate_pre * gate_pre
        bend = jnp.tanh(0.7978845608028654 * gate_pre * (1.0 + 0.044715 * square))
        level = 0.5 * (1.0 + bend)
        gelu = gate_pre * level
        slope = level + 0.5 * gate_pre * (1.0 - bend * bend) * (
            0.7978845608028654 * (1.0 + 3.0 * 0.044715 * square)
        )
        act[rows, lanes] = (gelu * up_pre).astype(BF16)
        du[rows, lanes] = (d_act * gelu).astype(BF16)
        dg[rows, lanes] = (d_act * up_pre * slope).astype(BF16)

    def input_gradient(first):
        rows = pl.ds(first, 320)
        return nn(dg[rows, :], wg[...]) + nn(du[rows, :], wu[...])

    def to_mate(source, target, index):
        return pltpu.make_async_remote_copy(
            source, target, t_send.at[index], t_recv.at[index], device_id=(mate, col), device_id_type=MESH_ID
        )

    def fold_group(source, group):
        rows = pl.ds(pl.multiple_of(group * 80, 16), 80)
        tall = jnp.concatenate([source[rows, q * QUARTER : (q + 1) * QUARTER] for q in range(4)], axis=0)
        return nn(fold[...], tall).astype(BF16)

    def output_part(first, which):
        totals = []
        for i in range(2):
            rows = slice(first + i * 320, first + (i + 1) * 320)
            value = nn(act[rows, :], wd[...])
            dxs[i * 320 : (i + 1) * 320, :] = value.astype(BF16)
            totals.append(jnp.sum(value * os[rows, :].astype(F32), axis=1, keepdims=True))
        total = jnp.concatenate(totals, axis=0)

        def fold_one(group, carry):
            outs[which, block(group, 320), :] = fold_group(dxs, group)
            return carry

        lax.fori_loop(0, 8, fold_one, 0)
        wide = jnp.where(iota((640, 128), 1) == slot_of[...], total, 0.0)
        return lax.dot_general(
            row_hot[...], wide, (((0,), (0,)), ((), ())), preferred_element_type=F32, precision=highest
        )

    def part_move(i):
        rows = pl.ds(i * 320, 320)
        return to_mate(part.at[rows], arrived.at[rows], i)

    take_tokens(1, 640)
    load(x_slots, 0, 0).start()
    load(o_slots, 0, 1).start()
    for copy in weights[0]:
        copy.wait()
    hidden_half(640, 0)
    take_tokens(0, 0)
    for copy in weights[1]:
        copy.wait()
    late.wait_recv()
    hidden_half(640, 1)
    for i in range(2):
        part[i * 320 : (i + 1) * 320, :] = input_gradient(640 + i * 320).astype(BF16)
        part_move(i).start()
    hidden_half(0, 0)
    hidden_half(0, 1)
    for n in range(2):
        lanes = slice(n * 512, (n + 1) * 512)
        grad_first[:, lanes] = tn(dg[:, PADDED:], xs[:, lanes])[0:SHARD].astype(BF16)
    first_move = pltpu.make_async_remote_copy(
        grad_first, grad_mate, first_send, first_recv, device_id=(partner, col), device_id_type=MESH_ID
    )
    first_move.start()
    gate_part[...] = output_part(640, 1)
    gate_move = to_mate(gate_part, gate_arrived, 2)
    gate_move.start()
    gates = output_part(0, 0)

    def message(dest, source):
        return pltpu.make_async_remote_copy(
            stage.at[0, block(dest, FOLDED)],
            dx_back.at[block(source, FOLDED)],
            m_send.at[dest],
            m_recv.at[source],
            device_id=(row, dest),
            device_id_type=MESH_ID,
        )

    def gate_message(dest, source):
        return pltpu.make_async_remote_copy(
            gate_out.at[dest],
            dg_back.at[source],
            r_send.at[dest],
            r_recv.at[source],
            device_id=(row, dest),
            device_id_type=MESH_ID,
        )

    own_dx = pltpu.make_async_copy(stage.at[0, block(col, FOLDED)], dx_back.at[block(col, FOLDED)], own_sem.at[0])
    own_dg = pltpu.make_async_copy(gate_out.at[col], dg_back.at[col], own_sem.at[1])
    for i in range(2):
        rows = slice(i * 320, (i + 1) * 320)
        value = input_gradient(i * 320)
        part_move(i).wait_recv()
        dxs[rows, :] = (value + arrived[rows, :].astype(F32)).astype(BF16)

        def return_group(k, carry, i=i):
            group = i * 4 + lax.rem(lax.div(col, 4) + k, 4)
            stage[0, block(group, 320), :] = fold_group(dxs, group)
            for j in range(4):
                dest = group * 4 + j

                @pl.when(dest != col)
                def _():
                    message(dest, col).start()

                @pl.when(dest == col)
                def _():
                    own_dx.start()

            return carry

        lax.fori_loop(0, 4, return_group, 0)
    gate_move.wait_recv()
    gates = gates + gate_arrived[...]
    for e in range(EXPERTS):
        gate_out[e] = jnp.broadcast_to(gates[e : e + 1, :], (8, 128))

    def send_gates(step, carry):
        gate_message(lax.rem(col + step, EXPERTS), col).start()
        return carry

    lax.fori_loop(1, EXPERTS, send_gates, 0)
    own_dg.start()

    pending = {}
    turn = 0
    pairs = ((dg, xs), (du, xs), (act, dys))
    for which, half in ((1, 1), (2, 1), (0, 0), (1, 0), (2, 0)):
        left, right = pairs[which]
        for n in range(2):
            lanes = slice(n * 512, (n + 1) * 512)
            value = tn(left[:, half * PADDED : (half + 1) * PADDED], right[:, lanes])[0:SHARD]
            slot = turn % 2
            turn += 1
            if slot in pending:
                pending[slot].wait()
            if half == 0:
                grad_stage[slot] = value
                source, target = grad_stage.at[slot], grad_own.at[pl.ds(which * SHARD, SHARD), pl.ds(n * 512, 512)]
            else:
                grad_half[slot] = value.astype(BF16)
                source, target = grad_half.at[slot], grad_send.at[pl.ds((which - 1) * SHARD, SHARD), pl.ds(n * 512, 512)]
            pending[slot] = pltpu.make_async_copy(source, target, out_sem.at[slot])
            pending[slot].start()
    for copy in pending.values():
        copy.wait()

    def wait_source(step, carry):
        source = lax.rem(col + step, EXPERTS)
        message(col, source).wait_recv()
        gate_message(col, source).wait_recv()
        message(source, col).wait_send()
        gate_message(source, col).wait_send()
        return carry

    lax.fori_loop(1, EXPERTS, wait_source, 0)
    own_dx.wait()
    own_dg.wait()
    for i in range(2):
        part_move(i).wait_send()
    gate_move.wait_send()
    late.wait_send()
    first_move.wait()


def experts(x_slots, o_slots, g_slots, consts, own, other):
    def out(shape, dtype):
        return jax.ShapeDtypeStruct(shape, dtype)

    hidden = (2 * 640, 2 * PADDED)
    return pl.pallas_call(
        expert_kernel,
        out_shape=(
            out((PIECES, QUARTER), BF16),
            out((EXPERTS, 8, 128), F32),
            out((2, PIECES, QUARTER), BF16),
            out((GRAD_ROWS, WIDTH), F32),
            out((2 * SHARD, WIDTH), BF16),
            out((SHARD, WIDTH), BF16),
        ),
        in_specs=[HBM_SPEC] * 2 + [VMEM_SPEC] * 5 + [HBM_SPEC] * 6,
        out_specs=[HBM_SPEC] * 2 + [VMEM_SPEC] + [HBM_SPEC] * 3,
        scratch_shapes=[
            pltpu.VMEM((2, PIECES, QUARTER), BF16),
            pltpu.VMEM((1280, WIDTH), BF16),
            pltpu.VMEM((1280, WIDTH), BF16),
            pltpu.VMEM((1280, WIDTH), BF16),
            pltpu.VMEM((2 * PADDED, WIDTH), BF16),
            pltpu.VMEM((2 * PADDED, WIDTH), BF16),
            pltpu.VMEM((2 * PADDED, WIDTH), BF16),
            pltpu.VMEM(hidden, BF16),
            pltpu.VMEM(hidden, BF16),
            pltpu.VMEM(hidden, BF16),
            pltpu.VMEM((640, WIDTH), BF16),
            pltpu.VMEM((640, WIDTH), BF16),
            pltpu.VMEM((640, WIDTH), BF16),
            pltpu.VMEM((EXPERTS, 128), F32),
            pltpu.VMEM((EXPERTS, 128), F32),
            pltpu.VMEM((EXPERTS, 8, 128), F32),
            pltpu.VMEM((2, SHARD, 512), F32),
            pltpu.VMEM((2, SHARD, 512), BF16),
            pltpu.VMEM((SHARD, WIDTH), BF16),
            DMA((2,)),
            DMA((3, 2)),
            DMA,
            DMA,
            DMA,
            DMA,
            DMA((3,)),
            DMA((3,)),
            DMA((EXPERTS,)),
            DMA((EXPERTS,)),
            DMA((EXPERTS,)),
            DMA((EXPERTS,)),
            DMA((2,)),
            DMA((2,)),
        ],
        compiler_params=pltpu.CompilerParams(
            collective_id=2, has_side_effects=True, vmem_limit_bytes=62 * 1024 * 1024
        ),
        name="experts",
    )(x_slots, o_slots, g_slots, *consts, *own, *other)


def backward_kernel(
    long_len, short_len, tokens, cot, routes, routes_t, gain_a, gain_m, rel_bias_t, router_t, ids_t, wq, wk, wv, wo,
    resid, probs_t, rnorm_t, query, long_kv, short_kv, mixed, norm_l, norm_s, dx_back, dg_back, outs, grad_send,
    block_out, tokens_grad, grads_sum, small_sum, grad_mate,
    grads, small, total, branch, d_mixed, normed, flipped, d_query, d_kv, d_long, d_arrived, table_l, table_s, diag_l, diag_s,
    turned, out_arrived, out_sum, out_back,
    t_send, t_recv, kv_send, kv_recv, m_send, m_recv, own_sem, w_send, w_recv, *sum_refs,
):
    row = lax.axis_index("row")
    col = lax.axis_index("col")
    mate = 3 - row
    barrier = pltpu.get_barrier_semaphore()
    for step in (1, 2, 3):
        pl.semaphore_signal(barrier, inc=1, device_id=(lax.rem(row + step, 4), col), device_id_type=MESH_ID)

    def greet(step, carry):
        pl.semaphore_signal(barrier, inc=1, device_id=(row, lax.rem(col + step, EXPERTS)), device_id_type=MESH_ID)
        return carry

    lax.fori_loop(1, EXPERTS, greet, 0)
    pl.semaphore_wait(barrier, EXPERTS + 2)
    slots_end = 2 + 3 * SUM_COUNT
    sums = SumSteps(
        (grads, small), (grads_sum, small_sum), sum_refs[0:2], sum_refs[2:slots_end], sum_refs[slots_end:]
    )

    out_move = pltpu.make_async_remote_copy(
        outs.at[1], out_arrived, t_send, t_recv, device_id=(mate, col), device_id_type=MESH_ID
    )
    out_move.start()

    partner = row + 1 - 2 * lax.rem(row, 2)

    def weight_move(index):
        rows = pl.ds(sum(GRAD_PIECES[:index]), GRAD_PIECES[index])
        return pltpu.make_async_remote_copy(
            grad_send.at[rows],
            grad_mate.at[rows],
            w_send.at[index],
            w_recv.at[index],
            device_id=(partner, col),
            device_id_type=MESH_ID,
        )

    weight_move(0).start()

    def message(dest, source):
        return pltpu.make_async_remote_copy(
            out_sum.at[block(dest, FOLDED)],
            out_back.at[block(source, FOLDED)],
            m_send.at[dest],
            m_recv.at[source],
            device_id=(row, dest),
            device_id_type=MESH_ID,
        )

    own_out = pltpu.make_async_copy(out_sum.at[block(col, FOLDED)], out_back.at[block(col, FOLDED)], own_sem)

    hot_rows = [(iota((ROWS, EXPERTS), 1) == routes[:, k : k + 1]).astype(F32) for k in range(2)]
    before = (iota((ROWS, ROWS), 1) < iota((ROWS, ROWS), 0)).astype(BF16)
    earlier = nn(before, (hot_rows[0] + hot_rows[1]).astype(BF16))
    place = [
        routes[:, k : k + 1].astype(F32) * SLOTS + jnp.sum(earlier * hot_rows[k], axis=1, keepdims=True)
        for k in range(2)
    ]

    def gather_back(source):
        total[...] = jnp.zeros_like(total)

        def one(i, carry):
            here = block(i, 512)
            slot_id, quarter = ids_t[0:1, here], ids_t[1:2, here]
            match = (slot_id == place[0]) | (slot_id == place[1])
            values = source[here, :]
            for q in range(4):
                hot = jnp.where(match & (quarter == q), 1.0, 0.0).astype(BF16)
                total[:, q * QUARTER : (q + 1) * QUARTER] += nn(hot, values)
            return carry

        lax.fori_loop(0, PIECES // 512, one, 0)

    gather_back(dx_back)

    hots, both, slots, unused = route_places(routes_t[...])
    probs = probs_t[...]
    picked = [jnp.sum(probs * hot, axis=0, keepdims=True) for hot in hots]
    picked_sum = picked[0] + picked[1]
    gate_slots = jnp.concatenate([dg_back[e, 0:1, :] for e in range(EXPERTS)], axis=0)
    d_gates = [
        jnp.sum(hots[k] * nn(gate_slots, slot_hot(slots[k]), highest), axis=0, keepdims=True) for k in range(2)
    ]
    shared = (d_gates[0] * picked[0] + d_gates[1] * picked[1]) / (picked_sum * picked_sum)
    fraction = jnp.sum(both, axis=1, keepdims=True) / (2 * ROWS)
    d_probs = balance_coef * EXPERTS * fraction
    for k in range(2):
        d_probs = d_probs + (d_gates[k] / picked_sum - shared) * hots[k]
    d_logits = probs * (d_probs - jnp.sum(d_probs * probs, axis=0, keepdims=True))
    d_logits = d_logits + 2.0 * zloss_coef * rnorm_t[...] * probs

    x = resid[...]
    scale = lax.rsqrt(jnp.mean(x * x, axis=1, keepdims=True) + norm_eps)
    router_grad = nn(d_logits, x * scale * gain_m[...], highest)
    small[...] = jnp.zeros_like(small)
    for i in range(8):
        small[i * 32 : (i + 1) * 32, :] = router_grad[:, i * 128 : (i + 1) * 128]
    d_normed = total[...] + nn(d_logits.T, router_t[...], highest)
    gain_grad = jnp.sum(d_normed * (x * scale), axis=0, keepdims=True)
    for i in range(8):
        small[264 + i : 265 + i, :] = gain_grad[:, i * 128 : (i + 1) * 128]
    d_normed = d_normed * gain_m[...]
    shrink = jnp.mean(d_normed * x, axis=1, keepdims=True)
    d_resid = cot[...].astype(F32) + scale * d_normed - x * (scale * scale * scale * shrink)
    tokens_grad[...] = d_resid
    branch[...] = d_resid.astype(BF16)

    def flip(source):
        def one(i, carry):
            flipped[block(i, 128), :] = source[:, block(i, 128)].T
            return carry

        lax.fori_loop(0, 8, one, 0)

    def weight_gradient(which, value_of):
        def one(n, carry):
            out = nn(flipped[...], value_of(n)).astype(BF16)
            first = lax.div(n, 2) * SUM_ROWS[0] + which * 4096 + lax.rem(n, 2) * 2048
            grads[pl.ds(pl.multiple_of(first, 1024), 1024), :] = out[:, 0:128]
            grads[pl.ds(pl.multiple_of(first + 1024, 1024), 1024), :] = out[:, 128:256]
            return carry

        lax.fori_loop(0, 4, one, 0)

    flip(mixed)
    weight_gradient(0, lambda n: branch[:, block(n, 256)])
    sums.swap(0)

    def back_mixed(n, carry):
        rows = block(n, 256)
        d_mixed[:, rows] = nt(branch[...], wo[rows, :]).astype(BF16)
        return carry

    lax.fori_loop(0, 4, back_mixed, 0)

    sums.hop(0, 0)

    place_l = iota((1, TABLE), 1)
    place_l = jnp.where(place_l < 512, place_l, place_l - TABLE) - row * LONG
    place_s = iota((1, 256), 1)
    place_s = jnp.where(place_s < 128, place_s, place_s - 256)
    table_l[...] = nn(rel_bias_t[...], bucket_hot(place_l), highest)
    table_s[...] = nn(rel_bias_t[...], bucket_hot(place_s), highest)
    turned[...] = (iota((128, 128), 0) + iota((128, 128), 1) == 127).astype(BF16)
    lane = iota((1, 128), 1)

    def attend_back(first, keys_of, store_kv, table, diag, keep, count, width, norm_in):
        def one_pair(pair, carry):
            lanes = block(pair, 128)
            values = pl.ds(pl.multiple_of(pair * 128 + WIDTH, 128), 128)
            q2 = query[first : first + 128, lanes]
            m2 = d_mixed[first : first + 128, lanes]
            k2, v2 = keys_of(lanes), keys_of(values)
            d_k = jnp.zeros((count, 128), F32)
            d_v = jnp.zeros((count, 128), F32)
            d_q = []
            for side in range(2):
                head = pair * 2 + side
                here = (lane >= 64) if side else (lane < 64)
                q1 = jnp.where(here, q2, jnp.zeros_like(q2))
                m1 = jnp.where(here, m2, jnp.zeros_like(m2))
                norm = jnp.sum(jnp.where(lane == head, norm_in[...], 0.0), axis=1, keepdims=True)
                bias = pltpu.roll(
                    jnp.broadcast_to(table[pl.ds(head, 1), :], (128, width)), 0, 1, stride=1, stride_axis=0
                )[:, :count]
                scores = jnp.where(keep, nt(q1, k2) * 0.125 + bias, masked_score)
                probs = jnp.exp(scores - norm)
                d_probs = nt(m1, v2)
                shift = jnp.sum(probs * d_probs, axis=1, keepdims=True)
                d_scores = (probs * (d_probs - shift)).astype(BF16)
                d_v = d_v + tn(probs.astype(BF16), m1)
                d_k = d_k + tn(d_scores, q1)
                d_q.append(nn(d_scores, k2))
                reverse = nn(turned[...], d_scores)
                reverse = jnp.concatenate([reverse, jnp.zeros((128, width - count), F32)], axis=1)
                reverse = pltpu.roll(reverse, 0, 1, stride=1, stride_axis=0)
                diag[pl.ds(head, 1), :] = jnp.sum(reverse, axis=0, keepdims=True)
            d_query[first : first + 128, lanes] = (jnp.where(lane < 64, d_q[0], d_q[1]) * 0.125).astype(BF16)
            store_kv(lanes, d_k * 0.125)
            store_kv(values, d_v)
            return carry

        lax.fori_loop(0, HEADS // 2, one_pair, 0)

    def store_long(lanes, value):
        d_long[:, :, lanes] = value.astype(BF16).reshape(4, LONG, 128)

    def store_short(lanes, value):
        d_kv[LONG:, lanes] = value.astype(BF16)

    attend_back(
        0,
        lambda lanes: long_kv[:, :, lanes].reshape(512, 128),
        store_long,
        table_l,
        diag_l,
        iota((1, 512), 1) < long_len[0],
        512,
        TABLE,
        norm_l,
    )

    def kv_move(step):
        dest = lax.rem(row + step, 4)
        return pltpu.make_async_remote_copy(
            d_long.at[dest],
            d_arrived.at[step - 1],
            kv_send.at[step - 1],
            kv_recv.at[step - 1],
            device_id=(dest, col),
            device_id_type=MESH_ID,
        )

    for step in (1, 2, 3):
        kv_move(step).start()
    weight_move(1).start()
    sums.hop(0, 1)

    out_move.wait_recv()

    def return_group(i, carry):
        group = lax.rem(lax.div(col, 4) + i, 8)
        rows = block(group, 320)
        out_sum[rows, :] = (outs[0, rows, :].astype(F32) + out_arrived[rows, :].astype(F32)).astype(BF16)
        for j in range(4):
            dest = group * 4 + j

            @pl.when(dest != col)
            def _():
                message(dest, col).start()

            @pl.when(dest == col)
            def _():
                own_out.start()

        return carry

    lax.fori_loop(0, 8, return_group, 0)

    attend_back(
        LONG,
        lambda lanes: short_kv[:, lanes],
        store_short,
        table_s,
        diag_s,
        iota((1, 128), 1) < short_len[0],
        128,
        256,
        norm_s,
    )
    sums.hop(0, 2)
    weight_move(2).start()
    back_l = bucket_hot(iota((1, TABLE), 1) - 127 - row * LONG)
    back_s = bucket_hot(iota((1, 256), 1) - 127)
    small[272:288, 0:32] = nt(diag_l[...], back_l, highest) + nt(diag_s[...], back_s, highest)

    def norm_rows(i, carry):
        rows = block(i, 64)
        x = tokens[rows, :].astype(F32)
        scale = lax.rsqrt(jnp.mean(x * x, axis=1, keepdims=True) + norm_eps)
        normed[rows, :] = (x * scale * gain_a[...]).astype(BF16)
        return carry

    lax.fori_loop(0, 4, norm_rows, 0)
    flip(normed)
    weight_gradient(1, lambda n: d_query[:, block(n, 256)])
    sums.swap(1)
    sums.gather(0, 2)
    weight_move(3).start()
    for step in (1, 2, 3):
        kv_move(step).wait()

    def add_kv(i, carry):
        lanes = block(i, 256)
        value = d_long[row, :, lanes].astype(F32)
        for step in range(3):
            value = value + d_arrived[step, :, lanes].astype(F32)
        d_kv[0:LONG, lanes] = value.astype(BF16)
        return carry

    lax.fori_loop(0, 8, add_kv, 0)
    sums.hop(1, 0)
    weight_gradient(2, lambda n: d_kv[:, block(n, 256)])
    weight_gradient(3, lambda n: d_kv[:, pl.ds(pl.multiple_of(n * 256 + WIDTH, 256), 256)])
    for part in (2, 3, 4):
        sums.swap(part)
    sums.gather(0, 1)

    def back_normed(n, carry):
        rows = block(n, 256)
        value = nt(d_query[...], wq[rows, :]) + nt(d_kv[:, 0:WIDTH], wk[rows, :])
        total[:, rows] = value + nt(d_kv[:, WIDTH:], wv[rows, :])
        return carry

    lax.fori_loop(0, 4, back_normed, 0)
    for part in (2, 3, 4):
        sums.hop(part, 0)
    weight_move(4).start()
    sums.hop(1, 1)
    x = tokens[...].astype(F32)
    scale = lax.rsqrt(jnp.mean(x * x, axis=1, keepdims=True) + norm_eps)
    d_normed = total[...]
    gain_grad = jnp.sum(d_normed * (x * scale), axis=0, keepdims=True)
    for i in range(8):
        small[256 + i : 257 + i, :] = gain_grad[:, i * 128 : (i + 1) * 128]
    d_normed = d_normed * gain_a[...]
    shrink = jnp.mean(d_normed * x, axis=1, keepdims=True)
    tokens_grad[...] = tokens_grad[...] + scale * d_normed - x * (scale * scale * scale * shrink)

    sums.gather(0, 0)
    sums.hop(1, 2)

    def wait_source(step, carry):
        source = lax.rem(col + step, EXPERTS)
        message(col, source).wait_recv()
        message(source, col).wait_send()
        return carry

    lax.fori_loop(1, EXPERTS, wait_source, 0)
    own_out.wait()
    out_move.wait_send()
    total[...] = jnp.zeros_like(total)
    gates = [picked[k] / picked_sum for k in range(2)]
    gates = [jnp.broadcast_to(gate, (128, ROWS)).T[:, 0:1] for gate in gates]

    def combine(i, carry):
        here = block(i, 512)
        slot_id, quarter = ids_t[0:1, here], ids_t[1:2, here]
        weight = jnp.where(slot_id == place[0], gates[0], 0.0) + jnp.where(slot_id == place[1], gates[1], 0.0)
        high = weight.astype(BF16)
        rest = (weight - high.astype(F32)).astype(BF16)
        values = out_back[here, :]
        for q in range(4):
            here_q = quarter == q
            part = nn(jnp.where(here_q, high, jnp.zeros_like(high)), values)
            part = part + nn(jnp.where(here_q, rest, jnp.zeros_like(rest)), values)
            total[:, q * QUARTER : (q + 1) * QUARTER] += part
        return carry

    lax.fori_loop(0, PIECES // 512, combine, 0)
    branch_m = total[...]
    live = live_column(long_len[0], short_len[0], row)
    resid_now = resid[...]
    result = resid_now + branch_m
    block_out[...] = result
    branch_a = resid_now - tokens[...].astype(F32)
    tallies = [
        jnp.sum(live * jnp.sum(field * field, axis=1, keepdims=True), axis=0, keepdims=True)
        for field in (result, branch_a, branch_m)
    ]
    tallies.append(jnp.sum(live, axis=0, keepdims=True))
    packed = jnp.zeros((8, 128), F32)
    for i, tally in enumerate(tallies):
        packed = jnp.where(iota((8, 128), 1) == i, tally, packed)
    small[288:296, :] = packed
    sums.swap(5)

    for part in (2, 3, 4):
        sums.hop(part, 1)
    sums.gather(1, 2)
    sums.hop(5, 0)
    sums.last(0)
    for part in (2, 3, 4):
        sums.hop(part, 2)
    sums.gather(1, 1)
    sums.hop(5, 1)
    for part in (2, 3, 4):
        sums.gather(part, 2)
    sums.gather(1, 0)
    sums.hop(5, 2)
    for part in (2, 3, 4):
        sums.gather(part, 1)
    sums.last(1)
    sums.gather(5, 2)
    for part in (2, 3, 4):
        sums.gather(part, 0)
    sums.gather(5, 1)
    for part in (2, 3, 4):
        sums.last(part)
    sums.gather(5, 0)
    sums.last(5)
    for part in range(SUM_COUNT):
        sums.end(part)
    for index in range(len(GRAD_PIECES)):
        weight_move(index).wait()


def backward(*args):
    def out(shape, dtype):
        return jax.ShapeDtypeStruct(shape, dtype)

    return pl.pallas_call(
        backward_kernel,
        out_shape=(
            out((ROWS, WIDTH), F32),
            out((ROWS, WIDTH), F32),
            out((2 * SUM_ROWS[0], 128), BF16),
            out((2 * SUM_ROWS[1], 128), F32),
            out((2 * SHARD, WIDTH), BF16),
        ),
        in_specs=[SMEM_SPEC] * 2 + [VMEM_SPEC] * (len(args) - 3) + [HBM_SPEC],
        out_specs=[VMEM_SPEC] * 2 + [HBM_SPEC] * 3,
        scratch_shapes=[
            pltpu.VMEM((2 * SUM_ROWS[0], 128), BF16),
            pltpu.VMEM((2 * SUM_ROWS[1], 128), F32),
            pltpu.VMEM((ROWS, WIDTH), F32),
            pltpu.VMEM((ROWS, WIDTH), BF16),
            pltpu.VMEM((ROWS, WIDTH), BF16),
            pltpu.VMEM((ROWS, WIDTH), BF16),
            pltpu.VMEM((WIDTH, ROWS), BF16),
            pltpu.VMEM((ROWS, WIDTH), BF16),
            pltpu.VMEM((ROWS, 2 * WIDTH), BF16),
            pltpu.VMEM((4, LONG, 2 * WIDTH), BF16),
            pltpu.VMEM((3, LONG, 2 * WIDTH), BF16),
            pltpu.VMEM((HEADS, TABLE), F32),
            pltpu.VMEM((HEADS, 256), F32),
            pltpu.VMEM((HEADS, TABLE), F32),
            pltpu.VMEM((HEADS, 256), F32),
            pltpu.VMEM((128, 128), BF16),
            pltpu.VMEM((PIECES, QUARTER), BF16),
            pltpu.VMEM((PIECES, QUARTER), BF16),
            pltpu.VMEM((PIECES, QUARTER), BF16),
            DMA,
            DMA,
            DMA((3,)),
            DMA((3,)),
            DMA((EXPERTS,)),
            DMA((EXPERTS,)),
            DMA,
            DMA((len(GRAD_PIECES),)),
            DMA((len(GRAD_PIECES),)),
        ]
        + sum_scratch(),
        compiler_params=pltpu.CompilerParams(
            collective_id=3, has_side_effects=True, vmem_limit_bytes=60 * 1024 * 1024
        ),
        name="backward_and_sums",
    )(*args)


def per_device(
    tokens_in, out_cot, long_lengths, short_lengths, routes, gain_attn, w_query, w_key, w_value, w_out, rel_bias,
    gain_moe, router, w_gate, w_up, w_down,
):
    own = (jnp.swapaxes(w_gate[0], 0, 1), jnp.swapaxes(w_up[0], 0, 1), w_down[0])
    routes_t = jnp.swapaxes(routes, 0, 1)
    router_t = jnp.swapaxes(router, 0, 1)
    rel_bias_t = jnp.swapaxes(rel_bias, 0, 1)
    gain_a, gain_m = gain_attn.reshape(1, WIDTH), gain_moe.reshape(1, WIDTH)
    ids = piece_ids()
    sent = forward(
        long_lengths, short_lengths, tokens_in, out_cot, routes_t, gain_a, gain_m, rel_bias_t, router_t,
        jnp.asarray(ids.T), w_query, w_key, w_value, w_out, *own,
    )
    x_slots, o_slots, g_slots, *other = sent[:6]
    query, long_kv, short_kv, mixed, norm_l, norm_s, resid, probs_t, rnorm_t = sent[6:]
    unfold = unfold_matrix()
    row_of = np.arange(640) // SLOTS
    consts = (
        jnp.asarray(unfold, BF16),
        jnp.asarray(unfold.T, BF16),
        jnp.asarray((row_of[:, None] == np.arange(EXPERTS)[None, :]).astype(np.float32)),
        jnp.asarray((np.arange(640) % SLOTS).astype(np.int32)[:, None]),
    )
    dx_back, dg_back, outs, grad_own, grad_send, grad_early = experts(x_slots, o_slots, g_slots, consts, own, other)
    block_out, tokens_grad, grads, small, grad_late = backward(
        long_lengths, short_lengths, tokens_in, out_cot, routes, routes_t, gain_a, gain_m, rel_bias_t, router_t,
        jnp.asarray(ids), w_query, w_key, w_value, w_out, resid, probs_t, rnorm_t, query, long_kv, short_kv, mixed,
        norm_l, norm_s, dx_back, dg_back, outs, grad_send,
    )
    grads = finish_sums(grads)
    expert_grads = finish_experts(grad_own, grad_early, grad_late)
    totals = small[288]
    statistics = jnp.sqrt(totals[0:3] / (totals[3] * WIDTH))
    router_grad = small[0:256].reshape(8, EXPERTS, 128).transpose(1, 0, 2).reshape(EXPERTS, WIDTH)
    return (
        block_out,
        tokens_grad,
        small[256:264].reshape(WIDTH),
        grads[1],
        grads[2],
        grads[3],
        grads[0],
        jnp.swapaxes(small[272:288, 0:32], 0, 1),
        small[264:272].reshape(WIDTH),
        jnp.swapaxes(router_grad, 0, 1),
        jnp.swapaxes(expert_grads[0], 0, 1)[None],
        jnp.swapaxes(expert_grads[1], 0, 1)[None],
        expert_grads[2][None],
        statistics,
    )


def solution(mesh):
    tokens = P(("row", "col"), None)
    whole = P()
    wide = P("col", None, "row")
    tall = P("col", "row", None)
    return jax.shard_map(
        per_device,
        mesh=mesh,
        in_specs=(tokens, tokens, P("col"), P(("row", "col")), tokens) + (whole,) * 8 + (wide, wide, tall),
        out_specs=(tokens, tokens) + (whole,) * 8 + (wide, wide, tall, whole),
        check_vma=False,
    )
```

```python
import functools

import numpy as np
import jax
import jax.numpy as jnp
from jax import lax
from jax.experimental import pallas as pl
from jax.experimental.pallas import tpu as pltpu
from jax.sharding import PartitionSpec as P

HEADS = 16
HEAD_DIM = 64
WIDTH = 1024
ROWS = 256
LONG = 128
EXPERTS = 32
SLOTS = 20
FOLDED = 80
QUARTER = 256
PIECES = EXPERTS * FOLDED
TABLE = 640
SHARD = 704
PADDED = 768
EARLY_DOWN = 352
FIRST_DOWN = 176
FIRST_GATE = 352
GRAD_ROWS = 3 * SHARD
GRAD_PIECES = (320, 160, 160, 160, 160, 448)

bucket_edges = (1, 2, 3, 4, 5, 6, 7, 8, 12, 16, 23, 32, 46, 64, 91)
norm_eps = 1e-06
balance_coef = 0.01
zloss_coef = 0.001
masked_score = -1e30
highest = lax.Precision.HIGHEST
MESH_ID = pl.DeviceIdType.MESH
F32 = jnp.float32
BF16 = jnp.bfloat16
VMEM_SPEC = pl.BlockSpec(memory_space=pltpu.VMEM)
HBM_SPEC = pl.BlockSpec(memory_space=pl.ANY)
SMEM_SPEC = pl.BlockSpec(memory_space=pltpu.SMEM)
DMA = pltpu.SemaphoreType.DMA


def piece_ids():
    row = np.arange(PIECES)
    slot = (row // FOLDED) * SLOTS + row % SLOTS
    quarter = (row % FOLDED) // SLOTS
    return np.stack([slot, quarter]).astype(np.float32)


def unfold_matrix():
    out = np.arange(320)
    quarter, message, slot = out // 80, (out % 80) // SLOTS, out % SLOTS
    hot = np.zeros((320, 320), np.float32)
    hot[out, message * FOLDED + quarter * SLOTS + slot] = 1
    return hot


def nt(left, right, precision=None):
    return lax.dot_general(
        left, right, (((1,), (1,)), ((), ())), preferred_element_type=F32, precision=precision
    )


def tn(left, right):
    return lax.dot_general(left, right, (((0,), (0,)), ((), ())), preferred_element_type=F32)


def nn(left, right, precision=None):
    return jnp.dot(left, right, preferred_element_type=F32, precision=precision)


def iota(shape, dim):
    return lax.broadcasted_iota(jnp.int32, shape, dim)


def block(index, size):
    return pl.ds(pl.multiple_of(index * size, size), size)


def bucket_hot(relative):
    magnitude = jnp.abs(relative)
    level = jnp.zeros_like(relative)
    for edge in bucket_edges:
        level = level + (magnitude >= edge).astype(jnp.int32)
    level = level + jnp.where(relative > 0, len(bucket_edges) + 1, 0)
    return (iota((32, relative.shape[1]), 0) == level).astype(F32)


def route_places(routes_t):
    hots = [(iota((EXPERTS, ROWS), 0) == routes_t[k : k + 1, :]).astype(F32) for k in range(2)]
    both = hots[0] + hots[1]
    before = (iota((ROWS, ROWS), 0) < iota((ROWS, ROWS), 1)).astype(BF16)
    earlier = nn(both.astype(BF16), before)
    slots = [jnp.sum(earlier * hot, axis=0, keepdims=True) for hot in hots]
    places = [routes_t[k : k + 1, :].astype(F32) * SLOTS + slots[k] for k in range(2)]
    return hots, both, slots, places


def slot_hot(slots_row):
    return (iota((128, ROWS), 0).astype(F32) == slots_row).astype(F32)


def live_column(long_len, short_len, row):
    position = iota((ROWS, 1), 0)
    is_long = position < LONG
    here = jnp.where(is_long, position + row * LONG, position - LONG)
    limit = jnp.where(is_long, long_len, short_len)
    return (here < limit).astype(F32)


SUM_PARTS = (
    (4096, 0, ("x", "z", "y"), 0),
    (512, 0, ("z", "x", "y"), 1),
)
SUM_ROWS = (4096, 512)
SUM_COUNT = len(SUM_PARTS)


def torus_place():
    row = lax.axis_index("row")
    col = lax.axis_index("col")
    return row, lax.div(col, 8), lax.rem(lax.div(col, 2), 4), lax.rem(col, 2)


def axis_peer(axis, step):
    row, z, x, core = torus_place()
    if axis == "y":
        row = lax.rem(row + step, 4)
    elif axis == "x":
        x = lax.rem(x + step, 4)
    elif axis == "z":
        z = lax.rem(z + step, 4)
    else:
        core = 1 - core
    return (row, (z * 4 + x) * 2 + core)


class SumSteps:
    def __init__(self, sources, results, other, slots, sems):
        self.sources, self.results, self.other, self.slots = sources, results, other, slots
        (
            self.core_send, self.core_recv, self.hop_send, self.hop_recv, self.gather_send, self.gather_recv,
            self.copy_sem, self.last_send, self.last_recv,
        ) = sems
        row, z, x, self.core = torus_place()
        self.place = {"x": x, "y": row, "z": z}
        self.flight = {}

    def base(self, p, levels):
        rows, first, order, kind = SUM_PARTS[p]
        base = self.core * SUM_ROWS[kind] + first
        for done in range(levels):
            base = base + self.place[order[done]] * (rows // 4 ** (done + 1))
        return base

    def at(self, kind, start, rows):
        return pl.ds(pl.multiple_of(start, 8 if kind else 16), rows)

    def add(self, kind, start, rows, terms):
        if kind:
            tile = min(rows, 128)
        else:
            tile = next(t for t in (512, 384, 256, 192, 128, 64, 48, 32) if rows % t == 0)
        source = self.sources[kind]

        def body(i, carry):
            here = self.at(kind, start + i * tile, tile)
            total = source[here, :].astype(F32)
            for ref, first in terms:
                total = total + ref[self.at(kind, first + i * tile, tile), :].astype(F32)
            source[here, :] = total.astype(source.dtype)
            return carry

        lax.fori_loop(0, rows // tile, body, 0)

    def swap(self, p):
        rows, first, order, kind = SUM_PARTS[p]
        theirs = (1 - self.core) * SUM_ROWS[kind] + first
        move = pltpu.make_async_remote_copy(
            self.sources[kind].at[self.at(kind, theirs, rows)],
            self.other[kind].at[pl.ds(first, rows)],
            self.core_send.at[p],
            self.core_recv.at[p],
            device_id=axis_peer("core", 1),
            device_id_type=MESH_ID,
        )
        move.start()
        self.flight[p] = [move]

    def hop(self, p, level):
        rows, first, order, kind = SUM_PARTS[p]
        for move in self.flight[p]:
            move.wait()
        if level == 0:
            self.add(kind, self.base(p, 0), rows, [(self.other[kind], first)])
        else:
            self.end_hop(p, level - 1)
        size = rows // 4 ** (level + 1)
        axis = order[level]
        self.flight[p] = []
        for step in (1, 2, 3):
            block_of = lax.rem(self.place[axis] + step, 4)
            move = pltpu.make_async_remote_copy(
                self.sources[kind].at[self.at(kind, self.base(p, level) + block_of * size, size)],
                self.slots[p * 3 + level].at[pl.ds((step - 1) * size, size)],
                self.hop_send.at[p, level, step - 1],
                self.hop_recv.at[p, level, step - 1],
                device_id=axis_peer(axis, step),
                device_id_type=MESH_ID,
            )
            move.start()
            self.flight[p].append(move)

    def end_hop(self, p, level):
        rows, first, order, kind = SUM_PARTS[p]
        size = rows // 4 ** (level + 1)
        slots = self.slots[p * 3 + level]
        self.add(kind, self.base(p, level + 1), size, [(slots, step * size) for step in range(3)])

    def gather(self, p, level):
        rows, first, order, kind = SUM_PARTS[p]
        for move in self.flight[p]:
            move.wait()
        if level == 2:
            self.end_hop(p, 2)
        here = self.at(kind, self.base(p, level + 1), rows // 4 ** (level + 1))
        source = self.sources[kind].at[here] if level == 2 else self.results[kind].at[here]
        target = self.results[kind].at[here]
        self.flight[p] = []
        for step in (1, 2, 3):
            move = pltpu.make_async_remote_copy(
                source,
                target,
                self.gather_send.at[p, level, step - 1],
                self.gather_recv.at[p, level, step - 1],
                device_id=axis_peer(order[level], step),
                device_id_type=MESH_ID,
            )
            move.start()
            self.flight[p].append(move)
        if level == 2:
            keep = pltpu.make_async_copy(source, target, self.copy_sem.at[p])
            keep.start()
            self.flight[p].append(keep)

    def last(self, p):
        rows, first, order, kind = SUM_PARTS[p]
        size = rows // 4
        moves = []
        for index in range(4):
            if index > 0:
                self.flight[p][index - 1].wait()
            block_of = lax.rem(self.place[order[0]] + 4 - index, 4)
            here = self.results[kind].at[self.at(kind, self.base(p, 0) + block_of * size, size)]
            move = pltpu.make_async_remote_copy(
                here,
                here,
                self.last_send.at[p, index],
                self.last_recv.at[p, index],
                device_id=axis_peer("core", 1),
                device_id_type=MESH_ID,
            )
            move.start()
            moves.append(move)
        self.flight[p] = moves

    def end(self, p):
        for move in self.flight[p]:
            move.wait()


HEAD_ROWS = 3 * WIDTH
HEAD_ORDERS = (("x", "z"), ("z", "x"), ("x", "z"))


class HeadSums:
    def __init__(self, source, result, other, slots, sems):
        self.source, self.result, self.other, self.slots = source, result, other, slots
        (
            self.core_send, self.core_recv, self.hop_send, self.hop_recv, self.gather_send, self.gather_recv,
            self.copy_sem, self.last_send, self.last_recv,
        ) = sems
        self.row, z, x, self.core = torus_place()
        self.place = {"x": x, "y": self.row, "z": z}
        self.flight = {}

    def base(self, p, levels):
        base = self.core * HEAD_ROWS + p * WIDTH
        for done in range(levels):
            base = base + self.place[HEAD_ORDERS[p][done]] * (WIDTH // 4 ** (done + 1))
        return base

    def at(self, start, rows):
        return pl.ds(pl.multiple_of(start, 16), rows)

    def wait(self, p):
        for move in self.flight[p]:
            move.wait()

    def add(self, start, rows, terms):
        tile = min(rows, 256)

        def body(i, carry):
            here = self.at(start + i * tile, tile)
            total = self.source[here, :].astype(F32)
            for ref, first in terms:
                total = total + ref[self.at(first + i * tile, tile), :].astype(F32)
            self.source[here, :] = total.astype(BF16)
            return carry

        lax.fori_loop(0, rows // tile, body, 0)

    def send(self, p, moves, axis, send, recv, sems):
        self.flight[p] = []
        for step, (source, target) in zip((1, 2, 3), moves):
            move = pltpu.make_async_remote_copy(
                source,
                target,
                send.at[(*sems, step - 1)],
                recv.at[(*sems, step - 1)],
                device_id=axis_peer(axis, step),
                device_id_type=MESH_ID,
            )
            move.start()
            self.flight[p].append(move)

    def swap(self, p):
        move = pltpu.make_async_remote_copy(
            self.source.at[self.at((1 - self.core) * HEAD_ROWS + p * WIDTH, WIDTH)],
            self.other.at[pl.ds(p * WIDTH, WIDTH)],
            self.core_send.at[p],
            self.core_recv.at[p],
            device_id=axis_peer("core", 1),
            device_id_type=MESH_ID,
        )
        move.start()
        self.flight[p] = [move]

    def hop(self, p, level):
        self.wait(p)
        if level == 0:
            self.add(self.base(p, 0), WIDTH, [(self.other, p * WIDTH)])
        else:
            self.end_hop(p, level - 1)
        size = WIDTH // 4 ** (level + 1)
        axis = HEAD_ORDERS[p][level]
        moves = []
        for step in (1, 2, 3):
            block_of = lax.rem(self.place[axis] + step, 4)
            moves.append(
                (
                    self.source.at[self.at(self.base(p, level) + block_of * size, size)],
                    self.slots[p * 2 + level].at[pl.ds((step - 1) * size, size)],
                )
            )
        self.send(p, moves, axis, self.hop_send, self.hop_recv, (p, level))

    def end_hop(self, p, level):
        size = WIDTH // 4 ** (level + 1)
        slots = self.slots[p * 2 + level]
        self.add(self.base(p, level + 1), size, [(slots, step * size) for step in range(3)])

    def gather(self, p, turn):
        self.wait(p)
        row_last = p == 2
        if turn == 0:
            self.end_hop(p, 1)
        levels = (2, 1, 0) if row_last else (2, 2, 1)
        base = self.base(p, levels[turn])
        here = self.at(base, WIDTH // 4 ** levels[turn])
        if row_last:
            axis = (HEAD_ORDERS[p][1], HEAD_ORDERS[p][0], "y")[turn]
        else:
            axis = ("y", HEAD_ORDERS[p][1], HEAD_ORDERS[p][0])[turn]
        whole = turn > 0 and not row_last
        target = self.result.at[:, here] if whole else self.result.at[self.row, here]
        source = self.source.at[here] if turn == 0 else target
        self.send(p, [(source, target)] * 3, axis, self.gather_send, self.gather_recv, (p, turn))
        if turn == 0:
            keep = pltpu.make_async_copy(source, target, self.copy_sem.at[p])
            keep.start()
            self.flight[p].append(keep)

    def last(self, p):
        moves = []
        for index in range(4):
            if index > 0:
                self.flight[p][index - 1].wait()
            if p == 2:
                here = self.result.at[lax.rem(self.row + 4 - index, 4), self.at(self.base(p, 0), WIDTH)]
            else:
                size = WIDTH // 4
                block_of = lax.rem(self.place[HEAD_ORDERS[p][0]] + 4 - index, 4)
                here = self.result.at[:, self.at(self.base(p, 0) + block_of * size, size)]
            move = pltpu.make_async_remote_copy(
                here,
                here,
                self.last_send.at[p, index],
                self.last_recv.at[p, index],
                device_id=axis_peer("core", 1),
                device_id_type=MESH_ID,
            )
            move.start()
            moves.append(move)
        self.flight[p] = moves


def head_scratch():
    scratch = [pltpu.VMEM((HEAD_ROWS, 128), BF16)]
    for p in range(3):
        scratch += [pltpu.VMEM((3 * WIDTH // 4, 128), BF16), pltpu.VMEM((3 * WIDTH // 16, 128), BF16)]
    shapes = [(3,)] * 2 + [(3, 2, 3)] * 2 + [(3, 3, 3)] * 2 + [(3,)] + [(3, 4)] * 2
    return scratch + [DMA(shape) for shape in shapes]


def sum_scratch():
    scratch = [
        pltpu.VMEM((SUM_ROWS[0], 128), BF16),
        pltpu.VMEM((SUM_ROWS[1], 128), F32),
    ]
    for rows, first, order, kind in SUM_PARTS:
        for level in range(3):
            scratch.append(pltpu.VMEM((3 * rows // 4 ** (level + 1), 128), F32 if kind else BF16))
    shapes = [(SUM_COUNT,)] * 2 + [(SUM_COUNT, 3, 3)] * 4 + [(SUM_COUNT,)] + [(SUM_COUNT, 4)] * 2
    return scratch + [DMA(shape) for shape in shapes]


def finish(out_grads, head_grads, small, last, own, early, late):
    steps = 4
    sum_tile, expert_tile = WIDTH // steps, SHARD // steps

    def kernel(out_ref, head_ref, small_ref, last_ref, own_ref, early_ref, late_ref, *results):
        for i in range(8):
            lanes = slice(i * 128, (i + 1) * 128)
            results[0][:, lanes] = out_ref[i // 4, i % 4].astype(F32)
            for which in range(3):
                results[1 + which][:, lanes] = head_ref[i // 2, i % 2, which].astype(F32)
        for which, result in enumerate(results[4:7]):
            part = early_ref[...] if which == 0 else late_ref[which - 1]
            result[...] = own_ref[which] + part.astype(F32)
        gain_a, gain_m, bias, router, statistics = results[7:]

        @pl.when(pl.program_id(0) == 0)
        def _():
            for i in range(8):
                router[:, i * 128 : (i + 1) * 128] = small_ref[i * 32 : (i + 1) * 32, :]
            gain_a[...] = last_ref[0:8, :]
            gain_m[...] = small_ref[264:272, :]
            bias[...] = small_ref[272:288, 0:32]
            totals = last_ref[8:9, :]
            count = jnp.sum(jnp.where(iota((1, 128), 1) == 3, totals, 0.0), axis=1, keepdims=True)
            statistics[...] = jnp.sqrt(totals / (count * WIDTH))

    def whole(shape):
        return pl.BlockSpec(shape, lambda i: (0,) * len(shape))

    def rows(tile):
        return pl.BlockSpec((tile, WIDTH), lambda i: (i, 0))

    small_shapes = ((8, 128), (8, 128), (HEADS, 32), (EXPERTS, WIDTH), (1, 128))
    return pl.pallas_call(
        kernel,
        grid=(steps,),
        out_shape=(jax.ShapeDtypeStruct((WIDTH, WIDTH), F32),) * 4
        + (jax.ShapeDtypeStruct((SHARD, WIDTH), F32),) * 3
        + tuple(jax.ShapeDtypeStruct(shape, F32) for shape in small_shapes),
        in_specs=[
            pl.BlockSpec((2, 4, sum_tile, 128), lambda i: (0, 0, i, 0)),
            pl.BlockSpec((4, 2, 3, sum_tile, 128), lambda i: (0, 0, 0, i, 0)),
            whole((288, 128)),
            whole((16, 128)),
            pl.BlockSpec((3, expert_tile, WIDTH), lambda i: (0, i, 0)),
            rows(expert_tile),
            pl.BlockSpec((2, expert_tile, WIDTH), lambda i: (0, i, 0)),
        ],
        out_specs=(rows(sum_tile),) * 4 + (rows(expert_tile),) * 3 + tuple(whole(shape) for shape in small_shapes),
        compiler_params=pltpu.CompilerParams(vmem_limit_bytes=62 * 1024 * 1024),
        name="finish",
    )(
        out_grads.reshape(2, 4, WIDTH, 128),
        head_grads.reshape(4, 2, 3, WIDTH, 128),
        small,
        last,
        own.reshape(3, SHARD, WIDTH),
        early,
        late.reshape(2, SHARD, WIDTH),
    )


def forward_kernel(
    long_len, short_len, tokens, cot, routes_t, gain_a, gain_m, rel_bias_t, router_t, ids, wq, wk, wv, wo, wg_own, wu_own, wd_own,
    x_slots, o_slots, g_slots, wg_mate, wu_mate, wd_mate, normed_a, heads_in, short_qkv, mixed, norm_l, norm_s, resid, probs_t, rnorm_t,
    normed, heads_out, mix_out, buffer_o, buffer_x, gate_out, table_l, table_s,
    o_send, o_recv, x_send, x_recv, g_send, g_recv, own_sem, h_send, h_recv, mix_send, mix_recv, t_send, t_recv, w_send, w_recv,
):
    row = lax.axis_index("row")
    col = lax.axis_index("col")
    mate = 3 - row
    barrier = pltpu.get_barrier_semaphore()
    for step in (1, 2, 3):
        pl.semaphore_signal(barrier, inc=1, device_id=(lax.rem(row + step, 4), col), device_id_type=MESH_ID)

    def greet(step, carry):
        pl.semaphore_signal(barrier, inc=1, device_id=(row, lax.rem(col + step, EXPERTS)), device_id_type=MESH_ID)
        return carry

    lax.fori_loop(1, EXPERTS, greet, 0)

    hots, both, slots, places = route_places(routes_t[...])

    def message(buffer, slots_ref, send, recv, dest, source):
        return pltpu.make_async_remote_copy(
            buffer.at[block(dest, FOLDED)],
            slots_ref.at[0, block(source, FOLDED)],
            send.at[dest],
            recv.at[source],
            device_id=(row, dest),
            device_id_type=MESH_ID,
        )

    def dispatch(source, buffer, slots_ref, send, recv, own):
        def one_group(i, carry):
            group = lax.rem(lax.div(col, 4) + i, 8)
            rows = block(group, 320)
            slot_id = ids[rows, 0:1]
            quarter = ids[rows, 1:2]
            match = (slot_id == places[0]) | (slot_id == places[1])
            total = jnp.zeros((320, QUARTER), F32)
            for q in range(4):
                hot = jnp.where(match & (quarter == q), 1.0, 0.0).astype(BF16)
                total = total + nn(hot, source[:, q * QUARTER : (q + 1) * QUARTER])
            buffer[rows, :] = total.astype(BF16)
            for j in range(4):
                dest = group * 4 + j

                @pl.when(dest != col)
                def _():
                    message(buffer, slots_ref, send, recv, dest, col).start()

                @pl.when(dest == col)
                def _():
                    pltpu.make_async_copy(
                        buffer.at[block(dest, FOLDED)], slots_ref.at[0, block(dest, FOLDED)], own
                    ).start()

            return carry

        lax.fori_loop(0, 8, one_group, 0, unroll=2)

    def wait_source(buffer, slots_ref, send, recv, own, source):
        @pl.when(source != col)
        def _():
            message(buffer, slots_ref, send, recv, col, source).wait_recv()

        @pl.when(source == col)
        def _():
            pltpu.make_async_copy(
                buffer.at[block(col, FOLDED)], slots_ref.at[0, block(col, FOLDED)], own
            ).wait()

    def wait_sends(buffer, slots_ref, send, recv):
        def one(step, carry):
            message(buffer, slots_ref, send, recv, lax.rem(col + step, EXPERTS), col).wait_send()
            return carry

        lax.fori_loop(1, EXPERTS, one, 0)

    pl.semaphore_wait(barrier, EXPERTS + 2)

    partner = row + 1 - 2 * lax.rem(row, 2)
    weight_moves = []
    for own, target, first, last in (
        (wd_own, wd_mate, 0, FIRST_DOWN),
        (wg_own, wg_mate, 0, FIRST_GATE),
        (wg_own, wg_mate, FIRST_GATE, SHARD),
        (wu_own, wu_mate, 0, SHARD),
        (wd_own, wd_mate, FIRST_DOWN, EARLY_DOWN),
    ):
        rows = pl.ds(first, last - first)
        i = len(weight_moves)
        weight_moves.append(
            pltpu.make_async_remote_copy(
                own.at[rows], target.at[rows], w_send.at[i], w_recv.at[i], device_id=(partner, col),
                device_id_type=MESH_ID,
            )
        )
    weight_moves[0].start()

    def norm_rows(i, carry):
        rows = block(i, 64)
        x = tokens[rows, :].astype(F32)
        scale = lax.rsqrt(jnp.mean(x * x, axis=1, keepdims=True) + norm_eps)
        normed_a[rows, :] = (x * scale * gain_a[...]).astype(BF16)
        return carry

    lax.fori_loop(0, 4, norm_rows, 0, unroll=4)

    def heads_move(step):
        dest = lax.rem(row + step, 4)
        return pltpu.make_async_remote_copy(
            heads_out.at[dest],
            heads_in.at[row],
            h_send.at[step - 1],
            h_recv.at[step - 1],
            device_id=(dest, col),
            device_id_type=MESH_ID,
        )

    def heads_arrival(step):
        source = lax.rem(row + 4 - step, 4)
        return pltpu.make_async_remote_copy(
            heads_out.at[source],
            heads_in.at[source],
            h_send.at[step - 1],
            h_recv.at[step - 1],
            device_id=(source, col),
            device_id_type=MESH_ID,
        )

    for step in (1, 2, 3, 0):
        dest = lax.rem(row + step, 4)
        lanes = block(dest, 256)
        for which, weight in enumerate((wq, wk, wv)):
            part = nn(normed_a[...], weight[:, lanes]).astype(BF16)
            here = slice(which * 256, (which + 1) * 256)
            if step == 0:
                heads_in[row, :, here] = part[:LONG]
            else:
                heads_out[dest, :, here] = part[:LONG]
            short_qkv[:, pl.ds(pl.multiple_of(dest * 256 + which * WIDTH, 256), 256)] = part[LONG:]
        if step > 0:
            heads_move(step).start()
    weight_moves[1].start()

    dispatch(cot, buffer_o, o_slots, o_send, o_recv, own_sem.at[0])

    place_s = iota((1, 256), 1)
    place_s = jnp.where(place_s < 128, place_s, place_s - 256)
    table_s[...] = nn(rel_bias_t[...], bucket_hot(place_s), highest)
    place_l = iota((1, TABLE), 1)
    place_l = jnp.where(place_l < 512, place_l, place_l - TABLE)
    for part in range(4):
        table_l[part] = nn(rel_bias_t[...], bucket_hot(place_l - part * LONG), highest)

    lane = iota((1, 128), 1)

    def attend(q2, k2, v2, bias_row, keep, count, width):
        bias = pltpu.roll(jnp.broadcast_to(bias_row, (128, width)), 0, 1, stride=1, stride_axis=0)[:, :count]
        scores = jnp.where(keep, nt(q2, k2) * 0.125 + bias, masked_score)
        row_max = jnp.max(scores, axis=1, keepdims=True)
        terms = jnp.exp(scores - row_max)
        total = jnp.sum(terms, axis=1, keepdims=True)
        return nn((terms / total).astype(BF16), v2), row_max + jnp.log(total)

    def attend_pair(q2, k2, v2, bias_row_of, keep, count, width, first, norms):
        outs = []
        for side in range(2):
            here = (lane >= 64) if side else (lane < 64)
            out, norm = attend(
                jnp.where(here, q2, jnp.zeros_like(q2)), k2, v2, bias_row_of(side), keep, count, width
            )
            outs.append(out)
            norms = jnp.where(lane == first + side, norm, norms)
        return jnp.where(lane < 64, outs[0], outs[1]).astype(BF16), norms

    norm_s[...] = jnp.zeros_like(norm_s)

    def short_pair(pair, carry):
        q2, k2, v2 = (
            short_qkv[:, pl.ds(pl.multiple_of(pair * 128 + which * WIDTH, 128), 128)] for which in range(3)
        )
        out, norms = attend_pair(
            q2, k2, v2, lambda side: table_s[pl.ds(pair * 2 + side, 1), :], iota((1, 128), 1) < short_len[0], 128, 256,
            pair * 2, norm_s[...],
        )
        mixed[LONG:, block(pair, 128)] = out
        norm_s[...] = norms
        return carry

    lax.fori_loop(0, HEADS // 2, short_pair, 0, unroll=2)

    def to_mate(source, target, index):
        return pltpu.make_async_remote_copy(
            source, target, t_send.at[index], t_recv.at[index], device_id=(mate, col), device_id_type=MESH_ID
        )

    def o_move(group):
        rows = block(group, 320)
        return to_mate(o_slots.at[0, rows], o_slots.at[1, rows], 9 + group)

    def forward_o(i, carry):
        group = lax.rem(lax.div(col, 4) + 8 - i, 8)
        for j in range(4):
            wait_source(buffer_o, o_slots, o_send, o_recv, own_sem.at[0], group * 4 + j)
        o_move(group).start()
        return carry

    lax.fori_loop(0, 4, forward_o, 0)

    for step in (1, 2, 3):
        heads_arrival(step).wait_recv()

    def mix_move(step, dest):
        return pltpu.make_async_remote_copy(
            mix_out.at[dest],
            mixed.at[pl.ds(0, LONG), block(row, 256)],
            mix_send.at[step - 1],
            mix_recv.at[step - 1],
            device_id=(dest, col),
            device_id_type=MESH_ID,
        )

    def mix_arrival(step):
        source = lax.rem(row + 4 - step, 4)
        return pltpu.make_async_remote_copy(
            mix_out.at[source],
            mixed.at[pl.ds(0, LONG), block(source, 256)],
            mix_send.at[step - 1],
            mix_recv.at[step - 1],
            device_id=(source, col),
            device_id_type=MESH_ID,
        )

    def long_part(step, carry):
        part = lax.rem(row + step, 4)
        norms = jnp.zeros((128, 128), F32)
        outs = []
        for pair in range(2):
            here = slice(pair * 128, (pair + 1) * 128)
            q2 = heads_in[part, :, here]
            k2 = heads_in[:, :, 256 + pair * 128 : 384 + pair * 128].reshape(512, 128)
            v2 = heads_in[:, :, 512 + pair * 128 : 640 + pair * 128].reshape(512, 128)
            out, norms = attend_pair(
                q2, k2, v2, lambda side, pair=pair: table_l[part, pl.ds(row * 4 + pair * 2 + side, 1), :],
                iota((1, 512), 1) < long_len[0], 512, TABLE, pair * 2, norms,
            )
            outs.append(out)
        norm_l[part] = norms
        mix_out[part] = jnp.concatenate(outs, axis=1)
        return carry

    def long_and_send(step, carry):
        long_part(step, carry)
        mix_move(step, lax.rem(row + step, 4)).start()
        return carry

    lax.fori_loop(1, 4, long_and_send, 0)
    long_part(0, 0)
    mixed[0:LONG, block(row, 256)] = mix_out[row]
    for move in weight_moves[2:]:
        move.start()

    lax.fori_loop(4, 8, forward_o, 0)

    for step in (1, 2, 3):
        mix_arrival(step).wait_recv()

    def project_out(i, carry):
        lanes = block(i, 256)
        resid[:, lanes] = tokens[:, lanes].astype(F32) + nn(mixed[...], wo[:, lanes])
        return carry

    lax.fori_loop(0, 4, project_out, 0, unroll=4)

    def norm_again(i, carry):
        rows = block(i, 64)
        x = resid[rows, :]
        scale = lax.rsqrt(jnp.mean(x * x, axis=1, keepdims=True) + norm_eps)
        normed[rows, :] = (x * scale * gain_m[...]).astype(BF16)
        return carry

    lax.fori_loop(0, 4, norm_again, 0, unroll=4)
    dispatch(normed, buffer_x, x_slots, x_send, x_recv, own_sem.at[1])

    x = resid[...]
    scale = lax.rsqrt(jnp.mean(x * x, axis=1, keepdims=True) + norm_eps)
    logits = nt(router_t[...], x * scale * gain_m[...], highest)
    row_max = jnp.max(logits, axis=0, keepdims=True)
    terms = jnp.exp(logits - row_max)
    total = jnp.sum(terms, axis=0, keepdims=True)
    probs = terms / total
    probs_t[...] = probs
    rnorm_t[...] = row_max + jnp.log(total)
    picked = [jnp.sum(probs * hot, axis=0, keepdims=True) for hot in hots]
    picked_sum = picked[0] + picked[1]
    gate_slots = jnp.zeros((EXPERTS, 128), F32)
    for k in range(2):
        gate_slots = gate_slots + nt(hots[k] * (picked[k] / picked_sum), slot_hot(slots[k]), highest)
    for e in range(EXPERTS):
        gate_out[e] = jnp.broadcast_to(gate_slots[e : e + 1, :], (8, 128))

    def gate_message(dest, source):
        return pltpu.make_async_remote_copy(
            gate_out.at[dest],
            g_slots.at[0, source],
            g_send.at[dest],
            g_recv.at[source],
            device_id=(row, dest),
            device_id_type=MESH_ID,
        )

    def send_gates(step, carry):
        gate_message(lax.rem(col + step, EXPERTS), col).start()
        return carry

    lax.fori_loop(1, EXPERTS, send_gates, 0)
    own_gates = pltpu.make_async_copy(gate_out.at[col], g_slots.at[0, col], own_sem.at[2])
    own_gates.start()

    def x_move(group):
        rows = block(group, 320)
        return to_mate(x_slots.at[0, rows], x_slots.at[1, rows], group)

    def forward_x(i, carry):
        group = lax.rem(lax.div(col, 4) + 8 - i, 8)
        for j in range(4):
            wait_source(buffer_x, x_slots, x_send, x_recv, own_sem.at[1], group * 4 + j)
        x_move(group).start()
        return carry

    lax.fori_loop(0, 8, forward_x, 0)

    def wait_gates(step, carry):
        gate_message(col, lax.rem(col + step, EXPERTS)).wait_recv()
        return carry

    lax.fori_loop(1, EXPERTS, wait_gates, 0)
    own_gates.wait()
    g_move = to_mate(g_slots.at[0], g_slots.at[1], 8)
    g_move.start()

    for step in (1, 2, 3):
        heads_move(step).wait_send()
        mix_move(step, lax.rem(row + step, 4)).wait_send()
    wait_sends(buffer_o, o_slots, o_send, o_recv)
    wait_sends(buffer_x, x_slots, x_send, x_recv)

    def wait_gate_sends(step, carry):
        gate_message(lax.rem(col + step, EXPERTS), col).wait_send()
        return carry

    lax.fori_loop(1, EXPERTS, wait_gate_sends, 0)

    def wait_o(group, carry):
        o_move(group).wait()
        return carry

    lax.fori_loop(0, 8, wait_o, 0)

    def wait_x(group, carry):
        x_move(group).wait()
        return carry

    lax.fori_loop(0, 8, wait_x, 0)
    g_move.wait()
    for move in weight_moves:
        move.wait()


def forward(long_lengths, short_lengths, tokens, cot, routes_t, gain_a, gain_m, rel_bias_t, router_t, ids, wq, wk, wv, wo, wg, wu, wd):
    def out(shape, dtype):
        return jax.ShapeDtypeStruct(shape, dtype)

    return pl.pallas_call(
        forward_kernel,
        out_shape=(
            out((2, PIECES, QUARTER), BF16),
            out((2, PIECES, QUARTER), BF16),
            out((2, EXPERTS, 8, 128), F32),
            out((SHARD, WIDTH), BF16),
            out((SHARD, WIDTH), BF16),
            out((EARLY_DOWN, WIDTH), BF16),
            out((ROWS, WIDTH), BF16),
            out((4, LONG, 768), BF16),
            out((LONG, 3 * WIDTH), BF16),
            out((ROWS, WIDTH), BF16),
            out((4, 128, 128), F32),
            out((128, 128), F32),
            out((ROWS, WIDTH), F32),
            out((EXPERTS, ROWS), F32),
            out((1, ROWS), F32),
        ),
        in_specs=[SMEM_SPEC] * 2 + [VMEM_SPEC] * 12 + [HBM_SPEC] * 3,
        out_specs=[HBM_SPEC] * 6 + [VMEM_SPEC] * 9,
        scratch_shapes=[
            pltpu.VMEM((ROWS, WIDTH), BF16),
            pltpu.VMEM((4, LONG, 768), BF16),
            pltpu.VMEM((4, LONG, 256), BF16),
            pltpu.VMEM((PIECES, QUARTER), BF16),
            pltpu.VMEM((PIECES, QUARTER), BF16),
            pltpu.VMEM((EXPERTS, 8, 128), F32),
            pltpu.VMEM((4, HEADS, TABLE), F32),
            pltpu.VMEM((HEADS, 256), F32),
            DMA((EXPERTS,)),
            DMA((EXPERTS,)),
            DMA((EXPERTS,)),
            DMA((EXPERTS,)),
            DMA((EXPERTS,)),
            DMA((EXPERTS,)),
            DMA((3,)),
            DMA((3,)),
            DMA((3,)),
            DMA((3,)),
            DMA((3,)),
            DMA((17,)),
            DMA((17,)),
            DMA((5,)),
            DMA((5,)),
        ],
        compiler_params=pltpu.CompilerParams(
            collective_id=1, has_side_effects=True, vmem_limit_bytes=56 * 1024 * 1024
        ),
        name="forward_and_dispatch",
    )(
        long_lengths, short_lengths, tokens, cot, routes_t, gain_a, gain_m, rel_bias_t, router_t, ids, wq, wk, wv, wo,
        wg, wu, wd,
    )


def expert_kernel(
    x_slots, o_slots, g_slots, unfold, fold, row_hot, slot_of, wg_own, wu_own, wd_own, wg_mate, wu_mate, wd_mate, normed_a,
    dx_back, dg_back, outs, out_first, normed_all, grad_own, grad_send, grad_mate,
    stage, xs, os, dys, wg, wu, wd, act, dg, du, part, arrived, dxs, gate_part, gate_arrived, gate_out, grad_stage,
    grad_half, grad_first, stage_sem, weight_sem, late_send, late_recv, first_send, first_recv, t_send, t_recv, m_send, m_recv, r_send, r_recv, n_send, n_recv, own_sem,
    out_sem,
):
    row = lax.axis_index("row")
    col = lax.axis_index("col")
    mate = 3 - row
    partner = row + 1 - 2 * lax.rem(row, 2)
    barrier = pltpu.get_barrier_semaphore()
    for step in (1, 2, 3):
        pl.semaphore_signal(barrier, inc=1, device_id=(lax.rem(row + step, 4), col), device_id_type=MESH_ID)

    def greet(step, carry):
        pl.semaphore_signal(barrier, inc=1, device_id=(row, lax.rem(col + step, EXPERTS)), device_id_type=MESH_ID)
        return carry

    lax.fori_loop(1, EXPERTS, greet, 0)

    def load(source, which, index):
        return pltpu.make_async_copy(source.at[which], stage.at[index], stage_sem.at[index])

    load(x_slots, 1, 0).start()
    load(o_slots, 1, 1).start()
    weights = [[], []]
    for j, sources in enumerate(((wg_own, wu_own, wd_own), (wg_mate, wu_mate, wd_mate))):
        for i, (source, held) in enumerate(zip(sources, (wg, wu, wd))):
            copy = pltpu.make_async_copy(
                source, held.at[pl.ds(j * PADDED, source.shape[0])], weight_sem.at[i, j]
            )
            copy.start()
            weights[j].append(copy)
    for held in (wg, wu, wd):
        for j in range(2):
            held[j * PADDED + SHARD : (j + 1) * PADDED, :] = jnp.zeros((PADDED - SHARD, WIDTH), BF16)
    pl.semaphore_wait(barrier, EXPERTS + 2)
    late = pltpu.make_async_remote_copy(
        wd_own.at[pl.ds(EARLY_DOWN, SHARD - EARLY_DOWN)],
        wd.at[pl.ds(PADDED + EARLY_DOWN, SHARD - EARLY_DOWN)],
        late_send,
        late_recv,
        device_id=(partner, col),
        device_id_type=MESH_ID,
    )
    late.start()

    def rows_move(index, dest, of_row):
        source = normed_a if index < 2 else normed_all.at[of_row]
        return pltpu.make_async_remote_copy(
            source,
            normed_all.at[of_row],
            n_send.at[index],
            n_recv.at[index],
            device_id=(dest, col),
            device_id_type=MESH_ID,
        )

    rows_move(0, mate, row).start()
    rows_move(1, partner, row).start()
    own_rows = pltpu.make_async_copy(normed_a, normed_all.at[row], own_sem.at[2])
    own_rows.start()

    def spread(index, target, first):
        def one(group, carry):
            wide = nn(unfold[...], stage[index, block(group, 320), :]).astype(BF16)
            rows = pl.ds(pl.multiple_of(first + group * 80, 16), 80)
            for q in range(4):
                target[rows, q * QUARTER : (q + 1) * QUARTER] = wide[q * 80 : (q + 1) * 80]
            return carry

        lax.fori_loop(0, 8, one, 0, unroll=4)

    def gate_column(which):
        gates = jnp.concatenate([g_slots[which, e, 0:1, :] for e in range(EXPERTS)], axis=0)
        wide = nn(row_hot[...], gates, highest)
        lanes = iota((640, 128), 1)
        return jnp.sum(jnp.where(lanes == slot_of[...], wide, 0.0), axis=1, keepdims=True)

    def take_tokens(which, first):
        load(x_slots, which, 0).wait()
        spread(0, xs, first)
        load(o_slots, which, 1).wait()
        spread(1, os, first)
        rows = pl.ds(first, 640)
        dys[rows, :] = (os[rows, :].astype(F32) * gate_column(which)).astype(BF16)

    def hidden_half(first, half, before_down=None):
        lanes = slice(half * PADDED, (half + 1) * PADDED)
        rows = slice(first, first + 640)
        gate_pre = nt(xs[rows, :], wg[lanes, :])
        up_pre = nt(xs[rows, :], wu[lanes, :])
        if before_down is not None:
            before_down()
        d_act = nt(dys[rows, :], wd[lanes, :])
        square = gate_pre * gate_pre
        bend = jnp.tanh(0.7978845608028654 * gate_pre * (1.0 + 0.044715 * square))
        level = 0.5 * (1.0 + bend)
        gelu = gate_pre * level
        slope = level + 0.5 * gate_pre * (1.0 - bend * bend) * (
            0.7978845608028654 * (1.0 + 3.0 * 0.044715 * square)
        )
        act[rows, lanes] = (gelu * up_pre).astype(BF16)
        du[rows, lanes] = (d_act * gelu).astype(BF16)
        dg[rows, lanes] = (d_act * up_pre * slope).astype(BF16)

    def input_gradient(first):
        rows = pl.ds(first, 320)
        return nn(dg[rows, :], wg[...]) + nn(du[rows, :], wu[...])

    def to_mate(source, target, index):
        return pltpu.make_async_remote_copy(
            source, target, t_send.at[index], t_recv.at[index], device_id=(mate, col), device_id_type=MESH_ID
        )

    def fold_group(source, group):
        rows = pl.ds(pl.multiple_of(group * 80, 16), 80)
        tall = jnp.concatenate([source[rows, q * QUARTER : (q + 1) * QUARTER] for q in range(4)], axis=0)
        return nn(fold[...], tall).astype(BF16)

    def output_part(first, which):
        totals = []
        for i in range(2):
            rows = slice(first + i * 320, first + (i + 1) * 320)
            value = nn(act[rows, :], wd[...])
            dxs[i * 320 : (i + 1) * 320, :] = value.astype(BF16)
            totals.append(jnp.sum(value * os[rows, :].astype(F32), axis=1, keepdims=True))
        total = jnp.concatenate(totals, axis=0)

        def fold_one(group, carry):
            outs[which, block(group, 320), :] = fold_group(dxs, group)
            return carry

        lax.fori_loop(0, 8, fold_one, 0, unroll=4)
        wide = jnp.where(iota((640, 128), 1) == slot_of[...], total, 0.0)
        return lax.dot_general(
            row_hot[...], wide, (((0,), (0,)), ((), ())), preferred_element_type=F32, precision=highest
        )

    def part_move(i):
        rows = pl.ds(i * 320, 320)
        return to_mate(part.at[rows], arrived.at[rows], i)

    take_tokens(1, 640)
    load(x_slots, 0, 0).start()
    load(o_slots, 0, 1).start()
    for copy in weights[0]:
        copy.wait()
    hidden_half(640, 0)
    take_tokens(0, 0)
    for copy in weights[1]:
        copy.wait()
    rows_move(0, mate, mate).wait_recv()
    rows_move(2, partner, mate).start()
    hidden_half(640, 1, late.wait_recv)
    for i in range(2):
        part[i * 320 : (i + 1) * 320, :] = input_gradient(640 + i * 320).astype(BF16)
        part_move(i).start()
    hidden_half(0, 0)
    hidden_half(0, 1)
    for n in range(2):
        lanes = slice(n * 512, (n + 1) * 512)
        grad_first[:, lanes] = tn(dg[:, PADDED:], xs[:, lanes])[0:SHARD].astype(BF16)
    first_move = pltpu.make_async_remote_copy(
        grad_first, grad_mate, first_send, first_recv, device_id=(partner, col), device_id_type=MESH_ID
    )
    first_move.start()
    gate_part[...] = output_part(640, 1)
    gate_move = to_mate(gate_part, gate_arrived, 2)
    gate_move.start()
    out_move = to_mate(outs.at[1, pl.ds(0, PIECES // 2)], out_first, 3)
    out_move.start()
    gates = output_part(0, 0)

    def message(dest, source):
        return pltpu.make_async_remote_copy(
            stage.at[0, block(dest, FOLDED)],
            dx_back.at[block(source, FOLDED)],
            m_send.at[dest],
            m_recv.at[source],
            device_id=(row, dest),
            device_id_type=MESH_ID,
        )

    def gate_message(dest, source):
        return pltpu.make_async_remote_copy(
            gate_out.at[dest],
            dg_back.at[source],
            r_send.at[dest],
            r_recv.at[source],
            device_id=(row, dest),
            device_id_type=MESH_ID,
        )

    own_dx = pltpu.make_async_copy(stage.at[0, block(col, FOLDED)], dx_back.at[block(col, FOLDED)], own_sem.at[0])
    own_dg = pltpu.make_async_copy(gate_out.at[col], dg_back.at[col], own_sem.at[1])
    for i in range(2):
        rows = slice(i * 320, (i + 1) * 320)
        value = input_gradient(i * 320)
        part_move(i).wait_recv()
        dxs[rows, :] = (value + arrived[rows, :].astype(F32)).astype(BF16)

        def return_group(k, carry, i=i):
            group = i * 4 + lax.rem(lax.div(col, 4) + k, 4)
            stage[0, block(group, 320), :] = fold_group(dxs, group)
            for j in range(4):
                dest = group * 4 + j

                @pl.when(dest != col)
                def _():
                    message(dest, col).start()

                @pl.when(dest == col)
                def _():
                    own_dx.start()

            return carry

        lax.fori_loop(0, 4, return_group, 0, unroll=2)
    gate_move.wait_recv()
    gates = gates + gate_arrived[...]
    for e in range(EXPERTS):
        gate_out[e] = jnp.broadcast_to(gates[e : e + 1, :], (8, 128))

    def send_gates(step, carry):
        gate_message(lax.rem(col + step, EXPERTS), col).start()
        return carry

    lax.fori_loop(1, EXPERTS, send_gates, 0)
    own_dg.start()

    pending = {}
    turn = 0
    pairs = ((dg, xs), (du, xs), (act, dys))
    for which, half in ((1, 1), (2, 1), (0, 0), (1, 0), (2, 0)):
        left, right = pairs[which]
        for n in range(2):
            lanes = slice(n * 512, (n + 1) * 512)
            value = tn(left[:, half * PADDED : (half + 1) * PADDED], right[:, lanes])[0:SHARD]
            slot = turn % 2
            turn += 1
            if slot in pending:
                pending[slot].wait()
            if half == 0:
                grad_stage[slot] = value
                source, target = grad_stage.at[slot], grad_own.at[pl.ds(which * SHARD, SHARD), pl.ds(n * 512, 512)]
            else:
                grad_half[slot] = value.astype(BF16)
                source, target = grad_half.at[slot], grad_send.at[pl.ds((which - 1) * SHARD, SHARD), pl.ds(n * 512, 512)]
            pending[slot] = pltpu.make_async_copy(source, target, out_sem.at[slot])
            pending[slot].start()
    for copy in pending.values():
        copy.wait()

    def wait_source(step, carry):
        source = lax.rem(col + step, EXPERTS)
        message(col, source).wait_recv()
        gate_message(col, source).wait_recv()
        message(source, col).wait_send()
        gate_message(source, col).wait_send()
        return carry

    lax.fori_loop(1, EXPERTS, wait_source, 0)
    own_dx.wait()
    own_dg.wait()
    for i in range(2):
        part_move(i).wait_send()
    gate_move.wait_send()
    out_move.wait()
    rows_move(0, mate, row).wait_send()
    rows_move(1, partner, partner).wait()
    rows_move(2, partner, 3 - partner).wait()
    own_rows.wait()
    late.wait_send()
    first_move.wait()


def experts(x_slots, o_slots, g_slots, consts, own, other, normed_a):
    def out(shape, dtype):
        return jax.ShapeDtypeStruct(shape, dtype)

    hidden = (2 * 640, 2 * PADDED)
    return pl.pallas_call(
        expert_kernel,
        out_shape=(
            out((PIECES, QUARTER), BF16),
            out((EXPERTS, 8, 128), F32),
            out((2, PIECES, QUARTER), BF16),
            out((PIECES // 2, QUARTER), BF16),
            out((4, ROWS, WIDTH), BF16),
            out((GRAD_ROWS, WIDTH), F32),
            out((2 * SHARD, WIDTH), BF16),
            out((SHARD, WIDTH), BF16),
        ),
        in_specs=[HBM_SPEC] * 2 + [VMEM_SPEC] * 5 + [HBM_SPEC] * 7,
        out_specs=[HBM_SPEC] * 2 + [VMEM_SPEC] + [HBM_SPEC] * 5,
        scratch_shapes=[
            pltpu.VMEM((2, PIECES, QUARTER), BF16),
            pltpu.VMEM((1280, WIDTH), BF16),
            pltpu.VMEM((1280, WIDTH), BF16),
            pltpu.VMEM((1280, WIDTH), BF16),
            pltpu.VMEM((2 * PADDED, WIDTH), BF16),
            pltpu.VMEM((2 * PADDED, WIDTH), BF16),
            pltpu.VMEM((2 * PADDED, WIDTH), BF16),
            pltpu.VMEM(hidden, BF16),
            pltpu.VMEM(hidden, BF16),
            pltpu.VMEM(hidden, BF16),
            pltpu.VMEM((640, WIDTH), BF16),
            pltpu.VMEM((640, WIDTH), BF16),
            pltpu.VMEM((640, WIDTH), BF16),
            pltpu.VMEM((EXPERTS, 128), F32),
            pltpu.VMEM((EXPERTS, 128), F32),
            pltpu.VMEM((EXPERTS, 8, 128), F32),
            pltpu.VMEM((2, SHARD, 512), F32),
            pltpu.VMEM((2, SHARD, 512), BF16),
            pltpu.VMEM((SHARD, WIDTH), BF16),
            DMA((2,)),
            DMA((3, 2)),
            DMA,
            DMA,
            DMA,
            DMA,
            DMA((4,)),
            DMA((4,)),
            DMA((EXPERTS,)),
            DMA((EXPERTS,)),
            DMA((EXPERTS,)),
            DMA((EXPERTS,)),
            DMA((3,)),
            DMA((3,)),
            DMA((3,)),
            DMA((2,)),
        ],
        compiler_params=pltpu.CompilerParams(
            collective_id=2, has_side_effects=True, vmem_limit_bytes=62 * 1024 * 1024
        ),
        name="experts",
    )(x_slots, o_slots, g_slots, *consts, *own, *other, normed_a)


def backward_kernel(
    long_len, short_len, tokens, cot, routes_t, gain_a, gain_m, rel_bias_t, router_t, ids_t, wq, wk, wv, wo,
    resid, probs_t, rnorm_t, heads_in, short_qkv, mixed, norm_l, norm_s, dx_back, dg_back, outs, out_first, normed_all, grad_send,
    block_out, tokens_grad, last_sum, out_grads_sum, head_grads_sum, small_sum, grad_mate,
    out_grads, head_grads, small, total, branch, d_mixed, mix_out, mix_in, flipped, normed_t, d_qkv, d_heads, mix_short, d_arrived,
    d_key, d_value,
    table_l, table_s, diag_l, diag_s,
    turned, out_arrived, out_sum, out_back, last_own, last_col, last_row,
    t_send, t_recv, mix_send, mix_recv, h_send, h_recv, s_send, s_recv, m_send, m_recv, own_sem, w_send, w_recv, c_send, c_recv, r_send, r_recv, *sum_refs,
):
    row = lax.axis_index("row")
    col = lax.axis_index("col")
    mate = 3 - row
    barrier = pltpu.get_barrier_semaphore()
    for step in (1, 2, 3):
        pl.semaphore_signal(barrier, inc=1, device_id=(lax.rem(row + step, 4), col), device_id_type=MESH_ID)

    def greet(step, carry):
        pl.semaphore_signal(barrier, inc=1, device_id=(row, lax.rem(col + step, EXPERTS)), device_id_type=MESH_ID)
        return carry

    lax.fori_loop(1, EXPERTS, greet, 0)
    pl.semaphore_wait(barrier, EXPERTS + 2)
    slots_end = 2 + 3 * SUM_COUNT
    sums = SumSteps(
        (out_grads, small),
        (out_grads_sum, small_sum),
        sum_refs[0:2],
        sum_refs[2:slots_end],
        sum_refs[slots_end : slots_end + 9],
    )
    head_refs = sum_refs[slots_end + 9 :]
    heads = HeadSums(head_grads, head_grads_sum, head_refs[0], head_refs[1:7], head_refs[7:])

    out_move = pltpu.make_async_remote_copy(
        outs.at[1, pl.ds(PIECES // 2, PIECES // 2)], out_arrived, t_send, t_recv, device_id=(mate, col), device_id_type=MESH_ID
    )
    out_move.start()

    partner = row + 1 - 2 * lax.rem(row, 2)

    def weight_move(index):
        rows = pl.ds(sum(GRAD_PIECES[:index]), GRAD_PIECES[index])
        return pltpu.make_async_remote_copy(
            grad_send.at[rows],
            grad_mate.at[rows],
            w_send.at[index],
            w_recv.at[index],
            device_id=(partner, col),
            device_id_type=MESH_ID,
        )

    weight_move(0).start()

    def message(dest, source):
        return pltpu.make_async_remote_copy(
            out_sum.at[block(dest, FOLDED)],
            out_back.at[block(source, FOLDED)],
            m_send.at[dest],
            m_recv.at[source],
            device_id=(row, dest),
            device_id_type=MESH_ID,
        )

    own_out = pltpu.make_async_copy(out_sum.at[block(col, FOLDED)], out_back.at[block(col, FOLDED)], own_sem)

    def return_half(half, arrived):
        def one(i, carry):
            group = lax.rem(lax.div(col, 4) + i, 4)
            rows = block(half * 4 + group, 320)
            out_sum[rows, :] = (outs[0, rows, :].astype(F32) + arrived[block(group, 320), :].astype(F32)).astype(BF16)
            for j in range(4):
                dest = half * 16 + group * 4 + j

                @pl.when(dest != col)
                def _():
                    message(dest, col).start()

                @pl.when(dest == col)
                def _():
                    own_out.start()

            return carry

        lax.fori_loop(0, 4, one, 0)

    return_half(0, out_first)

    hots, both, slots, place_rows = route_places(routes_t[...])

    def column(value):
        return jnp.broadcast_to(value, (128, ROWS)).T[:, 0:1]

    place = [column(value) for value in place_rows]

    def gather_back(source):
        total[...] = jnp.zeros_like(total)

        def one(i, carry):
            here = block(i, 512)
            slot_id, quarter = ids_t[0:1, here], ids_t[1:2, here]
            match = (slot_id == place[0]) | (slot_id == place[1])
            values = source[here, :]
            for q in range(4):
                hot = jnp.where(match & (quarter == q), 1.0, 0.0).astype(BF16)
                total[:, q * QUARTER : (q + 1) * QUARTER] += nn(hot, values)
            return carry

        lax.fori_loop(0, PIECES // 512, one, 0, unroll=5)

    gather_back(dx_back)

    probs = probs_t[...]
    picked = [jnp.sum(probs * hot, axis=0, keepdims=True) for hot in hots]
    picked_sum = picked[0] + picked[1]
    gate_slots = jnp.concatenate([dg_back[e, 0:1, :] for e in range(EXPERTS)], axis=0)
    d_gates = [
        jnp.sum(hots[k] * nn(gate_slots, slot_hot(slots[k]), highest), axis=0, keepdims=True) for k in range(2)
    ]
    shared = (d_gates[0] * picked[0] + d_gates[1] * picked[1]) / (picked_sum * picked_sum)
    fraction = jnp.sum(both, axis=1, keepdims=True) / (2 * ROWS)
    d_probs = balance_coef * EXPERTS * fraction
    for k in range(2):
        d_probs = d_probs + (d_gates[k] / picked_sum - shared) * hots[k]
    d_logits = probs * (d_probs - jnp.sum(d_probs * probs, axis=0, keepdims=True))
    d_logits = d_logits + 2.0 * zloss_coef * rnorm_t[...] * probs

    x = resid[...]
    scale = lax.rsqrt(jnp.mean(x * x, axis=1, keepdims=True) + norm_eps)
    router_grad = nn(d_logits, x * scale * gain_m[...], highest)
    small[...] = jnp.zeros_like(small)
    for i in range(8):
        small[i * 32 : (i + 1) * 32, :] = router_grad[:, i * 128 : (i + 1) * 128]
    d_normed = total[...] + nn(d_logits.T, router_t[...], highest)
    gain_grad = jnp.sum(d_normed * (x * scale), axis=0, keepdims=True)
    for i in range(8):
        small[264 + i : 265 + i, :] = gain_grad[:, i * 128 : (i + 1) * 128]
    d_normed = d_normed * gain_m[...]
    shrink = jnp.mean(d_normed * x, axis=1, keepdims=True)
    d_resid = cot[...].astype(F32) + scale * d_normed - x * (scale * scale * scale * shrink)
    tokens_grad[...] = d_resid
    branch[...] = d_resid.astype(BF16)

    def flip(source, target, first):
        def one(i, carry):
            target[block(i, 128), first : first + ROWS] = source[:, block(i, 128)].T
            return carry

        lax.fori_loop(0, 8, one, 0, unroll=4)

    def mix_move(step, dest):
        return pltpu.make_async_remote_copy(
            mix_out.at[dest],
            mix_in.at[row],
            mix_send.at[step - 1],
            mix_recv.at[step - 1],
            device_id=(dest, col),
            device_id_type=MESH_ID,
        )

    def mix_arrival(step):
        source = lax.rem(row + 4 - step, 4)
        return pltpu.make_async_remote_copy(
            mix_out.at[source],
            mix_in.at[source],
            mix_send.at[step - 1],
            mix_recv.at[step - 1],
            device_id=(source, col),
            device_id_type=MESH_ID,
        )

    for step in (1, 2, 3, 0):
        dest = lax.rem(row + step, 4)
        value = nt(branch[...], wo[block(dest, 256), :]).astype(BF16)
        d_mixed[:, block(dest, 256)] = value[LONG:]
        if step == 0:
            mix_in[row] = value[:LONG]
        else:
            mix_out[dest] = value[:LONG]
            mix_move(step, dest).start()
    weight_move(1).start()

    flip(mixed, flipped, 0)

    def out_gradient(n, carry):
        out = nn(flipped[...], branch[:, block(n, 256)]).astype(BF16)
        out_grads[block(n * 2, WIDTH), :] = out[:, 0:128]
        out_grads[block(n * 2 + 1, WIDTH), :] = out[:, 128:256]
        return carry

    lax.fori_loop(0, 4, out_gradient, 0, unroll=2)
    sums.swap(0)

    out_move.wait_recv()
    return_half(1, out_arrived)

    sums.hop(0, 0)

    place_s = iota((1, 256), 1)
    place_s = jnp.where(place_s < 128, place_s, place_s - 256)
    table_s[...] = nn(rel_bias_t[...], bucket_hot(place_s), highest)
    place_l = iota((1, TABLE), 1)
    place_l = jnp.where(place_l < 512, place_l, place_l - TABLE)
    for part in range(4):
        table_l[part] = nn(rel_bias_t[...], bucket_hot(place_l - part * LONG), highest)
    diag_l[...] = jnp.zeros_like(diag_l)
    turned[...] = (iota((128, 128), 0) + iota((128, 128), 1) == 127).astype(BF16)
    lane = iota((1, 128), 1)

    def attend_pair_back(q2, k2, v2, m2, norms, first, bias_row_of, store_diag, keep, count, width):
        d_k = jnp.zeros((count, 128), F32)
        d_v = jnp.zeros((count, 128), F32)
        d_q = []
        for side in range(2):
            here = (lane >= 64) if side else (lane < 64)
            q1 = jnp.where(here, q2, jnp.zeros_like(q2))
            m1 = jnp.where(here, m2, jnp.zeros_like(m2))
            norm = jnp.sum(jnp.where(lane == first + side, norms, 0.0), axis=1, keepdims=True)
            bias = pltpu.roll(
                jnp.broadcast_to(bias_row_of(side), (128, width)), 0, 1, stride=1, stride_axis=0
            )[:, :count]
            scores = jnp.where(keep, nt(q1, k2) * 0.125 + bias, masked_score)
            probs = jnp.exp(scores - norm)
            d_probs = nt(m1, v2)
            shift = jnp.sum(probs * d_probs, axis=1, keepdims=True)
            d_scores = (probs * (d_probs - shift)).astype(BF16)
            d_v = d_v + tn(probs.astype(BF16), m1)
            d_k = d_k + tn(d_scores, q1)
            d_q.append(nn(d_scores, k2))
            reverse = nn(turned[...], d_scores)
            reverse = jnp.concatenate([reverse, jnp.zeros((128, width - count), F32)], axis=1)
            reverse = pltpu.roll(reverse, 0, 1, stride=1, stride_axis=0)
            store_diag(side, jnp.sum(reverse, axis=0, keepdims=True))
        d_q = (jnp.where(lane < 64, d_q[0], d_q[1]) * 0.125).astype(BF16)
        return d_q, d_k * 0.125, d_v

    def short_pair(pair, carry):
        lanes = [pl.ds(pl.multiple_of(pair * 128 + which * WIDTH, 128), 128) for which in range(3)]

        def store_diag(side, value):
            diag_s[pl.ds(pair * 2 + side, 1), :] = value

        parts = attend_pair_back(
            *(short_qkv[:, here] for here in lanes),
            d_mixed[:, lanes[0]],
            norm_s[...],
            pair * 2,
            lambda side: table_s[pl.ds(pair * 2 + side, 1), :],
            store_diag,
            iota((1, 128), 1) < short_len[0],
            128,
            256,
        )
        for here, part in zip(lanes, parts):
            d_qkv[LONG:, here] = part.astype(BF16)
        return carry

    lax.fori_loop(0, HEADS // 2, short_pair, 0, unroll=2)

    def short_move(step):
        dest = lax.rem(row + step, 4)
        return pltpu.make_async_remote_copy(
            mix_short.at[dest],
            d_heads.at[row, pl.ds(LONG, LONG)],
            s_send.at[step - 1],
            s_recv.at[step - 1],
            device_id=(dest, col),
            device_id_type=MESH_ID,
        )

    def short_arrival(step):
        source = lax.rem(row + 4 - step, 4)
        return pltpu.make_async_remote_copy(
            mix_short.at[source],
            d_heads.at[source, pl.ds(LONG, LONG)],
            s_send.at[step - 1],
            s_recv.at[step - 1],
            device_id=(source, col),
            device_id_type=MESH_ID,
        )

    for step in (1, 2, 3, 0):
        dest = lax.rem(row + step, 4)
        for which in range(3):
            value = d_qkv[LONG:, pl.ds(pl.multiple_of(dest * 256 + which * WIDTH, 256), 256)]
            if step == 0:
                d_heads[row, LONG:, which * 256 : (which + 1) * 256] = value
            else:
                mix_short[dest, :, which * 256 : (which + 1) * 256] = value
        if step > 0:
            short_move(step).start()
    weight_move(2).start()
    for source in range(4):
        flip(normed_all.at[source], normed_t, source * ROWS)

    for step in (1, 2, 3):
        mix_arrival(step).wait_recv()
    d_key[...] = jnp.zeros_like(d_key)
    d_value[...] = jnp.zeros_like(d_value)

    def long_part(part, carry):
        norms = norm_l[part]
        for pair in range(2):
            here = slice(pair * 128, (pair + 1) * 128)

            def store_diag(side, value, pair=pair):
                diag_l[part, pl.ds(row * 4 + pair * 2 + side, 1), :] = value

            d_q, d_k, d_v = attend_pair_back(
                heads_in[part, :, here],
                heads_in[:, :, 256 + pair * 128 : 384 + pair * 128].reshape(512, 128),
                heads_in[:, :, 512 + pair * 128 : 640 + pair * 128].reshape(512, 128),
                mix_in[part, :, here],
                norms,
                pair * 2,
                lambda side, pair=pair: table_l[part, pl.ds(row * 4 + pair * 2 + side, 1), :],
                store_diag,
                iota((1, 512), 1) < long_len[0],
                512,
                TABLE,
            )
            d_heads[part, 0:LONG, here] = d_q
            d_key[:, here] += d_k
            d_value[:, here] += d_v
        return carry

    lax.fori_loop(0, 4, long_part, 0)
    d_heads[:, 0:LONG, 256:512] = d_key[...].astype(BF16).reshape(4, LONG, 256)
    d_heads[:, 0:LONG, 512:768] = d_value[...].astype(BF16).reshape(4, LONG, 256)

    def heads_move(step):
        dest = lax.rem(row + step, 4)
        return pltpu.make_async_remote_copy(
            d_heads.at[dest, pl.ds(0, LONG)],
            d_arrived.at[row],
            h_send.at[step - 1],
            h_recv.at[step - 1],
            device_id=(dest, col),
            device_id_type=MESH_ID,
        )

    def heads_arrival(step):
        source = lax.rem(row + 4 - step, 4)
        return pltpu.make_async_remote_copy(
            d_heads.at[source, pl.ds(0, LONG)],
            d_arrived.at[source],
            h_send.at[step - 1],
            h_recv.at[step - 1],
            device_id=(source, col),
            device_id_type=MESH_ID,
        )

    for step in (1, 2, 3):
        heads_move(step).start()
    weight_move(3).start()
    for step in (1, 2, 3):
        short_arrival(step).wait_recv()

    for which in range(3):
        here = slice(which * 256, (which + 1) * 256)
        out = nn(normed_t[...], d_heads[:, :, here].reshape(4 * ROWS, 256)).astype(BF16)
        for core in range(2):
            first = core * HEAD_ROWS + which * WIDTH
            head_grads[first : first + WIDTH, :] = out[:, core * 128 : (core + 1) * 128]
        heads.swap(which)
    sums.hop(0, 1)

    for which in range(3):
        heads.hop(which, 0)

    for step in (1, 2, 3):
        heads_arrival(step).wait_recv()
    for step in range(4):
        source = lax.rem(row + 4 - step, 4)
        for which in range(3):
            lanes = slice(which * 256, (which + 1) * 256)
            value = d_heads[row, 0:LONG, lanes] if step == 0 else d_arrived[source, :, lanes]
            d_qkv[0:LONG, pl.ds(pl.multiple_of(source * 256 + which * WIDTH, 256), 256)] = value

    def back_normed(n, carry):
        rows = block(n, 256)
        value = nt(d_qkv[:, 0:WIDTH], wq[rows, :]) + nt(d_qkv[:, WIDTH : 2 * WIDTH], wk[rows, :])
        total[:, rows] = value + nt(d_qkv[:, 2 * WIDTH :], wv[rows, :])
        return carry

    lax.fori_loop(0, 2, back_normed, 0, unroll=2)
    bias_grad = nt(diag_s[...], bucket_hot(iota((1, 256), 1) - 127), highest)
    for part in range(4):
        bias_grad = bias_grad + nt(diag_l[part], bucket_hot(iota((1, TABLE), 1) - 127 - part * LONG), highest)
    small[272:288, 0:32] = bias_grad
    sums.swap(1)
    sums.hop(0, 2)
    for which in range(3):
        heads.hop(which, 1)
    lax.fori_loop(2, 4, back_normed, 0, unroll=2)
    sums.hop(1, 0)
    for which in range(3):
        heads.gather(which, 0)
    weight_move(4).start()
    sums.gather(0, 2)
    x = tokens[...].astype(F32)
    scale = lax.rsqrt(jnp.mean(x * x, axis=1, keepdims=True) + norm_eps)
    d_normed = total[...]
    gain_grad = jnp.sum(d_normed * (x * scale), axis=0, keepdims=True)
    for i in range(8):
        last_own[i : i + 1, :] = gain_grad[:, i * 128 : (i + 1) * 128]
    d_normed = d_normed * gain_a[...]
    shrink = jnp.mean(d_normed * x, axis=1, keepdims=True)
    tokens_grad[...] = tokens_grad[...] + scale * d_normed - x * (scale * scale * scale * shrink)

    for which in range(3):
        heads.gather(which, 1)
    sums.hop(1, 1)
    sums.gather(0, 1)

    def wait_source(step, carry):
        source = lax.rem(col + step, EXPERTS)
        message(col, source).wait_recv()
        message(source, col).wait_send()
        return carry

    lax.fori_loop(1, EXPERTS, wait_source, 0)
    own_out.wait()
    out_move.wait_send()
    total[...] = jnp.zeros_like(total)
    gates = [picked[k] / picked_sum for k in range(2)]
    gates = [column(gate) for gate in gates]

    def combine(i, carry):
        here = block(i, 512)
        slot_id, quarter = ids_t[0:1, here], ids_t[1:2, here]
        weight = jnp.where(slot_id == place[0], gates[0], 0.0) + jnp.where(slot_id == place[1], gates[1], 0.0)
        high = weight.astype(BF16)
        rest = (weight - high.astype(F32)).astype(BF16)
        values = out_back[here, :]
        for q in range(4):
            here_q = quarter == q
            part = nn(jnp.where(here_q, high, jnp.zeros_like(high)), values)
            part = part + nn(jnp.where(here_q, rest, jnp.zeros_like(rest)), values)
            total[:, q * QUARTER : (q + 1) * QUARTER] += part
        return carry

    lax.fori_loop(0, PIECES // 512, combine, 0, unroll=5)
    branch_m = total[...]
    live = live_column(long_len[0], short_len[0], row)
    resid_now = resid[...]
    result = resid_now + branch_m
    block_out[...] = result
    branch_a = resid_now - tokens[...].astype(F32)
    tallies = [
        jnp.sum(live * jnp.sum(field * field, axis=1, keepdims=True), axis=0, keepdims=True)
        for field in (result, branch_a, branch_m)
    ]
    tallies.append(jnp.sum(live, axis=0, keepdims=True))
    packed = jnp.zeros((8, 128), F32)
    for i, tally in enumerate(tallies):
        packed = jnp.where(iota((8, 128), 1) == i, tally, packed)
    last_own[8:16, :] = packed

    def column_move(dest, source):
        return pltpu.make_async_remote_copy(
            last_own,
            last_col.at[source],
            c_send.at[dest],
            c_recv.at[source],
            device_id=(row, dest),
            device_id_type=MESH_ID,
        )

    def row_move(step):
        return pltpu.make_async_remote_copy(
            last_sum,
            last_row.at[step - 1],
            r_send.at[step - 1],
            r_recv.at[step - 1],
            device_id=(lax.rem(row + step, 4), col),
            device_id_type=MESH_ID,
        )

    def send_last(step, carry):
        column_move(lax.rem(col + step, EXPERTS), col).start()
        return carry

    lax.fori_loop(1, EXPERTS, send_last, 0)
    last_col[col] = last_own[...]

    for which in range(3):
        heads.gather(which, 2)
    sums.gather(0, 0)
    sums.hop(1, 2)

    def wait_last(step, carry):
        column_move(col, lax.rem(col + step, EXPERTS)).wait_recv()
        column_move(lax.rem(col + step, EXPERTS), col).wait_send()
        return carry

    lax.fori_loop(1, EXPERTS, wait_last, 0)
    last_sum[...] = jnp.sum(last_col[...], axis=0)
    for step in (1, 2, 3):
        row_move(step).start()
    weight_move(5).start()
    sums.gather(1, 2)
    for which in range(3):
        heads.last(which)
    sums.gather(1, 1)
    sums.last(0)
    sums.gather(1, 0)
    for step in (1, 2, 3):
        row_move(step).wait()
    last_sum[...] = last_sum[...] + (last_row[0] + last_row[1] + last_row[2])
    sums.last(1)
    for which in range(3):
        heads.wait(which)
    for part in range(SUM_COUNT):
        sums.end(part)
    for step in (1, 2, 3):
        mix_move(step, lax.rem(row + step, 4)).wait_send()
        heads_move(step).wait_send()
        short_move(step).wait_send()
    for index in range(len(GRAD_PIECES)):
        weight_move(index).wait()


def backward(*args):
    def out(shape, dtype):
        return jax.ShapeDtypeStruct(shape, dtype)

    return pl.pallas_call(
        backward_kernel,
        out_shape=(
            out((ROWS, WIDTH), F32),
            out((ROWS, WIDTH), F32),
            out((16, 128), F32),
            out((2 * SUM_ROWS[0], 128), BF16),
            out((4, 2 * HEAD_ROWS, 128), BF16),
            out((2 * SUM_ROWS[1], 128), F32),
            out((2 * SHARD, WIDTH), BF16),
        ),
        in_specs=[SMEM_SPEC] * 2 + [VMEM_SPEC] * (len(args) - 3) + [HBM_SPEC],
        out_specs=[VMEM_SPEC] * 3 + [HBM_SPEC] * 4,
        scratch_shapes=[
            pltpu.VMEM((2 * SUM_ROWS[0], 128), BF16),
            pltpu.VMEM((2 * HEAD_ROWS, 128), BF16),
            pltpu.VMEM((2 * SUM_ROWS[1], 128), F32),
            pltpu.VMEM((ROWS, WIDTH), F32),
            pltpu.VMEM((ROWS, WIDTH), BF16),
            pltpu.VMEM((LONG, WIDTH), BF16),
            pltpu.VMEM((4, LONG, 256), BF16),
            pltpu.VMEM((4, LONG, 256), BF16),
            pltpu.VMEM((WIDTH, ROWS), BF16),
            pltpu.VMEM((WIDTH, 4 * ROWS), BF16),
            pltpu.VMEM((ROWS, 3 * WIDTH), BF16),
            pltpu.VMEM((4, ROWS, 768), BF16),
            pltpu.VMEM((4, LONG, 768), BF16),
            pltpu.VMEM((4, LONG, 768), BF16),
            pltpu.VMEM((512, 256), F32),
            pltpu.VMEM((512, 256), F32),
            pltpu.VMEM((4, HEADS, TABLE), F32),
            pltpu.VMEM((HEADS, 256), F32),
            pltpu.VMEM((4, HEADS, TABLE), F32),
            pltpu.VMEM((HEADS, 256), F32),
            pltpu.VMEM((128, 128), BF16),
            pltpu.VMEM((PIECES // 2, QUARTER), BF16),
            pltpu.VMEM((PIECES, QUARTER), BF16),
            pltpu.VMEM((PIECES, QUARTER), BF16),
            pltpu.VMEM((16, 128), F32),
            pltpu.VMEM((EXPERTS, 16, 128), F32),
            pltpu.VMEM((3, 16, 128), F32),
            DMA,
            DMA,
            DMA((3,)),
            DMA((3,)),
            DMA((3,)),
            DMA((3,)),
            DMA((3,)),
            DMA((3,)),
            DMA((EXPERTS,)),
            DMA((EXPERTS,)),
            DMA,
            DMA((len(GRAD_PIECES),)),
            DMA((len(GRAD_PIECES),)),
            DMA((EXPERTS,)),
            DMA((EXPERTS,)),
            DMA((3,)),
            DMA((3,)),
        ]
        + sum_scratch()
        + head_scratch(),
        compiler_params=pltpu.CompilerParams(
            collective_id=3, has_side_effects=True, vmem_limit_bytes=60 * 1024 * 1024
        ),
        name="backward_and_sums",
    )(*args)


def per_device(
    tokens_in, out_cot, long_lengths, short_lengths, routes, gain_attn, w_query, w_key, w_value, w_out, rel_bias,
    gain_moe, router, w_gate, w_up, w_down,
):
    own = (jnp.swapaxes(w_gate[0], 0, 1), jnp.swapaxes(w_up[0], 0, 1), w_down[0])
    routes_t = jnp.swapaxes(routes, 0, 1)
    router_t = jnp.swapaxes(router, 0, 1)
    rel_bias_t = jnp.swapaxes(rel_bias, 0, 1)
    gain_a, gain_m = gain_attn.reshape(1, WIDTH), gain_moe.reshape(1, WIDTH)
    ids = piece_ids()
    sent = forward(
        long_lengths, short_lengths, tokens_in, out_cot, routes_t, gain_a, gain_m, rel_bias_t, router_t,
        jnp.asarray(ids.T), w_query, w_key, w_value, w_out, *own,
    )
    x_slots, o_slots, g_slots, *other = sent[:6]
    normed_a, heads_in, short_qkv, mixed, norm_l, norm_s, resid, probs_t, rnorm_t = sent[6:]
    unfold = unfold_matrix()
    row_of = np.arange(640) // SLOTS
    consts = (
        jnp.asarray(unfold, BF16),
        jnp.asarray(unfold.T, BF16),
        jnp.asarray((row_of[:, None] == np.arange(EXPERTS)[None, :]).astype(np.float32)),
        jnp.asarray((np.arange(640) % SLOTS).astype(np.int32)[:, None]),
    )
    dx_back, dg_back, outs, out_first, normed_all, grad_own, grad_send, grad_early = experts(x_slots, o_slots, g_slots, consts, own, other, normed_a)
    block_out, tokens_grad, last, out_grads, head_grads, small, grad_late = backward(
        long_lengths, short_lengths, tokens_in, out_cot, routes_t, gain_a, gain_m, rel_bias_t, router_t,
        jnp.asarray(ids), w_query, w_key, w_value, w_out, resid, probs_t, rnorm_t, heads_in, short_qkv, mixed,
        norm_l, norm_s, dx_back, dg_back, outs, out_first, normed_all, grad_send,
    )
    wo_sum, wq_sum, wk_sum, wv_sum, wg_sum, wu_sum, wd_sum, gain_a_sum, gain_m_sum, bias, router_sum, stats = finish(
        out_grads, head_grads, small, last, grad_own, grad_early, grad_late
    )
    return (
        block_out,
        tokens_grad,
        gain_a_sum.reshape(WIDTH),
        wq_sum,
        wk_sum,
        wv_sum,
        wo_sum,
        jnp.swapaxes(bias, 0, 1),
        gain_m_sum.reshape(WIDTH),
        jnp.swapaxes(router_sum, 0, 1),
        jnp.swapaxes(wg_sum, 0, 1)[None],
        jnp.swapaxes(wu_sum, 0, 1)[None],
        wd_sum[None],
        stats[0, 0:3],
    )


def solution(mesh):
    tokens = P(("row", "col"), None)
    whole = P()
    wide = P("col", None, "row")
    tall = P("col", "row", None)
    return jax.shard_map(
        per_device,
        mesh=mesh,
        in_specs=(tokens, tokens, P("col"), P(("row", "col")), tokens) + (whole,) * 8 + (wide, wide, tall),
        out_specs=(tokens, tokens) + (whole,) * 8 + (wide, wide, tall, whole),
        check_vma=False,
    )
```

```python
import functools

import numpy as np
import jax
import jax.numpy as jnp
from jax import lax
from jax.experimental import pallas as pl
from jax.experimental.pallas import tpu as pltpu
from jax.sharding import PartitionSpec as P

HEADS = 16
HEAD_DIM = 64
WIDTH = 1024
ROWS = 256
LONG = 128
EXPERTS = 32
SLOTS = 20
FOLDED = 80
QUARTER = 256
PIECES = EXPERTS * FOLDED
TABLE = 640
SHARD = 704
PADDED = 768
EARLY_DOWN = 352
FIRST_DOWN = 176
FIRST_GATE = 352
GRAD_ROWS = 3 * SHARD
EARLY_UP = 176
GRAD_PIECES = (352, 160, 208, 160, 160, 192)

bucket_edges = (1, 2, 3, 4, 5, 6, 7, 8, 12, 16, 23, 32, 46, 64, 91)
norm_eps = 1e-06
balance_coef = 0.01
zloss_coef = 0.001
masked_score = -1e30
highest = lax.Precision.HIGHEST
MESH_ID = pl.DeviceIdType.MESH
F32 = jnp.float32
BF16 = jnp.bfloat16
VMEM_SPEC = pl.BlockSpec(memory_space=pltpu.VMEM)
HBM_SPEC = pl.BlockSpec(memory_space=pl.ANY)
SMEM_SPEC = pl.BlockSpec(memory_space=pltpu.SMEM)
DMA = pltpu.SemaphoreType.DMA


def piece_ids():
    row = np.arange(PIECES)
    slot = (row // FOLDED) * SLOTS + row % SLOTS
    quarter = (row % FOLDED) // SLOTS
    return np.stack([slot, quarter]).astype(np.float32)


def unfold_matrix():
    out = np.arange(320)
    quarter, message, slot = out // 80, (out % 80) // SLOTS, out % SLOTS
    hot = np.zeros((320, 320), np.float32)
    hot[out, message * FOLDED + quarter * SLOTS + slot] = 1
    return hot


def nt(left, right, precision=None):
    return lax.dot_general(
        left, right, (((1,), (1,)), ((), ())), preferred_element_type=F32, precision=precision
    )


def tn(left, right):
    return lax.dot_general(left, right, (((0,), (0,)), ((), ())), preferred_element_type=F32)


def nn(left, right, precision=None):
    return jnp.dot(left, right, preferred_element_type=F32, precision=precision)


def iota(shape, dim):
    return lax.broadcasted_iota(jnp.int32, shape, dim)


def block(index, size):
    return pl.ds(pl.multiple_of(index * size, size), size)


def bucket_hot(relative):
    magnitude = jnp.abs(relative)
    level = jnp.zeros_like(relative)
    for edge in bucket_edges:
        level = level + (magnitude >= edge).astype(jnp.int32)
    level = level + jnp.where(relative > 0, len(bucket_edges) + 1, 0)
    return (iota((32, relative.shape[1]), 0) == level).astype(F32)


def route_places(routes_t):
    hots = [(iota((EXPERTS, ROWS), 0) == routes_t[k : k + 1, :]).astype(F32) for k in range(2)]
    both = hots[0] + hots[1]
    before = (iota((ROWS, ROWS), 0) < iota((ROWS, ROWS), 1)).astype(BF16)
    earlier = nn(both.astype(BF16), before)
    slots = [jnp.sum(earlier * hot, axis=0, keepdims=True) for hot in hots]
    places = [routes_t[k : k + 1, :].astype(F32) * SLOTS + slots[k] for k in range(2)]
    return hots, both, slots, places


def slot_hot(slots_row):
    return (iota((128, ROWS), 0).astype(F32) == slots_row).astype(F32)


def live_column(long_len, short_len, row):
    position = iota((ROWS, 1), 0)
    is_long = position < LONG
    here = jnp.where(is_long, position + row * LONG, position - LONG)
    limit = jnp.where(is_long, long_len, short_len)
    return (here < limit).astype(F32)


def row_pairs():
    row = lax.axis_index("row")
    core = lax.rem(lax.axis_index("col"), 2)
    near, far = row + 1 - 2 * lax.rem(row, 2), 3 - row
    partner = near * (1 - core) + far * core
    return partner, near + far - partner


SUM_PARTS = (
    (4096, 0, ("x", "z", "y"), 0),
    (512, 0, ("z", "x", "y"), 1),
)
SUM_ROWS = (4096, 512)
SUM_COUNT = len(SUM_PARTS)


def torus_place():
    row = lax.axis_index("row")
    col = lax.axis_index("col")
    return row, lax.div(col, 8), lax.rem(lax.div(col, 2), 4), lax.rem(col, 2)


def axis_peer(axis, step):
    row, z, x, core = torus_place()
    if axis == "y":
        row = lax.rem(row + step, 4)
    elif axis == "x":
        x = lax.rem(x + step, 4)
    elif axis == "z":
        z = lax.rem(z + step, 4)
    else:
        core = 1 - core
    return (row, (z * 4 + x) * 2 + core)


class SumSteps:
    def __init__(self, sources, results, other, slots, sems):
        self.sources, self.results, self.other, self.slots = sources, results, other, slots
        (
            self.core_send, self.core_recv, self.hop_send, self.hop_recv, self.gather_send, self.gather_recv,
            self.copy_sem, self.last_send, self.last_recv,
        ) = sems
        row, z, x, self.core = torus_place()
        self.place = {"x": x, "y": row, "z": z}
        self.flight = {}

    def base(self, p, levels):
        rows, first, order, kind = SUM_PARTS[p]
        base = self.core * SUM_ROWS[kind] + first
        for done in range(levels):
            base = base + self.place[order[done]] * (rows // 4 ** (done + 1))
        return base

    def at(self, kind, start, rows):
        return pl.ds(pl.multiple_of(start, 8 if kind else 16), rows)

    def add(self, kind, start, rows, terms):
        if kind:
            tile = min(rows, 128)
        else:
            tile = next(t for t in (512, 384, 256, 192, 128, 64, 48, 32) if rows % t == 0)
        source = self.sources[kind]

        def body(i, carry):
            here = self.at(kind, start + i * tile, tile)
            total = source[here, :].astype(F32)
            for ref, first in terms:
                total = total + ref[self.at(kind, first + i * tile, tile), :].astype(F32)
            source[here, :] = total.astype(source.dtype)
            return carry

        lax.fori_loop(0, rows // tile, body, 0)

    def swap(self, p):
        rows, first, order, kind = SUM_PARTS[p]
        theirs = (1 - self.core) * SUM_ROWS[kind] + first
        move = pltpu.make_async_remote_copy(
            self.sources[kind].at[self.at(kind, theirs, rows)],
            self.other[kind].at[pl.ds(first, rows)],
            self.core_send.at[p],
            self.core_recv.at[p],
            device_id=axis_peer("core", 1),
            device_id_type=MESH_ID,
        )
        move.start()
        self.flight[p] = [move]

    def hop(self, p, level):
        rows, first, order, kind = SUM_PARTS[p]
        for move in self.flight[p]:
            move.wait()
        if level == 0:
            self.add(kind, self.base(p, 0), rows, [(self.other[kind], first)])
        else:
            self.end_hop(p, level - 1)
        size = rows // 4 ** (level + 1)
        axis = order[level]
        self.flight[p] = []
        for step in (1, 2, 3):
            block_of = lax.rem(self.place[axis] + step, 4)
            move = pltpu.make_async_remote_copy(
                self.sources[kind].at[self.at(kind, self.base(p, level) + block_of * size, size)],
                self.slots[p * 3 + level].at[pl.ds((step - 1) * size, size)],
                self.hop_send.at[p, level, step - 1],
                self.hop_recv.at[p, level, step - 1],
                device_id=axis_peer(axis, step),
                device_id_type=MESH_ID,
            )
            move.start()
            self.flight[p].append(move)

    def end_hop(self, p, level):
        rows, first, order, kind = SUM_PARTS[p]
        size = rows // 4 ** (level + 1)
        slots = self.slots[p * 3 + level]
        self.add(kind, self.base(p, level + 1), size, [(slots, step * size) for step in range(3)])

    def gather(self, p, level):
        rows, first, order, kind = SUM_PARTS[p]
        for move in self.flight[p]:
            move.wait()
        if level == 2:
            self.end_hop(p, 2)
        here = self.at(kind, self.base(p, level + 1), rows // 4 ** (level + 1))
        source = self.sources[kind].at[here] if level == 2 else self.results[kind].at[here]
        target = self.results[kind].at[here]
        self.flight[p] = []
        for step in (1, 2, 3):
            move = pltpu.make_async_remote_copy(
                source,
                target,
                self.gather_send.at[p, level, step - 1],
                self.gather_recv.at[p, level, step - 1],
                device_id=axis_peer(order[level], step),
                device_id_type=MESH_ID,
            )
            move.start()
            self.flight[p].append(move)
        if level == 2:
            keep = pltpu.make_async_copy(source, target, self.copy_sem.at[p])
            keep.start()
            self.flight[p].append(keep)

    def last(self, p):
        rows, first, order, kind = SUM_PARTS[p]
        size = rows // 4
        moves = []
        for index in range(4):
            if index > 0:
                self.flight[p][index - 1].wait()
            block_of = lax.rem(self.place[order[0]] + 4 - index, 4)
            here = self.results[kind].at[self.at(kind, self.base(p, 0) + block_of * size, size)]
            move = pltpu.make_async_remote_copy(
                here,
                here,
                self.last_send.at[p, index],
                self.last_recv.at[p, index],
                device_id=axis_peer("core", 1),
                device_id_type=MESH_ID,
            )
            move.start()
            moves.append(move)
        self.flight[p] = moves

    def end(self, p):
        for move in self.flight[p]:
            move.wait()


HEAD_ROWS = 3 * WIDTH
HEAD_ORDERS = (("x", "z"), ("z", "x"), ("x", "z"))


class HeadSums:
    def __init__(self, source, result, other, slots, sems):
        self.source, self.result, self.other, self.slots = source, result, other, slots
        (
            self.core_send, self.core_recv, self.hop_send, self.hop_recv, self.gather_send, self.gather_recv,
            self.copy_sem, self.last_send, self.last_recv,
        ) = sems
        self.row, z, x, self.core = torus_place()
        self.place = {"x": x, "y": self.row, "z": z}
        self.flight = {}

    def base(self, p, levels):
        base = self.core * HEAD_ROWS + p * WIDTH
        for done in range(levels):
            base = base + self.place[HEAD_ORDERS[p][done]] * (WIDTH // 4 ** (done + 1))
        return base

    def at(self, start, rows):
        return pl.ds(pl.multiple_of(start, 16), rows)

    def wait(self, p):
        for move in self.flight[p]:
            move.wait()

    def add(self, start, rows, terms):
        tile = min(rows, 256)

        def body(i, carry):
            here = self.at(start + i * tile, tile)
            total = self.source[here, :].astype(F32)
            for ref, first in terms:
                total = total + ref[self.at(first + i * tile, tile), :].astype(F32)
            self.source[here, :] = total.astype(BF16)
            return carry

        lax.fori_loop(0, rows // tile, body, 0)

    def send(self, p, moves, axis, send, recv, sems):
        self.flight[p] = []
        for step, (source, target) in zip((1, 2, 3), moves):
            move = pltpu.make_async_remote_copy(
                source,
                target,
                send.at[(*sems, step - 1)],
                recv.at[(*sems, step - 1)],
                device_id=axis_peer(axis, step),
                device_id_type=MESH_ID,
            )
            move.start()
            self.flight[p].append(move)

    def swap(self, p):
        move = pltpu.make_async_remote_copy(
            self.source.at[self.at((1 - self.core) * HEAD_ROWS + p * WIDTH, WIDTH)],
            self.other.at[pl.ds(p * WIDTH, WIDTH)],
            self.core_send.at[p],
            self.core_recv.at[p],
            device_id=axis_peer("core", 1),
            device_id_type=MESH_ID,
        )
        move.start()
        self.flight[p] = [move]

    def hop(self, p, level):
        self.wait(p)
        if level == 0:
            self.add(self.base(p, 0), WIDTH, [(self.other, p * WIDTH)])
        else:
            self.end_hop(p, level - 1)
        size = WIDTH // 4 ** (level + 1)
        axis = HEAD_ORDERS[p][level]
        moves = []
        for step in (1, 2, 3):
            block_of = lax.rem(self.place[axis] + step, 4)
            moves.append(
                (
                    self.source.at[self.at(self.base(p, level) + block_of * size, size)],
                    self.slots[p * 2 + level].at[pl.ds((step - 1) * size, size)],
                )
            )
        self.send(p, moves, axis, self.hop_send, self.hop_recv, (p, level))

    def end_hop(self, p, level):
        size = WIDTH // 4 ** (level + 1)
        slots = self.slots[p * 2 + level]
        self.add(self.base(p, level + 1), size, [(slots, step * size) for step in range(3)])

    def gather(self, p, turn):
        self.wait(p)
        row_last = p == 2
        if turn == 0:
            self.end_hop(p, 1)
        levels = (2, 1, 0) if row_last else (2, 2, 1)
        base = self.base(p, levels[turn])
        here = self.at(base, WIDTH // 4 ** levels[turn])
        if row_last:
            axis = (HEAD_ORDERS[p][1], HEAD_ORDERS[p][0], "y")[turn]
        else:
            axis = ("y", HEAD_ORDERS[p][1], HEAD_ORDERS[p][0])[turn]
        whole = turn > 0 and not row_last
        target = self.result.at[:, here] if whole else self.result.at[self.row, here]
        source = self.source.at[here] if turn == 0 else target
        self.send(p, [(source, target)] * 3, axis, self.gather_send, self.gather_recv, (p, turn))
        if turn == 0:
            keep = pltpu.make_async_copy(source, target, self.copy_sem.at[p])
            keep.start()
            self.flight[p].append(keep)

    def last(self, p):
        moves = []
        for index in range(4):
            if index > 0:
                self.flight[p][index - 1].wait()
            if p == 2:
                here = self.result.at[lax.rem(self.row + 4 - index, 4), self.at(self.base(p, 0), WIDTH)]
            else:
                size = WIDTH // 4
                block_of = lax.rem(self.place[HEAD_ORDERS[p][0]] + 4 - index, 4)
                here = self.result.at[:, self.at(self.base(p, 0) + block_of * size, size)]
            move = pltpu.make_async_remote_copy(
                here,
                here,
                self.last_send.at[p, index],
                self.last_recv.at[p, index],
                device_id=axis_peer("core", 1),
                device_id_type=MESH_ID,
            )
            move.start()
            moves.append(move)
        self.flight[p] = moves


def head_scratch():
    scratch = [pltpu.VMEM((HEAD_ROWS, 128), BF16)]
    for p in range(3):
        scratch += [pltpu.VMEM((3 * WIDTH // 4, 128), BF16), pltpu.VMEM((3 * WIDTH // 16, 128), BF16)]
    shapes = [(3,)] * 2 + [(3, 2, 3)] * 2 + [(3, 3, 3)] * 2 + [(3,)] + [(3, 4)] * 2
    return scratch + [DMA(shape) for shape in shapes]


def sum_scratch():
    scratch = [
        pltpu.VMEM((SUM_ROWS[0], 128), BF16),
        pltpu.VMEM((SUM_ROWS[1], 128), F32),
    ]
    for rows, first, order, kind in SUM_PARTS:
        for level in range(3):
            scratch.append(pltpu.VMEM((3 * rows // 4 ** (level + 1), 128), F32 if kind else BF16))
    shapes = [(SUM_COUNT,)] * 2 + [(SUM_COUNT, 3, 3)] * 4 + [(SUM_COUNT,)] + [(SUM_COUNT, 4)] * 2
    return scratch + [DMA(shape) for shape in shapes]


def finish(out_grads, head_grads, small, last, own, early, late):
    steps = 4
    sum_tile, expert_tile = WIDTH // steps, SHARD // steps

    def kernel(out_ref, head_ref, small_ref, last_ref, own_ref, gate_ref, up_ref, more_up_ref, down_ref, *results):
        for i in range(8):
            lanes = slice(i * 128, (i + 1) * 128)
            results[0][:, lanes] = out_ref[i // 4, i % 4].astype(F32)
            for which in range(3):
                results[1 + which][:, lanes] = head_ref[i // 2, i % 2, which].astype(F32)
        for which, result in enumerate(results[4:7]):
            if which == 1:
                part = jnp.where(pl.program_id(0) == 0, up_ref[...], more_up_ref[...])
            else:
                part = (gate_ref, up_ref, down_ref)[which][...]
            result[...] = own_ref[which] + part.astype(F32)
        gain_a, gain_m, bias, router, statistics = results[7:]

        @pl.when(pl.program_id(0) == 0)
        def _():
            for i in range(8):
                router[:, i * 128 : (i + 1) * 128] = small_ref[i * 32 : (i + 1) * 32, :]
            gain_a[...] = last_ref[0:8, :]
            gain_m[...] = small_ref[264:272, :]
            bias[...] = small_ref[272:288, 0:32]
            totals = last_ref[8:9, :]
            count = jnp.sum(jnp.where(iota((1, 128), 1) == 3, totals, 0.0), axis=1, keepdims=True)
            statistics[...] = jnp.sqrt(totals / (count * WIDTH))

    def whole(shape):
        return pl.BlockSpec(shape, lambda i: (0,) * len(shape))

    def rows(tile):
        return pl.BlockSpec((tile, WIDTH), lambda i: (i, 0))

    small_shapes = ((8, 128), (8, 128), (HEADS, 32), (EXPERTS, WIDTH), (1, 128))
    return pl.pallas_call(
        kernel,
        grid=(steps,),
        out_shape=(jax.ShapeDtypeStruct((WIDTH, WIDTH), F32),) * 4
        + (jax.ShapeDtypeStruct((SHARD, WIDTH), F32),) * 3
        + tuple(jax.ShapeDtypeStruct(shape, F32) for shape in small_shapes),
        in_specs=[
            pl.BlockSpec((2, 4, sum_tile, 128), lambda i: (0, 0, i, 0)),
            pl.BlockSpec((4, 2, 3, sum_tile, 128), lambda i: (0, 0, 0, i, 0)),
            whole((288, 128)),
            whole((16, 128)),
            pl.BlockSpec((3, expert_tile, WIDTH), lambda i: (0, i, 0)),
            rows(expert_tile),
            pl.BlockSpec((expert_tile, WIDTH), lambda i: (steps, 0)),
            pl.BlockSpec((expert_tile, WIDTH), lambda i: (jnp.maximum(i - 1, 0), 0)),
            pl.BlockSpec((expert_tile, WIDTH), lambda i: (i + steps - 1, 0)),
        ],
        out_specs=(rows(sum_tile),) * 4 + (rows(expert_tile),) * 3 + tuple(whole(shape) for shape in small_shapes),
        compiler_params=pltpu.CompilerParams(vmem_limit_bytes=62 * 1024 * 1024),
        name="finish",
    )(
        out_grads.reshape(2, 4, WIDTH, 128),
        head_grads.reshape(4, 2, 3, WIDTH, 128),
        small,
        last,
        own.reshape(3, SHARD, WIDTH),
        early,
        early,
        late,
        late,
    )


def forward_kernel(
    long_len, short_len, tokens, cot, routes_t, gain_a, gain_m, rel_bias_t, router_t, ids, wq, wk, wv, wo, wg_own, wu_own, wd_own,
    x_slots, o_slots, g_slots, wg_mate, wu_mate, wd_mate, normed_a, heads_in, short_qkv, mixed, norm_l, norm_s, resid, probs_t, rnorm_t,
    normed, heads_out, mix_out, buffer_o, buffer_x, gate_out, table_l, table_s,
    o_send, o_recv, x_send, x_recv, g_send, g_recv, own_sem, h_send, h_recv, mix_send, mix_recv, t_send, t_recv, w_send, w_recv,
):
    row = lax.axis_index("row")
    col = lax.axis_index("col")
    partner, mate = row_pairs()
    barrier = pltpu.get_barrier_semaphore()
    for step in (1, 2, 3):
        pl.semaphore_signal(barrier, inc=1, device_id=(lax.rem(row + step, 4), col), device_id_type=MESH_ID)

    def greet(step, carry):
        pl.semaphore_signal(barrier, inc=1, device_id=(row, lax.rem(col + step, EXPERTS)), device_id_type=MESH_ID)
        return carry

    lax.fori_loop(1, EXPERTS, greet, 0)

    hots, both, slots, places = route_places(routes_t[...])

    def message(buffer, slots_ref, send, recv, dest, source):
        return pltpu.make_async_remote_copy(
            buffer.at[block(dest, FOLDED)],
            slots_ref.at[0, block(source, FOLDED)],
            send.at[dest],
            recv.at[source],
            device_id=(row, dest),
            device_id_type=MESH_ID,
        )

    def dispatch(source, buffer, slots_ref, send, recv, own):
        def one_group(i, carry):
            group = lax.rem(lax.div(col, 4) + i, 8)
            rows = block(group, 320)
            slot_id = ids[rows, 0:1]
            quarter = ids[rows, 1:2]
            match = (slot_id == places[0]) | (slot_id == places[1])
            total = jnp.zeros((320, QUARTER), F32)
            for q in range(4):
                hot = jnp.where(match & (quarter == q), 1.0, 0.0).astype(BF16)
                total = total + nn(hot, source[:, q * QUARTER : (q + 1) * QUARTER])
            buffer[rows, :] = total.astype(BF16)
            for j in range(4):
                dest = group * 4 + j

                @pl.when(dest != col)
                def _():
                    message(buffer, slots_ref, send, recv, dest, col).start()

                @pl.when(dest == col)
                def _():
                    pltpu.make_async_copy(
                        buffer.at[block(dest, FOLDED)], slots_ref.at[0, block(dest, FOLDED)], own
                    ).start()

            return carry

        lax.fori_loop(0, 8, one_group, 0, unroll=2)

    def wait_source(buffer, slots_ref, send, recv, own, source):
        @pl.when(source != col)
        def _():
            message(buffer, slots_ref, send, recv, col, source).wait_recv()

        @pl.when(source == col)
        def _():
            pltpu.make_async_copy(
                buffer.at[block(col, FOLDED)], slots_ref.at[0, block(col, FOLDED)], own
            ).wait()

    def wait_sends(buffer, slots_ref, send, recv):
        def one(step, carry):
            message(buffer, slots_ref, send, recv, lax.rem(col + step, EXPERTS), col).wait_send()
            return carry

        lax.fori_loop(1, EXPERTS, one, 0)

    pl.semaphore_wait(barrier, EXPERTS + 2)

    weight_moves = []
    for own, target, first, last in (
        (wd_own, wd_mate, 0, FIRST_DOWN),
        (wg_own, wg_mate, 0, FIRST_GATE),
        (wg_own, wg_mate, FIRST_GATE, SHARD),
        (wu_own, wu_mate, 0, SHARD),
        (wd_own, wd_mate, FIRST_DOWN, EARLY_DOWN),
    ):
        rows = pl.ds(first, last - first)
        i = len(weight_moves)
        weight_moves.append(
            pltpu.make_async_remote_copy(
                own.at[rows], target.at[rows], w_send.at[i], w_recv.at[i], device_id=(partner, col),
                device_id_type=MESH_ID,
            )
        )
    weight_moves[0].start()

    def norm_rows(i, carry):
        rows = block(i, 64)
        x = tokens[rows, :].astype(F32)
        scale = lax.rsqrt(jnp.mean(x * x, axis=1, keepdims=True) + norm_eps)
        normed_a[rows, :] = (x * scale * gain_a[...]).astype(BF16)
        return carry

    lax.fori_loop(0, 4, norm_rows, 0, unroll=4)

    def heads_move(step):
        dest = lax.rem(row + step, 4)
        return pltpu.make_async_remote_copy(
            heads_out.at[dest],
            heads_in.at[row],
            h_send.at[step - 1],
            h_recv.at[step - 1],
            device_id=(dest, col),
            device_id_type=MESH_ID,
        )

    def heads_arrival(step):
        source = lax.rem(row + 4 - step, 4)
        return pltpu.make_async_remote_copy(
            heads_out.at[source],
            heads_in.at[source],
            h_send.at[step - 1],
            h_recv.at[step - 1],
            device_id=(source, col),
            device_id_type=MESH_ID,
        )

    for step in (1, 2, 3, 0):
        dest = lax.rem(row + step, 4)
        lanes = block(dest, 256)
        for which, weight in enumerate((wq, wk, wv)):
            part = nn(normed_a[...], weight[:, lanes]).astype(BF16)
            here = slice(which * 256, (which + 1) * 256)
            if step == 0:
                heads_in[row, :, here] = part[:LONG]
            else:
                heads_out[dest, :, here] = part[:LONG]
            short_qkv[:, pl.ds(pl.multiple_of(dest * 256 + which * WIDTH, 256), 256)] = part[LONG:]
        if step > 0:
            heads_move(step).start()
    weight_moves[1].start()

    dispatch(cot, buffer_o, o_slots, o_send, o_recv, own_sem.at[0])

    place_s = iota((1, 256), 1)
    place_s = jnp.where(place_s < 128, place_s, place_s - 256)
    table_s[...] = nn(rel_bias_t[...], bucket_hot(place_s), highest)
    place_l = iota((1, TABLE), 1)
    place_l = jnp.where(place_l < 512, place_l, place_l - TABLE)
    for part in range(4):
        table_l[part] = nn(rel_bias_t[...], bucket_hot(place_l - part * LONG), highest)

    lane = iota((1, 128), 1)

    def attend(q2, k2, v2, bias_row, keep, count, width):
        bias = pltpu.roll(jnp.broadcast_to(bias_row, (128, width)), 0, 1, stride=1, stride_axis=0)[:, :count]
        scores = jnp.where(keep, nt(q2, k2) * 0.125 + bias, masked_score)
        row_max = jnp.max(scores, axis=1, keepdims=True)
        terms = jnp.exp(scores - row_max)
        total = jnp.sum(terms, axis=1, keepdims=True)
        return nn((terms / total).astype(BF16), v2), row_max + jnp.log(total)

    def attend_pair(q2, k2, v2, bias_row_of, keep, count, width, first, norms):
        outs = []
        for side in range(2):
            here = (lane >= 64) if side else (lane < 64)
            out, norm = attend(
                jnp.where(here, q2, jnp.zeros_like(q2)), k2, v2, bias_row_of(side), keep, count, width
            )
            outs.append(out)
            norms = jnp.where(lane == first + side, norm, norms)
        return jnp.where(lane < 64, outs[0], outs[1]).astype(BF16), norms

    norm_s[...] = jnp.zeros_like(norm_s)

    def short_pair(pair, carry):
        q2, k2, v2 = (
            short_qkv[:, pl.ds(pl.multiple_of(pair * 128 + which * WIDTH, 128), 128)] for which in range(3)
        )
        out, norms = attend_pair(
            q2, k2, v2, lambda side: table_s[pl.ds(pair * 2 + side, 1), :], iota((1, 128), 1) < short_len[0], 128, 256,
            pair * 2, norm_s[...],
        )
        mixed[LONG:, block(pair, 128)] = out
        norm_s[...] = norms
        return carry

    lax.fori_loop(0, HEADS // 2, short_pair, 0, unroll=2)

    def to_mate(source, target, index):
        return pltpu.make_async_remote_copy(
            source, target, t_send.at[index], t_recv.at[index], device_id=(mate, col), device_id_type=MESH_ID
        )

    def o_move(group):
        rows = block(group, 320)
        return to_mate(o_slots.at[0, rows], o_slots.at[1, rows], 9 + group)

    def forward_o(i, carry):
        group = lax.rem(lax.div(col, 4) + 8 - i, 8)
        for j in range(4):
            wait_source(buffer_o, o_slots, o_send, o_recv, own_sem.at[0], group * 4 + j)
        o_move(group).start()
        return carry

    lax.fori_loop(0, 4, forward_o, 0)

    for step in (1, 2, 3):
        heads_arrival(step).wait_recv()

    def mix_move(step, dest):
        return pltpu.make_async_remote_copy(
            mix_out.at[dest],
            mixed.at[pl.ds(0, LONG), block(row, 256)],
            mix_send.at[step - 1],
            mix_recv.at[step - 1],
            device_id=(dest, col),
            device_id_type=MESH_ID,
        )

    def mix_arrival(step):
        source = lax.rem(row + 4 - step, 4)
        return pltpu.make_async_remote_copy(
            mix_out.at[source],
            mixed.at[pl.ds(0, LONG), block(source, 256)],
            mix_send.at[step - 1],
            mix_recv.at[step - 1],
            device_id=(source, col),
            device_id_type=MESH_ID,
        )

    def long_part(step, carry):
        part = lax.rem(row + step, 4)
        norms = jnp.zeros((128, 128), F32)
        outs = []
        for pair in range(2):
            here = slice(pair * 128, (pair + 1) * 128)
            q2 = heads_in[part, :, here]
            k2 = heads_in[:, :, 256 + pair * 128 : 384 + pair * 128].reshape(512, 128)
            v2 = heads_in[:, :, 512 + pair * 128 : 640 + pair * 128].reshape(512, 128)
            out, norms = attend_pair(
                q2, k2, v2, lambda side, pair=pair: table_l[part, pl.ds(row * 4 + pair * 2 + side, 1), :],
                iota((1, 512), 1) < long_len[0], 512, TABLE, pair * 2, norms,
            )
            outs.append(out)
        norm_l[part] = norms
        mix_out[part] = jnp.concatenate(outs, axis=1)
        return carry

    def long_and_send(step, carry):
        long_part(step, carry)
        mix_move(step, lax.rem(row + step, 4)).start()
        return carry

    lax.fori_loop(1, 4, long_and_send, 0)
    long_part(0, 0)
    mixed[0:LONG, block(row, 256)] = mix_out[row]
    for move in weight_moves[2:]:
        move.start()

    lax.fori_loop(4, 8, forward_o, 0)

    for step in (1, 2, 3):
        mix_arrival(step).wait_recv()

    def project_out(i, carry):
        lanes = block(i, 256)
        resid[:, lanes] = tokens[:, lanes].astype(F32) + nn(mixed[...], wo[:, lanes])
        return carry

    lax.fori_loop(0, 4, project_out, 0, unroll=4)

    def norm_again(i, carry):
        rows = block(i, 64)
        x = resid[rows, :]
        scale = lax.rsqrt(jnp.mean(x * x, axis=1, keepdims=True) + norm_eps)
        normed[rows, :] = (x * scale * gain_m[...]).astype(BF16)
        return carry

    lax.fori_loop(0, 4, norm_again, 0, unroll=4)
    dispatch(normed, buffer_x, x_slots, x_send, x_recv, own_sem.at[1])

    x = resid[...]
    scale = lax.rsqrt(jnp.mean(x * x, axis=1, keepdims=True) + norm_eps)
    logits = nt(router_t[...], x * scale * gain_m[...], highest)
    row_max = jnp.max(logits, axis=0, keepdims=True)
    terms = jnp.exp(logits - row_max)
    total = jnp.sum(terms, axis=0, keepdims=True)
    probs = terms / total
    probs_t[...] = probs
    rnorm_t[...] = row_max + jnp.log(total)
    picked = [jnp.sum(probs * hot, axis=0, keepdims=True) for hot in hots]
    picked_sum = picked[0] + picked[1]
    gate_slots = jnp.zeros((EXPERTS, 128), F32)
    for k in range(2):
        gate_slots = gate_slots + nt(hots[k] * (picked[k] / picked_sum), slot_hot(slots[k]), highest)
    for e in range(EXPERTS):
        gate_out[e] = jnp.broadcast_to(gate_slots[e : e + 1, :], (8, 128))

    def gate_message(dest, source):
        return pltpu.make_async_remote_copy(
            gate_out.at[dest],
            g_slots.at[0, source],
            g_send.at[dest],
            g_recv.at[source],
            device_id=(row, dest),
            device_id_type=MESH_ID,
        )

    def send_gates(step, carry):
        gate_message(lax.rem(col + step, EXPERTS), col).start()
        return carry

    lax.fori_loop(1, EXPERTS, send_gates, 0)
    own_gates = pltpu.make_async_copy(gate_out.at[col], g_slots.at[0, col], own_sem.at[2])
    own_gates.start()

    def x_move(group):
        rows = block(group, 320)
        return to_mate(x_slots.at[0, rows], x_slots.at[1, rows], group)

    def forward_x(i, carry):
        group = lax.rem(lax.div(col, 4) + 8 - i, 8)
        for j in range(4):
            wait_source(buffer_x, x_slots, x_send, x_recv, own_sem.at[1], group * 4 + j)
        x_move(group).start()
        return carry

    lax.fori_loop(0, 8, forward_x, 0)

    def wait_gates(step, carry):
        gate_message(col, lax.rem(col + step, EXPERTS)).wait_recv()
        return carry

    lax.fori_loop(1, EXPERTS, wait_gates, 0)
    own_gates.wait()
    g_move = to_mate(g_slots.at[0], g_slots.at[1], 8)
    g_move.start()

    for step in (1, 2, 3):
        heads_move(step).wait_send()
        mix_move(step, lax.rem(row + step, 4)).wait_send()
    wait_sends(buffer_o, o_slots, o_send, o_recv)
    wait_sends(buffer_x, x_slots, x_send, x_recv)

    def wait_gate_sends(step, carry):
        gate_message(lax.rem(col + step, EXPERTS), col).wait_send()
        return carry

    lax.fori_loop(1, EXPERTS, wait_gate_sends, 0)

    def wait_o(group, carry):
        o_move(group).wait()
        return carry

    lax.fori_loop(0, 8, wait_o, 0)

    def wait_x(group, carry):
        x_move(group).wait()
        return carry

    lax.fori_loop(0, 8, wait_x, 0)
    g_move.wait()
    for move in weight_moves:
        move.wait()


def forward(long_lengths, short_lengths, tokens, cot, routes_t, gain_a, gain_m, rel_bias_t, router_t, ids, wq, wk, wv, wo, wg, wu, wd):
    def out(shape, dtype):
        return jax.ShapeDtypeStruct(shape, dtype)

    return pl.pallas_call(
        forward_kernel,
        out_shape=(
            out((2, PIECES, QUARTER), BF16),
            out((2, PIECES, QUARTER), BF16),
            out((2, EXPERTS, 8, 128), F32),
            out((SHARD, WIDTH), BF16),
            out((SHARD, WIDTH), BF16),
            out((EARLY_DOWN, WIDTH), BF16),
            out((ROWS, WIDTH), BF16),
            out((4, LONG, 768), BF16),
            out((LONG, 3 * WIDTH), BF16),
            out((ROWS, WIDTH), BF16),
            out((4, 128, 128), F32),
            out((128, 128), F32),
            out((ROWS, WIDTH), F32),
            out((EXPERTS, ROWS), F32),
            out((1, ROWS), F32),
        ),
        in_specs=[SMEM_SPEC] * 2 + [VMEM_SPEC] * 12 + [HBM_SPEC] * 3,
        out_specs=[HBM_SPEC] * 6 + [VMEM_SPEC] * 9,
        scratch_shapes=[
            pltpu.VMEM((ROWS, WIDTH), BF16),
            pltpu.VMEM((4, LONG, 768), BF16),
            pltpu.VMEM((4, LONG, 256), BF16),
            pltpu.VMEM((PIECES, QUARTER), BF16),
            pltpu.VMEM((PIECES, QUARTER), BF16),
            pltpu.VMEM((EXPERTS, 8, 128), F32),
            pltpu.VMEM((4, HEADS, TABLE), F32),
            pltpu.VMEM((HEADS, 256), F32),
            DMA((EXPERTS,)),
            DMA((EXPERTS,)),
            DMA((EXPERTS,)),
            DMA((EXPERTS,)),
            DMA((EXPERTS,)),
            DMA((EXPERTS,)),
            DMA((3,)),
            DMA((3,)),
            DMA((3,)),
            DMA((3,)),
            DMA((3,)),
            DMA((17,)),
            DMA((17,)),
            DMA((5,)),
            DMA((5,)),
        ],
        compiler_params=pltpu.CompilerParams(
            collective_id=1, has_side_effects=True, vmem_limit_bytes=56 * 1024 * 1024
        ),
        name="forward_and_dispatch",
    )(
        long_lengths, short_lengths, tokens, cot, routes_t, gain_a, gain_m, rel_bias_t, router_t, ids, wq, wk, wv, wo,
        wg, wu, wd,
    )


def expert_kernel(
    x_slots, o_slots, g_slots, unfold, fold, row_hot, slot_of, wg_own, wu_own, wd_own, wg_mate, wu_mate, wd_mate, normed_a,
    dx_back, dg_back, outs, out_first, normed_all, grad_own, grad_send, grad_mate,
    stage, xs, os, dys, wg, wu, wd, act, dg, du, part, arrived, dxs, gate_part, gate_arrived, gate_out, grad_stage,
    grad_half, grad_first, stage_sem, weight_sem, late_send, late_recv, first_send, first_recv, t_send, t_recv, m_send, m_recv, r_send, r_recv, n_send, n_recv, own_sem,
    out_sem,
):
    row = lax.axis_index("row")
    col = lax.axis_index("col")
    partner, mate = row_pairs()
    barrier = pltpu.get_barrier_semaphore()
    for step in (1, 2, 3):
        pl.semaphore_signal(barrier, inc=1, device_id=(lax.rem(row + step, 4), col), device_id_type=MESH_ID)

    def greet(step, carry):
        pl.semaphore_signal(barrier, inc=1, device_id=(row, lax.rem(col + step, EXPERTS)), device_id_type=MESH_ID)
        return carry

    lax.fori_loop(1, EXPERTS, greet, 0)

    def load(source, which, index):
        return pltpu.make_async_copy(source.at[which], stage.at[index], stage_sem.at[index])

    load(x_slots, 1, 0).start()
    load(o_slots, 1, 1).start()
    weights = [[], []]
    for j, sources in enumerate(((wg_own, wu_own, wd_own), (wg_mate, wu_mate, wd_mate))):
        for i, (source, held) in enumerate(zip(sources, (wg, wu, wd))):
            copy = pltpu.make_async_copy(
                source, held.at[pl.ds(j * PADDED, source.shape[0])], weight_sem.at[i, j]
            )
            copy.start()
            weights[j].append(copy)
    for held in (wg, wu, wd):
        for j in range(2):
            held[j * PADDED + SHARD : (j + 1) * PADDED, :] = jnp.zeros((PADDED - SHARD, WIDTH), BF16)
    pl.semaphore_wait(barrier, EXPERTS + 2)
    late = pltpu.make_async_remote_copy(
        wd_own.at[pl.ds(EARLY_DOWN, SHARD - EARLY_DOWN)],
        wd.at[pl.ds(PADDED + EARLY_DOWN, SHARD - EARLY_DOWN)],
        late_send,
        late_recv,
        device_id=(partner, col),
        device_id_type=MESH_ID,
    )
    late.start()

    def rows_move(index, dest, of_row):
        source = normed_a if index < 2 else normed_all.at[of_row]
        return pltpu.make_async_remote_copy(
            source,
            normed_all.at[of_row],
            n_send.at[index],
            n_recv.at[index],
            device_id=(dest, col),
            device_id_type=MESH_ID,
        )

    rows_move(0, mate, row).start()
    rows_move(1, partner, row).start()
    own_rows = pltpu.make_async_copy(normed_a, normed_all.at[row], own_sem.at[2])
    own_rows.start()

    def spread(index, target, first):
        def one(group, carry):
            wide = nn(unfold[...], stage[index, block(group, 320), :]).astype(BF16)
            rows = pl.ds(pl.multiple_of(first + group * 80, 16), 80)
            for q in range(4):
                target[rows, q * QUARTER : (q + 1) * QUARTER] = wide[q * 80 : (q + 1) * 80]
            return carry

        lax.fori_loop(0, 8, one, 0, unroll=4)

    def gate_column(which):
        gates = jnp.concatenate([g_slots[which, e, 0:1, :] for e in range(EXPERTS)], axis=0)
        wide = nn(row_hot[...], gates, highest)
        lanes = iota((640, 128), 1)
        return jnp.sum(jnp.where(lanes == slot_of[...], wide, 0.0), axis=1, keepdims=True)

    def take_tokens(which, first):
        load(x_slots, which, 0).wait()
        spread(0, xs, first)
        load(o_slots, which, 1).wait()
        spread(1, os, first)
        rows = pl.ds(first, 640)
        dys[rows, :] = (os[rows, :].astype(F32) * gate_column(which)).astype(BF16)

    def hidden_half(first, half, before_down=None):
        lanes = slice(half * PADDED, (half + 1) * PADDED)
        rows = slice(first, first + 640)
        gate_pre = nt(xs[rows, :], wg[lanes, :])
        up_pre = nt(xs[rows, :], wu[lanes, :])
        if before_down is not None:
            before_down()
        d_act = nt(dys[rows, :], wd[lanes, :])
        square = gate_pre * gate_pre
        bend = jnp.tanh(0.7978845608028654 * gate_pre * (1.0 + 0.044715 * square))
        level = 0.5 * (1.0 + bend)
        gelu = gate_pre * level
        slope = level + 0.5 * gate_pre * (1.0 - bend * bend) * (
            0.7978845608028654 * (1.0 + 3.0 * 0.044715 * square)
        )
        act[rows, lanes] = (gelu * up_pre).astype(BF16)
        du[rows, lanes] = (d_act * gelu).astype(BF16)
        dg[rows, lanes] = (d_act * up_pre * slope).astype(BF16)

    def input_gradient(first):
        rows = pl.ds(first, 320)
        return nn(dg[rows, :], wg[...]) + nn(du[rows, :], wu[...])

    def to_mate(source, target, index):
        return pltpu.make_async_remote_copy(
            source, target, t_send.at[index], t_recv.at[index], device_id=(mate, col), device_id_type=MESH_ID
        )

    def fold_group(source, group):
        rows = pl.ds(pl.multiple_of(group * 80, 16), 80)
        tall = jnp.concatenate([source[rows, q * QUARTER : (q + 1) * QUARTER] for q in range(4)], axis=0)
        return nn(fold[...], tall).astype(BF16)

    def output_part(first, which):
        totals = []
        for i in range(2):
            rows = slice(first + i * 320, first + (i + 1) * 320)
            value = nn(act[rows, :], wd[...])
            dxs[i * 320 : (i + 1) * 320, :] = value.astype(BF16)
            totals.append(jnp.sum(value * os[rows, :].astype(F32), axis=1, keepdims=True))
        total = jnp.concatenate(totals, axis=0)

        def fold_one(group, carry):
            outs[which, block(group, 320), :] = fold_group(dxs, group)
            return carry

        lax.fori_loop(0, 8, fold_one, 0, unroll=4)
        wide = jnp.where(iota((640, 128), 1) == slot_of[...], total, 0.0)
        return lax.dot_general(
            row_hot[...], wide, (((0,), (0,)), ((), ())), preferred_element_type=F32, precision=highest
        )

    def part_move(i):
        rows = pl.ds(i * 320, 320)
        return to_mate(part.at[rows], arrived.at[rows], i)

    def first_move(index, first, rows):
        return pltpu.make_async_remote_copy(
            grad_first.at[pl.ds(first, rows)],
            grad_mate.at[pl.ds(first, rows)],
            first_send.at[index],
            first_recv.at[index],
            device_id=(partner, col),
            device_id_type=MESH_ID,
        )

    take_tokens(1, 640)
    load(x_slots, 0, 0).start()
    load(o_slots, 0, 1).start()
    for copy in weights[0]:
        copy.wait()
    hidden_half(640, 0)
    take_tokens(0, 0)
    for copy in weights[1]:
        copy.wait()
    rows_move(0, mate, mate).wait_recv()
    rows_move(2, partner, mate).start()
    hidden_half(640, 1, late.wait_recv)
    for i in range(2):
        part[i * 320 : (i + 1) * 320, :] = input_gradient(640 + i * 320).astype(BF16)
        part_move(i).start()
    hidden_half(0, 1)
    for which, left in ((0, dg), (1, du)):
        for n in range(2):
            lanes = slice(n * 512, (n + 1) * 512)
            value = tn(left[:, PADDED:], xs[:, lanes])[0:SHARD].astype(BF16)
            grad_first[which * SHARD : (which + 1) * SHARD, lanes] = value
        if which == 0:
            first_moves = [first_move(0, 0, SHARD)]
        else:
            first_moves.append(first_move(1, SHARD, EARLY_UP))
        first_moves[which].start()
    keep_up = pltpu.make_async_copy(
        grad_first.at[pl.ds(SHARD + EARLY_UP, SHARD - EARLY_UP)],
        grad_send.at[pl.ds(0, SHARD - EARLY_UP)],
        own_sem.at[3],
    )
    keep_up.start()
    hidden_half(0, 0)
    def message(dest, source):
        return pltpu.make_async_remote_copy(
            stage.at[0, block(dest, FOLDED)],
            dx_back.at[block(source, FOLDED)],
            m_send.at[dest],
            m_recv.at[source],
            device_id=(row, dest),
            device_id_type=MESH_ID,
        )

    def gate_message(dest, source):
        return pltpu.make_async_remote_copy(
            gate_out.at[dest],
            dg_back.at[source],
            r_send.at[dest],
            r_recv.at[source],
            device_id=(row, dest),
            device_id_type=MESH_ID,
        )

    own_dx = pltpu.make_async_copy(stage.at[0, block(col, FOLDED)], dx_back.at[block(col, FOLDED)], own_sem.at[0])
    own_dg = pltpu.make_async_copy(gate_out.at[col], dg_back.at[col], own_sem.at[1])
    def own_gradient(i):
        rows = slice(i * 320, (i + 1) * 320)
        value = input_gradient(i * 320)
        part_move(i).wait_recv()
        dxs[rows, :] = (value + arrived[rows, :].astype(F32)).astype(BF16)

        def return_group(k, carry):
            group = i * 4 + lax.rem(lax.div(col, 4) + k, 4)
            stage[0, block(group, 320), :] = fold_group(dxs, group)
            for j in range(4):
                dest = group * 4 + j

                @pl.when(dest != col)
                def _():
                    message(dest, col).start()

                @pl.when(dest == col)
                def _():
                    own_dx.start()

            return carry

        lax.fori_loop(0, 4, return_group, 0, unroll=2)
    own_gradient(0)
    gate_part[...] = output_part(640, 1)
    gate_move = to_mate(gate_part, gate_arrived, 2)
    gate_move.start()
    out_move = to_mate(outs.at[1, pl.ds(0, PIECES // 2)], out_first, 3)
    out_move.start()
    own_gradient(1)
    gates = output_part(0, 0)
    gate_move.wait_recv()
    gates = gates + gate_arrived[...]
    for e in range(EXPERTS):
        gate_out[e] = jnp.broadcast_to(gates[e : e + 1, :], (8, 128))

    def send_gates(step, carry):
        gate_message(lax.rem(col + step, EXPERTS), col).start()
        return carry

    lax.fori_loop(1, EXPERTS, send_gates, 0)
    own_dg.start()

    pending = {}
    turn = 0
    pairs = ((dg, xs), (du, xs), (act, dys))
    for which, half in ((2, 1), (0, 0), (1, 0), (2, 0)):
        left, right = pairs[which]
        for n in range(2):
            lanes = slice(n * 512, (n + 1) * 512)
            value = tn(left[:, half * PADDED : (half + 1) * PADDED], right[:, lanes])[0:SHARD]
            slot = turn % 2
            turn += 1
            if slot in pending:
                pending[slot].wait()
            if half == 0:
                grad_stage[slot] = value
                source, target = grad_stage.at[slot], grad_own.at[pl.ds(which * SHARD, SHARD), pl.ds(n * 512, 512)]
            else:
                grad_half[slot] = value.astype(BF16)
                source, target = grad_half.at[slot], grad_send.at[pl.ds(SHARD - EARLY_UP, SHARD), pl.ds(n * 512, 512)]
            pending[slot] = pltpu.make_async_copy(source, target, out_sem.at[slot])
            pending[slot].start()
    for copy in pending.values():
        copy.wait()

    def wait_source(step, carry):
        source = lax.rem(col + step, EXPERTS)
        message(col, source).wait_recv()
        gate_message(col, source).wait_recv()
        message(source, col).wait_send()
        gate_message(source, col).wait_send()
        return carry

    lax.fori_loop(1, EXPERTS, wait_source, 0)
    own_dx.wait()
    own_dg.wait()
    for i in range(2):
        part_move(i).wait_send()
    gate_move.wait_send()
    out_move.wait()
    rows_move(0, mate, row).wait_send()
    rows_move(1, partner, partner).wait()
    rows_move(2, partner, 6 - row - partner - mate).wait()
    own_rows.wait()
    late.wait_send()
    for move in first_moves:
        move.wait()
    keep_up.wait()


def experts(x_slots, o_slots, g_slots, consts, own, other, normed_a):
    def out(shape, dtype):
        return jax.ShapeDtypeStruct(shape, dtype)

    hidden = (2 * 640, 2 * PADDED)
    return pl.pallas_call(
        expert_kernel,
        out_shape=(
            out((PIECES, QUARTER), BF16),
            out((EXPERTS, 8, 128), F32),
            out((2, PIECES, QUARTER), BF16),
            out((PIECES // 2, QUARTER), BF16),
            out((4, ROWS, WIDTH), BF16),
            out((GRAD_ROWS, WIDTH), F32),
            out((2 * SHARD - EARLY_UP, WIDTH), BF16),
            out((SHARD + EARLY_UP, WIDTH), BF16),
        ),
        in_specs=[HBM_SPEC] * 2 + [VMEM_SPEC] * 5 + [HBM_SPEC] * 7,
        out_specs=[HBM_SPEC] * 2 + [VMEM_SPEC] + [HBM_SPEC] * 5,
        scratch_shapes=[
            pltpu.VMEM((2, PIECES, QUARTER), BF16),
            pltpu.VMEM((1280, WIDTH), BF16),
            pltpu.VMEM((1280, WIDTH), BF16),
            pltpu.VMEM((1280, WIDTH), BF16),
            pltpu.VMEM((2 * PADDED, WIDTH), BF16),
            pltpu.VMEM((2 * PADDED, WIDTH), BF16),
            pltpu.VMEM((2 * PADDED, WIDTH), BF16),
            pltpu.VMEM(hidden, BF16),
            pltpu.VMEM(hidden, BF16),
            pltpu.VMEM(hidden, BF16),
            pltpu.VMEM((640, WIDTH), BF16),
            pltpu.VMEM((640, WIDTH), BF16),
            pltpu.VMEM((640, WIDTH), BF16),
            pltpu.VMEM((EXPERTS, 128), F32),
            pltpu.VMEM((EXPERTS, 128), F32),
            pltpu.VMEM((EXPERTS, 8, 128), F32),
            pltpu.VMEM((2, SHARD, 512), F32),
            pltpu.VMEM((2, SHARD, 512), BF16),
            pltpu.VMEM((2 * SHARD, WIDTH), BF16),
            DMA((2,)),
            DMA((3, 2)),
            DMA,
            DMA,
            DMA((2,)),
            DMA((2,)),
            DMA((4,)),
            DMA((4,)),
            DMA((EXPERTS,)),
            DMA((EXPERTS,)),
            DMA((EXPERTS,)),
            DMA((EXPERTS,)),
            DMA((3,)),
            DMA((3,)),
            DMA((4,)),
            DMA((2,)),
        ],
        compiler_params=pltpu.CompilerParams(
            collective_id=2, has_side_effects=True, vmem_limit_bytes=62 * 1024 * 1024
        ),
        name="experts",
    )(x_slots, o_slots, g_slots, *consts, *own, *other, normed_a)


def backward_kernel(
    long_len, short_len, tokens, cot, routes_t, gain_a, gain_m, rel_bias_t, router_t, ids_t, wq, wk, wv, wo,
    resid, probs_t, rnorm_t, heads_in, short_qkv, mixed, norm_l, norm_s, dx_back, dg_back, outs, out_first, normed_all, grad_send,
    block_out, tokens_grad, last_sum, out_grads_sum, head_grads_sum, small_sum, grad_mate,
    out_grads, head_grads, small, total, branch, d_mixed, mix_out, mix_in, flipped, normed_t, d_qkv, d_heads, mix_short, d_arrived,
    d_key, d_value,
    table_l, table_s, diag_l, diag_s,
    turned, out_arrived, out_sum, out_back, last_own, last_col, last_row,
    t_send, t_recv, mix_send, mix_recv, h_send, h_recv, s_send, s_recv, m_send, m_recv, own_sem, w_send, w_recv, c_send, c_recv, r_send, r_recv, *sum_refs,
):
    row = lax.axis_index("row")
    col = lax.axis_index("col")
    partner, mate = row_pairs()
    barrier = pltpu.get_barrier_semaphore()
    for step in (1, 2, 3):
        pl.semaphore_signal(barrier, inc=1, device_id=(lax.rem(row + step, 4), col), device_id_type=MESH_ID)

    def greet(step, carry):
        pl.semaphore_signal(barrier, inc=1, device_id=(row, lax.rem(col + step, EXPERTS)), device_id_type=MESH_ID)
        return carry

    lax.fori_loop(1, EXPERTS, greet, 0)
    pl.semaphore_wait(barrier, EXPERTS + 2)
    slots_end = 2 + 3 * SUM_COUNT
    sums = SumSteps(
        (out_grads, small),
        (out_grads_sum, small_sum),
        sum_refs[0:2],
        sum_refs[2:slots_end],
        sum_refs[slots_end : slots_end + 9],
    )
    head_refs = sum_refs[slots_end + 9 :]
    heads = HeadSums(head_grads, head_grads_sum, head_refs[0], head_refs[1:7], head_refs[7:])

    out_move = pltpu.make_async_remote_copy(
        outs.at[1, pl.ds(PIECES // 2, PIECES // 2)], out_arrived, t_send, t_recv, device_id=(mate, col), device_id_type=MESH_ID
    )
    out_move.start()


    def weight_move(index):
        rows = pl.ds(sum(GRAD_PIECES[:index]), GRAD_PIECES[index])
        return pltpu.make_async_remote_copy(
            grad_send.at[rows],
            grad_mate.at[rows],
            w_send.at[index],
            w_recv.at[index],
            device_id=(partner, col),
            device_id_type=MESH_ID,
        )

    weight_move(0).start()

    def message(dest, source):
        return pltpu.make_async_remote_copy(
            out_sum.at[block(dest, FOLDED)],
            out_back.at[block(source, FOLDED)],
            m_send.at[dest],
            m_recv.at[source],
            device_id=(row, dest),
            device_id_type=MESH_ID,
        )

    own_out = pltpu.make_async_copy(out_sum.at[block(col, FOLDED)], out_back.at[block(col, FOLDED)], own_sem)

    def return_half(half, arrived):
        def one(i, carry):
            group = lax.rem(lax.div(col, 4) + i, 4)
            rows = block(half * 4 + group, 320)
            out_sum[rows, :] = (outs[0, rows, :].astype(F32) + arrived[block(group, 320), :].astype(F32)).astype(BF16)
            for j in range(4):
                dest = half * 16 + group * 4 + j

                @pl.when(dest != col)
                def _():
                    message(dest, col).start()

                @pl.when(dest == col)
                def _():
                    own_out.start()

            return carry

        lax.fori_loop(0, 4, one, 0)

    return_half(0, out_first)

    hots, both, slots, place_rows = route_places(routes_t[...])

    def column(value):
        return jnp.broadcast_to(value, (128, ROWS)).T[:, 0:1]

    place = [column(value) for value in place_rows]

    def gather_back(source):
        total[...] = jnp.zeros_like(total)

        def one(i, carry):
            here = block(i, 512)
            slot_id, quarter = ids_t[0:1, here], ids_t[1:2, here]
            match = (slot_id == place[0]) | (slot_id == place[1])
            values = source[here, :]
            for q in range(4):
                hot = jnp.where(match & (quarter == q), 1.0, 0.0).astype(BF16)
                total[:, q * QUARTER : (q + 1) * QUARTER] += nn(hot, values)
            return carry

        lax.fori_loop(0, PIECES // 512, one, 0, unroll=5)

    gather_back(dx_back)

    probs = probs_t[...]
    picked = [jnp.sum(probs * hot, axis=0, keepdims=True) for hot in hots]
    picked_sum = picked[0] + picked[1]
    gate_slots = jnp.concatenate([dg_back[e, 0:1, :] for e in range(EXPERTS)], axis=0)
    d_gates = [
        jnp.sum(hots[k] * nn(gate_slots, slot_hot(slots[k]), highest), axis=0, keepdims=True) for k in range(2)
    ]
    shared = (d_gates[0] * picked[0] + d_gates[1] * picked[1]) / (picked_sum * picked_sum)
    fraction = jnp.sum(both, axis=1, keepdims=True) / (2 * ROWS)
    d_probs = balance_coef * EXPERTS * fraction
    for k in range(2):
        d_probs = d_probs + (d_gates[k] / picked_sum - shared) * hots[k]
    d_logits = probs * (d_probs - jnp.sum(d_probs * probs, axis=0, keepdims=True))
    d_logits = d_logits + 2.0 * zloss_coef * rnorm_t[...] * probs

    x = resid[...]
    scale = lax.rsqrt(jnp.mean(x * x, axis=1, keepdims=True) + norm_eps)
    router_grad = nn(d_logits, x * scale * gain_m[...], highest)
    small[...] = jnp.zeros_like(small)
    for i in range(8):
        small[i * 32 : (i + 1) * 32, :] = router_grad[:, i * 128 : (i + 1) * 128]
    d_normed = total[...] + nn(d_logits.T, router_t[...], highest)
    gain_grad = jnp.sum(d_normed * (x * scale), axis=0, keepdims=True)
    for i in range(8):
        small[264 + i : 265 + i, :] = gain_grad[:, i * 128 : (i + 1) * 128]
    d_normed = d_normed * gain_m[...]
    shrink = jnp.mean(d_normed * x, axis=1, keepdims=True)
    d_resid = cot[...].astype(F32) + scale * d_normed - x * (scale * scale * scale * shrink)
    tokens_grad[...] = d_resid
    branch[...] = d_resid.astype(BF16)

    def flip(source, target, first):
        def one(i, carry):
            target[block(i, 128), first : first + ROWS] = source[:, block(i, 128)].T
            return carry

        lax.fori_loop(0, 8, one, 0, unroll=4)

    def mix_move(step, dest):
        return pltpu.make_async_remote_copy(
            mix_out.at[dest],
            mix_in.at[row],
            mix_send.at[step - 1],
            mix_recv.at[step - 1],
            device_id=(dest, col),
            device_id_type=MESH_ID,
        )

    def mix_arrival(step):
        source = lax.rem(row + 4 - step, 4)
        return pltpu.make_async_remote_copy(
            mix_out.at[source],
            mix_in.at[source],
            mix_send.at[step - 1],
            mix_recv.at[step - 1],
            device_id=(source, col),
            device_id_type=MESH_ID,
        )

    for step in (1, 2, 3, 0):
        dest = lax.rem(row + step, 4)
        value = nt(branch[...], wo[block(dest, 256), :]).astype(BF16)
        d_mixed[:, block(dest, 256)] = value[LONG:]
        if step == 0:
            mix_in[row] = value[:LONG]
        else:
            mix_out[dest] = value[:LONG]
            mix_move(step, dest).start()
    weight_move(1).start()

    flip(mixed, flipped, 0)

    def out_gradient(n, carry):
        out = nn(flipped[...], branch[:, block(n, 256)]).astype(BF16)
        out_grads[block(n * 2, WIDTH), :] = out[:, 0:128]
        out_grads[block(n * 2 + 1, WIDTH), :] = out[:, 128:256]
        return carry

    lax.fori_loop(0, 4, out_gradient, 0, unroll=2)
    sums.swap(0)

    out_move.wait_recv()
    return_half(1, out_arrived)


    place_s = iota((1, 256), 1)
    place_s = jnp.where(place_s < 128, place_s, place_s - 256)
    table_s[...] = nn(rel_bias_t[...], bucket_hot(place_s), highest)
    place_l = iota((1, TABLE), 1)
    place_l = jnp.where(place_l < 512, place_l, place_l - TABLE)
    for part in range(4):
        table_l[part] = nn(rel_bias_t[...], bucket_hot(place_l - part * LONG), highest)
    diag_l[...] = jnp.zeros_like(diag_l)
    turned[...] = (iota((128, 128), 0) + iota((128, 128), 1) == 127).astype(BF16)
    lane = iota((1, 128), 1)

    def attend_pair_back(q2, k2, v2, m2, norms, first, bias_row_of, store_diag, keep, count, width):
        d_k = jnp.zeros((count, 128), F32)
        d_v = jnp.zeros((count, 128), F32)
        d_q = []
        for side in range(2):
            here = (lane >= 64) if side else (lane < 64)
            q1 = jnp.where(here, q2, jnp.zeros_like(q2))
            m1 = jnp.where(here, m2, jnp.zeros_like(m2))
            norm = jnp.sum(jnp.where(lane == first + side, norms, 0.0), axis=1, keepdims=True)
            bias = pltpu.roll(
                jnp.broadcast_to(bias_row_of(side), (128, width)), 0, 1, stride=1, stride_axis=0
            )[:, :count]
            scores = jnp.where(keep, nt(q1, k2) * 0.125 + bias, masked_score)
            probs = jnp.exp(scores - norm)
            d_probs = nt(m1, v2)
            shift = jnp.sum(probs * d_probs, axis=1, keepdims=True)
            d_scores = (probs * (d_probs - shift)).astype(BF16)
            d_v = d_v + tn(probs.astype(BF16), m1)
            d_k = d_k + tn(d_scores, q1)
            d_q.append(nn(d_scores, k2))
            reverse = nn(turned[...], d_scores)
            reverse = jnp.concatenate([reverse, jnp.zeros((128, width - count), F32)], axis=1)
            reverse = pltpu.roll(reverse, 0, 1, stride=1, stride_axis=0)
            store_diag(side, jnp.sum(reverse, axis=0, keepdims=True))
        d_q = (jnp.where(lane < 64, d_q[0], d_q[1]) * 0.125).astype(BF16)
        return d_q, d_k * 0.125, d_v

    def short_pair(pair, carry):
        lanes = [pl.ds(pl.multiple_of(pair * 128 + which * WIDTH, 128), 128) for which in range(3)]

        def store_diag(side, value):
            diag_s[pl.ds(pair * 2 + side, 1), :] = value

        parts = attend_pair_back(
            *(short_qkv[:, here] for here in lanes),
            d_mixed[:, lanes[0]],
            norm_s[...],
            pair * 2,
            lambda side: table_s[pl.ds(pair * 2 + side, 1), :],
            store_diag,
            iota((1, 128), 1) < short_len[0],
            128,
            256,
        )
        for here, part in zip(lanes, parts):
            d_qkv[LONG:, here] = part.astype(BF16)
        return carry

    lax.fori_loop(0, HEADS // 2, short_pair, 0, unroll=2)

    def short_move(step):
        dest = lax.rem(row + step, 4)
        return pltpu.make_async_remote_copy(
            mix_short.at[dest],
            d_heads.at[row, pl.ds(LONG, LONG)],
            s_send.at[step - 1],
            s_recv.at[step - 1],
            device_id=(dest, col),
            device_id_type=MESH_ID,
        )

    def short_arrival(step):
        source = lax.rem(row + 4 - step, 4)
        return pltpu.make_async_remote_copy(
            mix_short.at[source],
            d_heads.at[source, pl.ds(LONG, LONG)],
            s_send.at[step - 1],
            s_recv.at[step - 1],
            device_id=(source, col),
            device_id_type=MESH_ID,
        )

    for step in (1, 2, 3, 0):
        dest = lax.rem(row + step, 4)
        for which in range(3):
            value = d_qkv[LONG:, pl.ds(pl.multiple_of(dest * 256 + which * WIDTH, 256), 256)]
            if step == 0:
                d_heads[row, LONG:, which * 256 : (which + 1) * 256] = value
            else:
                mix_short[dest, :, which * 256 : (which + 1) * 256] = value
        if step > 0:
            short_move(step).start()
    weight_move(2).start()
    sums.hop(0, 0)
    for source in range(4):
        flip(normed_all.at[source], normed_t, source * ROWS)

    for step in (1, 2, 3):
        mix_arrival(step).wait_recv()
    d_key[...] = jnp.zeros_like(d_key)
    d_value[...] = jnp.zeros_like(d_value)

    def long_part(part, carry):
        norms = norm_l[part]
        for pair in range(2):
            here = slice(pair * 128, (pair + 1) * 128)

            def store_diag(side, value, pair=pair):
                diag_l[part, pl.ds(row * 4 + pair * 2 + side, 1), :] = value

            d_q, d_k, d_v = attend_pair_back(
                heads_in[part, :, here],
                heads_in[:, :, 256 + pair * 128 : 384 + pair * 128].reshape(512, 128),
                heads_in[:, :, 512 + pair * 128 : 640 + pair * 128].reshape(512, 128),
                mix_in[part, :, here],
                norms,
                pair * 2,
                lambda side, pair=pair: table_l[part, pl.ds(row * 4 + pair * 2 + side, 1), :],
                store_diag,
                iota((1, 512), 1) < long_len[0],
                512,
                TABLE,
            )
            d_heads[part, 0:LONG, here] = d_q
            d_key[:, here] += d_k
            d_value[:, here] += d_v
        return carry

    lax.fori_loop(0, 4, long_part, 0)
    d_heads[:, 0:LONG, 256:512] = d_key[...].astype(BF16).reshape(4, LONG, 256)
    d_heads[:, 0:LONG, 512:768] = d_value[...].astype(BF16).reshape(4, LONG, 256)

    def heads_move(step):
        dest = lax.rem(row + step, 4)
        return pltpu.make_async_remote_copy(
            d_heads.at[dest, pl.ds(0, LONG)],
            d_arrived.at[row],
            h_send.at[step - 1],
            h_recv.at[step - 1],
            device_id=(dest, col),
            device_id_type=MESH_ID,
        )

    def heads_arrival(step):
        source = lax.rem(row + 4 - step, 4)
        return pltpu.make_async_remote_copy(
            d_heads.at[source, pl.ds(0, LONG)],
            d_arrived.at[source],
            h_send.at[step - 1],
            h_recv.at[step - 1],
            device_id=(source, col),
            device_id_type=MESH_ID,
        )

    for step in (1, 2, 3):
        heads_move(step).start()
    weight_move(3).start()
    for step in (1, 2, 3):
        short_arrival(step).wait_recv()

    for which in range(3):
        here = slice(which * 256, (which + 1) * 256)
        out = nn(normed_t[...], d_heads[:, :, here].reshape(4 * ROWS, 256)).astype(BF16)
        for core in range(2):
            first = core * HEAD_ROWS + which * WIDTH
            head_grads[first : first + WIDTH, :] = out[:, core * 128 : (core + 1) * 128]
        heads.swap(which)
    sums.hop(0, 1)

    for which in range(3):
        heads.hop(which, 0)

    for step in (1, 2, 3):
        heads_arrival(step).wait_recv()
    for step in range(4):
        source = lax.rem(row + 4 - step, 4)
        for which in range(3):
            lanes = slice(which * 256, (which + 1) * 256)
            value = d_heads[row, 0:LONG, lanes] if step == 0 else d_arrived[source, :, lanes]
            d_qkv[0:LONG, pl.ds(pl.multiple_of(source * 256 + which * WIDTH, 256), 256)] = value

    def back_normed(n, carry):
        rows = block(n, 256)
        value = nt(d_qkv[:, 0:WIDTH], wq[rows, :]) + nt(d_qkv[:, WIDTH : 2 * WIDTH], wk[rows, :])
        total[:, rows] = value + nt(d_qkv[:, 2 * WIDTH :], wv[rows, :])
        return carry

    lax.fori_loop(0, 2, back_normed, 0, unroll=2)
    bias_grad = nt(diag_s[...], bucket_hot(iota((1, 256), 1) - 127), highest)
    for part in range(4):
        bias_grad = bias_grad + nt(diag_l[part], bucket_hot(iota((1, TABLE), 1) - 127 - part * LONG), highest)
    small[272:288, 0:32] = bias_grad
    sums.swap(1)
    sums.hop(0, 2)
    for which in range(3):
        heads.hop(which, 1)
    lax.fori_loop(2, 4, back_normed, 0, unroll=2)
    sums.hop(1, 0)
    for which in range(3):
        heads.gather(which, 0)
    sums.gather(0, 2)
    weight_move(4).start()
    x = tokens[...].astype(F32)
    scale = lax.rsqrt(jnp.mean(x * x, axis=1, keepdims=True) + norm_eps)
    d_normed = total[...]
    gain_grad = jnp.sum(d_normed * (x * scale), axis=0, keepdims=True)
    for i in range(8):
        last_own[i : i + 1, :] = gain_grad[:, i * 128 : (i + 1) * 128]
    d_normed = d_normed * gain_a[...]
    shrink = jnp.mean(d_normed * x, axis=1, keepdims=True)
    tokens_grad[...] = tokens_grad[...] + scale * d_normed - x * (scale * scale * scale * shrink)

    for which in range(3):
        heads.gather(which, 1)
    sums.hop(1, 1)
    sums.gather(0, 1)

    def wait_source(step, carry):
        source = lax.rem(col + step, EXPERTS)
        message(col, source).wait_recv()
        message(source, col).wait_send()
        return carry

    lax.fori_loop(1, EXPERTS, wait_source, 0)
    own_out.wait()
    out_move.wait_send()
    total[...] = jnp.zeros_like(total)
    gates = [picked[k] / picked_sum for k in range(2)]
    gates = [column(gate) for gate in gates]

    def combine(i, carry):
        here = block(i, 512)
        slot_id, quarter = ids_t[0:1, here], ids_t[1:2, here]
        weight = jnp.where(slot_id == place[0], gates[0], 0.0) + jnp.where(slot_id == place[1], gates[1], 0.0)
        high = weight.astype(BF16)
        rest = (weight - high.astype(F32)).astype(BF16)
        values = out_back[here, :]
        for q in range(4):
            here_q = quarter == q
            part = nn(jnp.where(here_q, high, jnp.zeros_like(high)), values)
            part = part + nn(jnp.where(here_q, rest, jnp.zeros_like(rest)), values)
            total[:, q * QUARTER : (q + 1) * QUARTER] += part
        return carry

    lax.fori_loop(0, PIECES // 512, combine, 0, unroll=5)
    branch_m = total[...]
    live = live_column(long_len[0], short_len[0], row)
    resid_now = resid[...]
    result = resid_now + branch_m
    block_out[...] = result
    branch_a = resid_now - tokens[...].astype(F32)
    tallies = [
        jnp.sum(live * jnp.sum(field * field, axis=1, keepdims=True), axis=0, keepdims=True)
        for field in (result, branch_a, branch_m)
    ]
    tallies.append(jnp.sum(live, axis=0, keepdims=True))
    packed = jnp.zeros((8, 128), F32)
    for i, tally in enumerate(tallies):
        packed = jnp.where(iota((8, 128), 1) == i, tally, packed)
    last_own[8:16, :] = packed

    def column_move(dest, source):
        return pltpu.make_async_remote_copy(
            last_own,
            last_col.at[source],
            c_send.at[dest],
            c_recv.at[source],
            device_id=(row, dest),
            device_id_type=MESH_ID,
        )

    def row_move(step):
        return pltpu.make_async_remote_copy(
            last_sum,
            last_row.at[step - 1],
            r_send.at[step - 1],
            r_recv.at[step - 1],
            device_id=(lax.rem(row + step, 4), col),
            device_id_type=MESH_ID,
        )

    def send_last(step, carry):
        column_move(lax.rem(col + step, EXPERTS), col).start()
        return carry

    lax.fori_loop(1, EXPERTS, send_last, 0)
    last_col[col] = last_own[...]

    for which in range(3):
        heads.gather(which, 2)
    sums.gather(0, 0)
    sums.hop(1, 2)

    def wait_last(step, carry):
        column_move(col, lax.rem(col + step, EXPERTS)).wait_recv()
        column_move(lax.rem(col + step, EXPERTS), col).wait_send()
        return carry

    lax.fori_loop(1, EXPERTS, wait_last, 0)
    last_sum[...] = jnp.sum(last_col[...], axis=0)
    for step in (1, 2, 3):
        row_move(step).start()
    weight_move(5).start()
    sums.gather(1, 2)
    for step in (1, 2, 3):
        row_move(step).wait()
    last_sum[...] = last_sum[...] + (last_row[0] + last_row[1] + last_row[2])
    sums.gather(1, 1)
    for which in range(3):
        heads.last(which)
    sums.gather(1, 0)
    sums.last(0)
    sums.last(1)
    for which in range(3):
        heads.wait(which)
    for part in range(SUM_COUNT):
        sums.end(part)
    for step in (1, 2, 3):
        mix_move(step, lax.rem(row + step, 4)).wait_send()
        heads_move(step).wait_send()
        short_move(step).wait_send()
    for index in range(len(GRAD_PIECES)):
        weight_move(index).wait()


def backward(*args):
    def out(shape, dtype):
        return jax.ShapeDtypeStruct(shape, dtype)

    return pl.pallas_call(
        backward_kernel,
        out_shape=(
            out((ROWS, WIDTH), F32),
            out((ROWS, WIDTH), F32),
            out((16, 128), F32),
            out((2 * SUM_ROWS[0], 128), BF16),
            out((4, 2 * HEAD_ROWS, 128), BF16),
            out((2 * SUM_ROWS[1], 128), F32),
            out((2 * SHARD - EARLY_UP, WIDTH), BF16),
        ),
        in_specs=[SMEM_SPEC] * 2 + [VMEM_SPEC] * (len(args) - 3) + [HBM_SPEC],
        out_specs=[VMEM_SPEC] * 3 + [HBM_SPEC] * 4,
        scratch_shapes=[
            pltpu.VMEM((2 * SUM_ROWS[0], 128), BF16),
            pltpu.VMEM((2 * HEAD_ROWS, 128), BF16),
            pltpu.VMEM((2 * SUM_ROWS[1], 128), F32),
            pltpu.VMEM((ROWS, WIDTH), F32),
            pltpu.VMEM((ROWS, WIDTH), BF16),
            pltpu.VMEM((LONG, WIDTH), BF16),
            pltpu.VMEM((4, LONG, 256), BF16),
            pltpu.VMEM((4, LONG, 256), BF16),
            pltpu.VMEM((WIDTH, ROWS), BF16),
            pltpu.VMEM((WIDTH, 4 * ROWS), BF16),
            pltpu.VMEM((ROWS, 3 * WIDTH), BF16),
            pltpu.VMEM((4, ROWS, 768), BF16),
            pltpu.VMEM((4, LONG, 768), BF16),
            pltpu.VMEM((4, LONG, 768), BF16),
            pltpu.VMEM((512, 256), F32),
            pltpu.VMEM((512, 256), F32),
            pltpu.VMEM((4, HEADS, TABLE), F32),
            pltpu.VMEM((HEADS, 256), F32),
            pltpu.VMEM((4, HEADS, TABLE), F32),
            pltpu.VMEM((HEADS, 256), F32),
            pltpu.VMEM((128, 128), BF16),
            pltpu.VMEM((PIECES // 2, QUARTER), BF16),
            pltpu.VMEM((PIECES, QUARTER), BF16),
            pltpu.VMEM((PIECES, QUARTER), BF16),
            pltpu.VMEM((16, 128), F32),
            pltpu.VMEM((EXPERTS, 16, 128), F32),
            pltpu.VMEM((3, 16, 128), F32),
            DMA,
            DMA,
            DMA((3,)),
            DMA((3,)),
            DMA((3,)),
            DMA((3,)),
            DMA((3,)),
            DMA((3,)),
            DMA((EXPERTS,)),
            DMA((EXPERTS,)),
            DMA,
            DMA((len(GRAD_PIECES),)),
            DMA((len(GRAD_PIECES),)),
            DMA((EXPERTS,)),
            DMA((EXPERTS,)),
            DMA((3,)),
            DMA((3,)),
        ]
        + sum_scratch()
        + head_scratch(),
        compiler_params=pltpu.CompilerParams(
            collective_id=3, has_side_effects=True, vmem_limit_bytes=60 * 1024 * 1024
        ),
        name="backward_and_sums",
    )(*args)


def per_device(
    tokens_in, out_cot, long_lengths, short_lengths, routes, gain_attn, w_query, w_key, w_value, w_out, rel_bias,
    gain_moe, router, w_gate, w_up, w_down,
):
    own = (jnp.swapaxes(w_gate[0], 0, 1), jnp.swapaxes(w_up[0], 0, 1), w_down[0])
    routes_t = jnp.swapaxes(routes, 0, 1)
    router_t = jnp.swapaxes(router, 0, 1)
    rel_bias_t = jnp.swapaxes(rel_bias, 0, 1)
    gain_a, gain_m = gain_attn.reshape(1, WIDTH), gain_moe.reshape(1, WIDTH)
    ids = piece_ids()
    sent = forward(
        long_lengths, short_lengths, tokens_in, out_cot, routes_t, gain_a, gain_m, rel_bias_t, router_t,
        jnp.asarray(ids.T), w_query, w_key, w_value, w_out, *own,
    )
    x_slots, o_slots, g_slots, *other = sent[:6]
    normed_a, heads_in, short_qkv, mixed, norm_l, norm_s, resid, probs_t, rnorm_t = sent[6:]
    unfold = unfold_matrix()
    row_of = np.arange(640) // SLOTS
    consts = (
        jnp.asarray(unfold, BF16),
        jnp.asarray(unfold.T, BF16),
        jnp.asarray((row_of[:, None] == np.arange(EXPERTS)[None, :]).astype(np.float32)),
        jnp.asarray((np.arange(640) % SLOTS).astype(np.int32)[:, None]),
    )
    dx_back, dg_back, outs, out_first, normed_all, grad_own, grad_send, grad_early = experts(x_slots, o_slots, g_slots, consts, own, other, normed_a)
    block_out, tokens_grad, last, out_grads, head_grads, small, grad_late = backward(
        long_lengths, short_lengths, tokens_in, out_cot, routes_t, gain_a, gain_m, rel_bias_t, router_t,
        jnp.asarray(ids), w_query, w_key, w_value, w_out, resid, probs_t, rnorm_t, heads_in, short_qkv, mixed,
        norm_l, norm_s, dx_back, dg_back, outs, out_first, normed_all, grad_send,
    )
    wo_sum, wq_sum, wk_sum, wv_sum, wg_sum, wu_sum, wd_sum, gain_a_sum, gain_m_sum, bias, router_sum, stats = finish(
        out_grads, head_grads, small, last, grad_own, grad_early, grad_late
    )
    return (
        block_out,
        tokens_grad,
        gain_a_sum.reshape(WIDTH),
        wq_sum,
        wk_sum,
        wv_sum,
        wo_sum,
        jnp.swapaxes(bias, 0, 1),
        gain_m_sum.reshape(WIDTH),
        jnp.swapaxes(router_sum, 0, 1),
        jnp.swapaxes(wg_sum, 0, 1)[None],
        jnp.swapaxes(wu_sum, 0, 1)[None],
        wd_sum[None],
        stats[0, 0:3],
    )


def solution(mesh):
    tokens = P(("row", "col"), None)
    whole = P()
    wide = P("col", None, "row")
    tall = P("col", "row", None)
    return jax.shard_map(
        per_device,
        mesh=mesh,
        in_specs=(tokens, tokens, P("col"), P(("row", "col")), tokens) + (whole,) * 8 + (wide, wide, tall),
        out_specs=(tokens, tokens) + (whole,) * 8 + (wide, wide, tall, whole),
        check_vma=False,
    )
```
